32 devices in a mesh: dp: 8 (over z, core), expert: 4 (over y, x).
Axes of the slice: x: 2, y: 2, z: 4, core: 2. Of those that a mesh axis runs over, the one named last changes fastest.
Arguments:
- tokens: bfloat16 [4096, 2560], P(('dp', 'expert')), may hold values from -6 to 6
- out_grad: bfloat16 [4096, 2560], P(('dp', 'expert')), may hold values from -0.29882812 to 0.29882812
- gate_up: bfloat16 [4096, 1, 1536], P(('dp', 'expert')), may hold values from -8 to 8
- route_weight: bfloat16 [4096, 1], P(('dp', 'expert')), may hold values from 0.19921875 to 1
- routes: int32 [4096, 1], P(('dp', 'expert')), may hold values from 0 to 3; in each aligned block of 128 rows (0 to 127, 128 to 255, ...) at most 64 rows name the same one
- down_weight: bfloat16 [4, 768, 2560], P('expert', 'dp'), may hold values from -0.21875 to 0.21875
- master: float32 [4, 8, 506880], P('expert', 'dp'), may hold values from -0.12 to 0.12
- moment_one: float32 [4, 8, 506880], P('expert', 'dp'), may hold values from -2 to 2
- moment_two: float32 [4, 8, 506880], P('expert', 'dp'), may hold values from 0.05 to 5
- offsets: int32 [9], replicated, may hold values from 0 to 3932160, as said below
Outputs:
- new_master: float32 [4, 8, 506880], P('expert', 'dp')
- new_moment_one: float32 [4, 8, 506880], P('expert', 'dp')
- new_moment_two: float32 [4, 8, 506880], P('expert', 'dp')
- new_weight: bfloat16 [4, 2560, 1536], P('expert', 'dp')
- router_grad: float32 [4096, 1], P(('dp', 'expert'))
The draws below stay inside these ranges and needn't reach their ends.
Inputs may be any that keep to these rules, and one draw needn't show every extreme that they name: `routes`: in each aligned block of 128 tokens (the tokens of one device) no expert is named more than 64 times, a bound that some block reaches; the 1 choices of a token differ. offsets[0] = 0, offsets[8] = 3932160; for 0 < j < 8, offsets[j] lies from j * 491520 - 15360 to j * 491520 - 2; offsets[7] = 3425280, so the last bucket holds exactly 506880 entries.
All inputs are finite; a program needn't handle non-finite values.
Results may differ from the reference program's by a relative error of at most 0.0012.
Values may be sent and summed in bfloat16 or wider, within the bound.
No kernel may reach another device: no remote copies, remote signals or barrier semaphores. Data moves between devices by JAX's collectives and lax.ppermute only.
A program may use at most 128 MiB of HBM per device.

```python
import math
import jax
import jax.numpy as jnp
import numpy as np
from jax import lax

D = 2560
F = 768
TOPK = 1
TOK_DEV = 128
EXPERTS = 4
TOKENS = 4096
CAP = 64
TWO_F = 1536
BUCKETS = 8
SPAN = 491520
SLACK = 15360
BCAP = 506880
N_DP = 8
N_EXPERT = 4


def draw_offsets(key, part):
    key = jax.random.fold_in(key, 7)
    sizes_drawn = jax.random.randint(key, (BUCKETS + 1,), 2, SLACK + 1).astype(jnp.int32)
    places = jnp.arange(BUCKETS + 1, dtype=jnp.int32)
    shifts = jnp.where(places == BUCKETS - 1, SLACK, sizes_drawn).astype(jnp.int32)
    shifts = jnp.where((places == 0) | (places == BUCKETS), 0, shifts).astype(jnp.int32)
    return (places * SPAN - shifts).astype(jnp.int32)


def with_spikes(values, key, source, target, blocks, factor):
    def block_of(dim):
        return (jnp.arange(values.shape[dim]) // (values.shape[dim] // blocks)).reshape((-1,) + (1,) * (values.ndim - 1 - dim))

    near = jax.random.permutation(key, blocks)[block_of(target)]
    far = (block_of(target) + blocks // 2) % blocks
    return jnp.where((block_of(source) == near) | (block_of(source) == far), factor * values, values)


def steps_of(own_key, extent, shards, smallest, high):
    def one(axis_at, parts):
        heights = jax.random.uniform(jax.random.fold_in(jax.random.fold_in(own_key, 6), axis_at), (parts,), jnp.float32, smallest / len(shards), high / len(shards))
        return jnp.repeat(jnp.exp(heights), extent[axis_at] // parts).reshape((-1,) + (1,) * (len(extent) - axis_at - 1))

    loudness = one(*shards[0])
    for cut in shards[1:]:
        loudness = loudness * one(*cut)
    return loudness


def shared_out(stream_key, own, number, rows, number_of, top, most, slope):
    sequence = jax.random.permutation(stream_key, number_of)
    heavy_load, ordinary = shares(number_of, rows * top, most, slope, True), shares(number_of, rows * top, most, slope, False)
    places = jnp.arange(number_of)

    def named(sizes, rotation):
        used = int((sizes > 0).sum())
        fixed = max(1, used // 4)
        passed = fixed + (places - fixed + rotation * (used - fixed)) % max(1, number_of - fixed)
        return jnp.zeros((number_of,), jnp.int32).at[sequence[jnp.where(places < fixed, places, passed)]].set(jnp.asarray(sizes, jnp.int32))

    sizes = jnp.where(number % 4 == 0, named(heavy_load, number // 4), named(ordinary, number - number // 4 - 1))
    mixed = jax.random.permutation(jax.random.fold_in(own, 3), number_of)
    source_of, taker = mixed[0:number_of // 2 * 2:2], mixed[1:number_of // 2 * 2:2]
    room = jnp.minimum(sizes[source_of] - 1, most - sizes[taker]) // 2
    room = jnp.where((source_of == sequence[0]) | (taker == sequence[0]) | (sizes[taker] == 0), 0, jnp.maximum(room, 0))
    passed = jax.random.randint(jax.random.fold_in(own, 4), (number_of // 2,), 0, 1 << 20) % (room + 1)
    sizes = sizes.at[source_of].add(-passed).at[taker].add(passed)
    items = jnp.searchsorted(jnp.cumsum(sizes), jnp.arange(rows * top), side="right").astype(jnp.int32)
    listing = items.reshape(top, rows).T
    listing = listing[jax.random.permutation(jax.random.fold_in(own, 1), rows)]
    rotation = jax.random.randint(jax.random.fold_in(own, 2), (rows, 1), 0, top)
    return jnp.take_along_axis(listing, (jnp.arange(top)[None, :] + rotation) % top, axis=1)


def shares(count, total, reach, lean, full):
    weights = [(1 << 20) // math.isqrt(rank ** lean) + 1 for rank in range(1, count + 1)]
    largest = reach if full else min(reach, max(-(-total // count), total * weights[0] // sum(weights)))
    least = 1 if total - largest >= count - 1 else 0
    given, spare = [largest] + [least] * (count - 1), total - largest - least * (count - 1)
    while spare > 0:
        candidates = [i for i in range(1, count) if given[i] < largest] or [i for i in range(1, count) if given[i] < reach]
        mass, remaining = sum([weights[i] for i in candidates]), spare
        for i in candidates:
            addition = min(reach - given[i], max(1, remaining * weights[i] // mass), spare)
            given[i] = given[i] + addition
            spare = spare - addition
    return np.array(given)


def gaussian(own_key, shape, scale, limit, cuts=(), held_as=jnp.bfloat16):
    gain = steps_of(own_key, shape, cuts, -0.22, 0.18) if cuts else 1.0
    result = jax.random.normal(own_key, shape, jnp.float32) * scale * gain
    return jnp.minimum(jnp.maximum(result, -limit), limit).astype(held_as)


def bell_draw_with(own_key, shape, scale, limit, cuts, heavy, kind=jnp.bfloat16):
    values = scale * jax.random.normal(own_key, shape, jnp.float32)
    if cuts:
        values = values * steps_of(own_key, shape, cuts, -0.22, 0.18)
    return jnp.clip(with_spikes(values, jax.random.fold_in(own_key, 3), *heavy), -limit, limit).astype(kind)


def setup_inputs(seed: int = 0) -> dict:
    keys = jax.random.split(jax.random.key(seed), 11)
    tokens = bell_draw_with(keys[0], (TOKENS, D), 1.0, 6.0, ((0, 32),), (0, 1, 32, 2.75))
    out_grad = gaussian(keys[1], (TOKENS, D), 0.05, 0.29882812, ((0, 32),))
    gate_up = gaussian(keys[2], (TOKENS, TOPK, TWO_F), 1.5, 8.0, ((0, 32),))
    route_weight = jnp.clip(0.19921875 + 0.80078125 * jax.random.uniform(keys[3], (TOKENS, TOPK), jnp.float32) ** steps_of(keys[3], (TOKENS, TOPK), ((0, 32),), -0.2, 0.2), 0.19921875, 1.0).astype(jnp.bfloat16)
    routes_keys = jax.random.split(jax.random.fold_in(keys[4], 1), TOKENS // TOK_DEV)
    routes_turns = jax.random.permutation(jax.random.fold_in(keys[4], 3), TOKENS // TOK_DEV)
    routes = jax.vmap(lambda own, number: shared_out(jax.random.fold_in(keys[4], 2), own, number, TOK_DEV, EXPERTS, TOPK, CAP, 2))(routes_keys, routes_turns).reshape((TOKENS, TOPK))
    down_weight = gaussian(keys[5], (EXPERTS, F, D), F ** -0.5, 0.21875, ((0, 4), (1, 8)))
    master = gaussian(keys[6], (EXPERTS, BUCKETS, BCAP), 0.02, 0.12, ((0, 4), (1, 8)), jnp.float32)
    moment_one = gaussian(keys[7], (EXPERTS, BUCKETS, BCAP), 0.3, 2.0, ((0, 4), (1, 8)), jnp.float32)
    moment_two = jnp.clip(jnp.exp(math.log(5.0) - 4.6051702 * jax.random.uniform(keys[8], (EXPERTS, BUCKETS, BCAP), jnp.float32) ** steps_of(keys[8], (EXPERTS, BUCKETS, BCAP), ((0, 4), (1, 8)), -0.2, 0.2)), 0.05, 5.0)
    offsets = draw_offsets(jax.random.fold_in(keys[10], 71), 0)
    return {"tokens": tokens, "out_grad": out_grad, "gate_up": gate_up, "route_weight": route_weight, "routes": routes, "down_weight": down_weight, "master": master, "moment_one": moment_one, "moment_two": moment_two, "offsets": offsets}


beta_one = 0.9
beta_two = 0.95
learn_rate = 0.001
decay_rate = 0.1
adam_eps = 1e-08
adam_step = 20.0

def slab_terms(slab_tokens, slab_grads, slab_saved, slab_weight, slab_routes, down_weight):
    row_limit = N_EXPERT * CAP
    row_total = slab_routes.shape[0]

    def per_expert(expert):
        hits = slab_routes == expert
        order = jnp.argsort(jnp.where(hits, 0, 1).astype(jnp.int32), stable=True).astype(jnp.int32)
        picked = order[:row_limit]
        in_use = jnp.arange(row_limit, dtype=jnp.int32) < jnp.sum(hits.astype(jnp.int32))
        token_of = (picked // TOPK).astype(jnp.int32)
        features = slab_tokens[token_of]
        cotangent = jnp.where(in_use[:, None], slab_grads[token_of], jnp.zeros((), slab_grads.dtype))
        saved_gu = jnp.where(in_use[:, None], slab_saved[picked], jnp.zeros((), slab_saved.dtype))
        weight_row = jnp.where(in_use, slab_weight[picked].astype(jnp.float32), jnp.float32(0.0))
        back_prod = jnp.dot(cotangent, down_weight[expert].T, preferred_element_type=jnp.float32)
        gate_pre = saved_gu[:, :F].astype(jnp.float32)
        up_part = saved_gu[:, F:].astype(jnp.float32)
        sigmoid_gate = jax.nn.sigmoid(gate_pre)
        activation = gate_pre * sigmoid_gate * up_part
        scores = lax.optimization_barrier(jnp.sum(activation * back_prod, axis=1))
        scaled = weight_row[:, None] * back_prod
        grad_gate = scaled * up_part * sigmoid_gate * (1.0 + gate_pre * (1.0 - sigmoid_gate))
        grad_up = scaled * gate_pre * sigmoid_gate
        grad_joined = jnp.concatenate([grad_gate, grad_up], axis=1).astype(jnp.bfloat16)
        partial_sum = jnp.dot(features.T, grad_joined, preferred_element_type=jnp.float32).astype(jnp.bfloat16)
        return (partial_sum, jnp.where(in_use, scores, jnp.float32(0.0)), picked)
    partials, scores, picked = lax.map(per_expert, jnp.arange(EXPERTS, dtype=jnp.int32))
    row_scores = jnp.zeros((row_total,), jnp.float32).at[picked.reshape(-1)].add(scores.reshape(-1))
    return (partials, row_scores)

def reference(tokens, out_grad, gate_up, route_weight, routes, down_weight, master, moment_one, moment_two, offsets):
    slab_tokens = N_EXPERT * TOK_DEV
    token_slabs = tokens.reshape(N_DP, slab_tokens, D)
    grad_slabs = out_grad.reshape(N_DP, slab_tokens, D)
    saved_slabs = gate_up.reshape(N_DP, slab_tokens * TOPK, 2 * F)
    weight_slabs = route_weight.reshape(N_DP, slab_tokens * TOPK)
    route_slabs = routes.reshape(N_DP, slab_tokens * TOPK)

    def add_slab(running, pieces):
        partials, row_scores = slab_terms(pieces[0], pieces[1], pieces[2], pieces[3], pieces[4], down_weight)
        return (running + partials.astype(jnp.float32), row_scores)
    grad_sum, all_scores = lax.scan(add_slab, jnp.zeros((EXPERTS, D, 2 * F), jnp.float32), (token_slabs, grad_slabs, saved_slabs, weight_slabs, route_slabs))
    router_grad = all_scores.reshape(TOKENS, TOPK)
    flat_size = D * 2 * F
    flat_grad = jnp.concatenate([grad_sum.reshape(EXPERTS, flat_size), jnp.zeros((EXPERTS, BCAP), jnp.float32)], axis=1)
    slot_ids = jnp.arange(BCAP, dtype=jnp.int32)
    bucket_len = (offsets[1:] - offsets[:-1]).astype(jnp.int32)
    in_bucket = slot_ids[None, :] < bucket_len[:, None]
    flat_index = (offsets[:-1, None] + slot_ids[None, :]).astype(jnp.int32)
    bucket_grad = jnp.where(in_bucket[None], flat_grad[:, flat_index], jnp.float32(0.0))
    moment_new = beta_one * moment_one + (1.0 - beta_one) * bucket_grad
    square_new = beta_two * moment_two + (1.0 - beta_two) * bucket_grad * bucket_grad
    update = moment_new / (1.0 - beta_one ** adam_step) / (jnp.sqrt(square_new / (1.0 - beta_two ** adam_step)) + adam_eps)
    master_new = master - learn_rate * (update + decay_rate * master)
    new_master = jnp.where(in_bucket[None], master_new, jnp.float32(0.0))
    new_moment_one = jnp.where(in_bucket[None], moment_new, jnp.float32(0.0))
    new_moment_two = jnp.where(in_bucket[None], square_new, jnp.float32(0.0))
    flat_pos = jnp.arange(flat_size, dtype=jnp.int32)
    owner = (jnp.searchsorted(offsets, flat_pos, side='right') - 1).astype(jnp.int32)
    owner = jnp.clip(owner, 0, N_DP - 1).astype(jnp.int32)
    inside = (flat_pos - offsets[owner]).astype(jnp.int32)
    new_weight = new_master[:, owner, inside].astype(jnp.bfloat16).reshape(EXPERTS, D, 2 * F)
    return (new_master, new_moment_one, new_moment_two, new_weight, router_grad)
```

```python
import functools

import jax
import jax.numpy as jnp
from jax import lax
from jax.experimental import pallas as pl
from jax.experimental.pallas import tpu as pltpu
from jax.sharding import PartitionSpec as P

beta_one = 0.9
beta_two = 0.95
learn_rate = 0.001
decay_rate = 0.1
adam_eps = 1e-08
adam_step = 20.0

LANES = 128
CHUNK = 120
VMEM_LIMIT = 56 * 1024 * 1024

f32 = jnp.float32
bf16 = jnp.bfloat16
i32 = jnp.int32


def round_up(value, unit):
    return -(-value // unit) * unit


def iota(shape, axis):
    return lax.broadcasted_iota(i32, shape, axis)


def params():
    return pltpu.CompilerParams(vmem_limit_bytes=VMEM_LIMIT)


def cost(flops, moved):
    return pl.CostEstimate(flops=int(flops), bytes_accessed=int(moved), transcendentals=0)


def pack_kernel(routes_ref, weight_ref, grads_ref, saved_ref, packed_ref, select_ref, target_ref, *, experts, cap):
    ids = routes_ref[...]
    count = ids.shape[1]
    width = grads_ref.shape[1]
    hits = iota((round_up(experts, 8), count), 0) == ids
    before = (iota((count, count), 0) < iota((count, count), 1)).astype(bf16)
    earlier = jnp.dot(hits.astype(f32).astype(bf16), before, preferred_element_type=f32)
    slot = jnp.sum(jnp.where(hits, earlier, 0.0), axis=0, keepdims=True)
    target = ids * cap + slot.astype(i32)
    chosen = iota((experts * cap, count), 0) == target
    select = chosen.astype(f32).astype(bf16)
    select_ref[...] = chosen.astype(f32)
    target_ref[...] = target.astype(f32)
    packed_ref[:, :width] = jnp.dot(select, grads_ref[...], preferred_element_type=f32).astype(bf16)
    packed_ref[:, width:-LANES] = jnp.dot(select, saved_ref[...], preferred_element_type=f32).astype(bf16)
    weight = jnp.sum(jnp.where(chosen, weight_ref[...].astype(f32), 0.0), axis=1, keepdims=True)
    packed_ref[:, -LANES:] = jnp.broadcast_to(weight, (experts * cap, LANES)).astype(bf16)


def window_kernel(target_ref, tokens_ref, out_ref, *, per, lead):
    parts, count, width = out_ref.shape
    diagonal = iota((count, count), 0) == iota((count, count), 1)
    column = jnp.sum(jnp.where(diagonal, target_ref[...], 0.0), axis=1, keepdims=True)
    note = jnp.broadcast_to(column, (count, width)).astype(bf16)
    lane = iota((count, width), 1)
    for j in range(parts):
        start = per * j - lead
        if start < 0:
            blank = jnp.zeros((count, -start), bf16)
            piece = jnp.concatenate([blank, tokens_ref[:, : start + width]], axis=1)
        else:
            piece = tokens_ref[:, start : start + width]
        out_ref[j] = jnp.where(lane == 0, note, piece)


def compact_kernel(windows_ref, out_ref):
    parts, count, width = windows_ref.shape
    experts, _, cap, _ = out_ref.shape
    diagonal = iota((count, count), 0) == iota((count, count), 1)
    slots = iota((experts * cap, count), 0)
    for i in range(parts):
        block = windows_ref[i]
        column = block[:, 0:1].astype(f32)
        target = jnp.sum(jnp.where(diagonal, column, 0.0), axis=0, keepdims=True).astype(i32)
        select = (slots == target).astype(f32).astype(bf16)
        rows = jnp.dot(select, block, preferred_element_type=f32).astype(bf16)
        for e in range(experts):
            out_ref[e, i] = rows[e * cap : (e + 1) * cap]


def turn_kernel(rows_ref, out_ref):
    groups, parts, cap, width = rows_ref.shape
    kept = out_ref.shape[1]
    for i in range(parts):
        slab = jnp.concatenate([rows_ref[x, i] for x in range(groups)], axis=0)
        out_ref[i] = slab.T[width - kept :, :]


def row_kernel(arrived_ref, down_ref, joined_ref, scores_ref):
    hidden, width = down_ref.shape
    rows = arrived_ref.shape[0]
    back = lax.dot_general(
        arrived_ref[:, :width], down_ref[...], (((1,), (1,)), ((), ())), preferred_element_type=f32
    )
    gate = arrived_ref[:, width : width + hidden].astype(f32)
    up = arrived_ref[:, width + hidden : width + 2 * hidden].astype(f32)
    weight = arrived_ref[:, width + 2 * hidden :].astype(f32)[:, 0:1]
    sig = jax.nn.sigmoid(gate)
    scores = jnp.sum(gate * sig * up * back, axis=1, keepdims=True)
    scores_ref[...] = jnp.broadcast_to(scores, (rows, LANES))
    scaled = weight * back
    joined_ref[:, :hidden] = (scaled * up * sig * (1.0 + gate * (1.0 - sig))).astype(bf16)
    joined_ref[:, hidden:] = (scaled * gate * sig).astype(bf16)


def router_kernel(select_ref, scores_ref, out_ref):
    out_ref[...] = jnp.sum(jnp.where(select_ref[...] > 0.5, scores_ref[...], 0.0), axis=0, keepdims=True)


def adam(grad, old, first, second):
    first_new = beta_one * first + (1.0 - beta_one) * grad
    second_new = beta_two * second + (1.0 - beta_two) * grad * grad
    update = (first_new * (1.0 / (1.0 - beta_one**adam_step))) / (
        jnp.sqrt(second_new * (1.0 / (1.0 - beta_two**adam_step))) + adam_eps
    )
    return old - learn_rate * (update + decay_rate * old), first_new, second_new


def final_kernel(
    position_ref,
    offsets_ref,
    joined_ref,
    turned_ref,
    heads_ref,
    master_any,
    first_any,
    second_any,
    out_master,
    out_first,
    out_second,
    weight_ref,
    sums,
    old,
    first,
    second,
    new_old,
    new_first,
    new_second,
    head_new,
    placed,
    sems,
    *,
    even_size,
    head_rows,
):
    parts, rows, columns = joined_ref.shape
    kept = turned_ref.shape[1]
    per = weight_ref.shape[0]
    lines = columns // LANES
    before = (kept - per) * lines
    bucket_rows = old.shape[0]
    flat_rows = even_size // LANES
    loads = [
        pltpu.make_async_copy(source, target, sems.at[n])
        for n, (source, target) in enumerate(((master_any, old), (first_any, first), (second_any, second)))
    ]
    for load in loads:
        load.start()

    position = position_ref[0]
    start = offsets_ref[position]
    finish = offsets_ref[position + 1]
    shift = position * even_size - start
    next_shift = (position + 1) * even_size - finish
    length = finish - start
    whole, part = shift // LANES, shift % LANES
    next_whole, next_part = next_shift // LANES, next_shift % LANES

    step = 2 * LANES
    for at in range(0, columns, step):
        total = None
        for i in range(parts):
            piece = jnp.dot(turned_ref[i], joined_ref[i, :, at : at + step], preferred_element_type=f32)
            piece = piece.astype(bf16).astype(f32)
            total = piece if total is None else total + piece
        for c in range(step // LANES):
            sums[pl.ds(at // LANES + c, kept, stride=lines), :] = total[:, c * LANES : (c + 1) * LANES]

    for load in loads:
        load.wait()

    def slots_of(row, count, by_rows, by_lanes):
        base = row + before - by_rows
        lane = iota((count, LANES), 1)
        here, above = sums[pl.ds(base, count), :], sums[pl.ds(base - 1, count), :]
        return pltpu.roll(jnp.where(lane < LANES - by_lanes, here, above), by_lanes, 1)

    def update(row, count):
        span = pl.ds(row, count)
        grad = slots_of(row, count, whole, part)
        inside = (row + iota((count, LANES), 0)) * LANES + iota((count, LANES), 1) < length
        grad = jnp.where(inside, grad, 0.0)
        a, b, c = adam(grad, old[span, :], first[span, :], second[span, :])
        new_old[span, :] = jnp.where(inside, a, 0.0)
        new_first[span, :] = jnp.where(inside, b, 0.0)
        new_second[span, :] = jnp.where(inside, c, 0.0)

    def full(n, carry):
        update(pl.multiple_of(n * CHUNK, 8), CHUNK)
        return carry

    lax.fori_loop(0, bucket_rows // CHUNK, full, 0)
    if bucket_rows % CHUNK:
        update(bucket_rows // CHUNK * CHUNK, bucket_rows % CHUNK)
    stores = [
        pltpu.make_async_copy(source, target, sems.at[3 + n])
        for n, (source, target) in enumerate(
            ((new_old.at[pl.ds(0, bucket_rows)], out_master), (new_first, out_first), (new_second, out_second))
        )
    ]
    for store in stores:
        store.start()

    grad = slots_of(flat_rows, head_rows, next_whole, next_part)
    head_new[pl.ds(head_rows, head_rows), :] = adam(grad, heads_ref[0], heads_ref[1], heads_ref[2])[0]

    def back_from(source, row, count, by_rows, by_lanes):
        lane = iota((count, LANES), 1)
        here, below = source[pl.ds(row + by_rows, count), :], source[pl.ds(row + by_rows + 1, count), :]
        return pltpu.roll(jnp.where(lane >= by_lanes, here, below), LANES - by_lanes, 1)

    def place(n, carry):
        row = pl.multiple_of(n * CHUNK, 8)
        placed[pl.ds(row, CHUNK), :] = back_from(new_old, row, CHUNK, whole, part)
        return carry

    lax.fori_loop(0, flat_rows // CHUNK, place, 0)
    if flat_rows % CHUNK:
        row = flat_rows // CHUNK * CHUNK
        placed[pl.ds(row, flat_rows % CHUNK), :] = back_from(new_old, row, flat_rows % CHUNK, whole, part)
    tail = flat_rows - head_rows
    own = placed[pl.ds(tail, head_rows), :]
    other = back_from(head_new, 0, head_rows, next_whole, next_part)
    flat = (tail + iota((head_rows, LANES), 0)) * LANES + iota((head_rows, LANES), 1)
    placed[pl.ds(tail, head_rows), :] = jnp.where(flat < even_size - next_shift, own, other)
    for c in range(lines):
        weight_ref[:, c * LANES : (c + 1) * LANES] = placed[pl.ds(c, per, stride=lines), :].astype(bf16)

    for store in stores:
        store.wait()


def vmem():
    return pl.BlockSpec(memory_space=pltpu.VMEM)


def anywhere():
    return pl.BlockSpec(memory_space=pl.ANY)


def smem():
    return pl.BlockSpec(memory_space=pltpu.SMEM)


def call(kernel, outs, args, name, flops=0, moved=0):
    many = isinstance(outs, (list, tuple))
    return pl.pallas_call(
        kernel,
        out_shape=outs,
        in_specs=[vmem()] * len(args),
        out_specs=[vmem()] * len(outs) if many else vmem(),
        compiler_params=params(),
        cost_estimate=cost(flops, moved),
        name=name,
    )(*args)


def struct(shape, kind):
    return jax.ShapeDtypeStruct(shape, kind)


def shards(
    tokens,
    out_grad,
    gate_up,
    route_weight,
    routes,
    down_weight,
    master,
    moment_one,
    moment_two,
    offsets,
):
    token_count, model_width = tokens.shape
    columns = gate_up.shape[2]
    hidden = columns // 2
    bucket_cap = master.shape[2]
    groups = lax.axis_size("expert")
    parts = lax.axis_size("dp")
    experts = groups * master.shape[0]
    cap = 2 * token_count // experts
    rows = experts * cap
    per = model_width // parts
    even_size = per * columns
    margin = bucket_cap - even_size
    extra = round_up(-(-margin // columns), 16)
    width = round_up(per + extra + 1, LANES)
    kept = per + extra
    lines = columns // LANES
    bucket_rows = bucket_cap // LANES
    head_rows = round_up(margin // LANES, 8)

    down = lax.all_gather(down_weight, "dp", axis=1, tiled=True)[0]
    packed, select, target = call(
        functools.partial(pack_kernel, experts=experts, cap=cap),
        [
            struct((rows, model_width + columns + LANES), bf16),
            struct((rows, token_count), f32),
            struct((1, token_count), f32),
        ],
        (
            routes.reshape(1, token_count),
            route_weight.reshape(1, token_count),
            out_grad,
            gate_up.reshape(token_count, columns),
        ),
        "pack",
        moved=6_000_000,
    )
    arrived = lax.all_to_all(
        packed.reshape(experts, cap, packed.shape[1]), "expert", split_axis=0, concat_axis=0, tiled=True
    )
    windows = call(
        functools.partial(window_kernel, per=per, lead=width - per),
        struct((parts, token_count, width), bf16),
        (target, tokens),
        "window",
        moved=2_000_000,
    )
    windows = lax.all_to_all(windows, "dp", split_axis=0, concat_axis=0, tiled=True)
    heads = jnp.concatenate([master, moment_one, moment_two], axis=0)[:, 0, : head_rows * LANES]
    heads = lax.ppermute(heads, "dp", [(i + 1, i) for i in range(parts - 1)])
    heads = heads.reshape(3, head_rows, LANES)
    compacted = call(
        compact_kernel,
        struct((experts, parts, cap, width), bf16),
        (windows,),
        "compact",
        moved=3_000_000,
    )
    compacted = lax.all_to_all(compacted, "expert", split_axis=0, concat_axis=0, tiled=True)
    joined, scores = call(
        row_kernel,
        [struct((rows, columns), bf16), struct((rows, LANES), f32)],
        (arrived.reshape(rows, packed.shape[1]), down),
        "rows",
        flops=2 * rows * model_width * hidden,
        moved=8_000_000,
    )
    turned = call(
        turn_kernel,
        struct((parts, kept, rows), bf16),
        (compacted,),
        "turn",
        moved=3_000_000,
    )
    gathered = lax.all_gather(joined, "dp", axis=0, tiled=False)
    scores = lax.all_to_all(
        scores.reshape(experts, cap, LANES), "expert", split_axis=0, concat_axis=0, tiled=True
    )
    router_grad = call(
        router_kernel,
        struct((1, token_count), f32),
        (select, scores.reshape(rows, LANES)),
        "router",
        moved=300_000,
    )
    state = struct((bucket_rows, LANES), f32)
    position = lax.axis_index("dp").astype(i32).reshape(1)
    kernel = functools.partial(final_kernel, even_size=even_size, head_rows=head_rows)
    flat_rows = even_size // LANES
    new_master, new_one, new_two, new_weight = pl.pallas_call(
        kernel,
        out_shape=[state, state, state, struct((per, columns), bf16)],
        in_specs=[smem(), smem(), vmem(), vmem(), vmem(), anywhere(), anywhere(), anywhere()],
        out_specs=[anywhere(), anywhere(), anywhere(), vmem()],
        scratch_shapes=[
            pltpu.VMEM((round_up(kept * lines + head_rows + 8, 8), LANES), f32),
            pltpu.VMEM((bucket_rows, LANES), f32),
            pltpu.VMEM((bucket_rows, LANES), f32),
            pltpu.VMEM((bucket_rows, LANES), f32),
            pltpu.VMEM((round_up(flat_rows + head_rows + 8, 8), LANES), f32),
            pltpu.VMEM((bucket_rows, LANES), f32),
            pltpu.VMEM((bucket_rows, LANES), f32),
            pltpu.VMEM((3 * head_rows + 8, LANES), f32),
            pltpu.VMEM((flat_rows, LANES), f32),
            pltpu.SemaphoreType.DMA((6,)),
        ],
        compiler_params=params(),
        cost_estimate=cost(2 * parts * rows * kept * columns, 25_000_000),
        name="final",
    )(
        position,
        offsets,
        gathered,
        turned,
        heads,
        master.reshape(bucket_rows, LANES),
        moment_one.reshape(bucket_rows, LANES),
        moment_two.reshape(bucket_rows, LANES),
    )
    return (
        new_master.reshape(1, 1, bucket_cap),
        new_one.reshape(1, 1, bucket_cap),
        new_two.reshape(1, 1, bucket_cap),
        new_weight[None],
        router_grad.reshape(token_count, 1),
    )


def solution(mesh):
    placed = (
        P(("dp", "expert"), None),
        P(("dp", "expert"), None),
        P(("dp", "expert"), None, None),
        P(("dp", "expert"), None),
        P(("dp", "expert"), None),
        P("expert", "dp", None),
        P("expert", "dp", None),
        P("expert", "dp", None),
        P("expert", "dp", None),
        P(),
    )
    return jax.shard_map(
        shards,
        mesh=mesh,
        in_specs=placed,
        out_specs=(
            P("expert", "dp", None),
            P("expert", "dp", None),
            P("expert", "dp", None),
            P("expert", "dp", None),
            P(("dp", "expert"), None),
        ),
        check_vma=False,
    )
```

```python
import functools

import jax
import jax.numpy as jnp
from jax import lax
from jax.experimental import pallas as pl
from jax.experimental.pallas import tpu as pltpu
from jax.sharding import PartitionSpec as P

beta_one = 0.9
beta_two = 0.95
learn_rate = 0.001
decay_rate = 0.1
adam_eps = 1e-08
adam_step = 20.0

LANES = 128
CHUNK = 120
VMEM_LIMIT = 56 * 1024 * 1024

f32 = jnp.float32
bf16 = jnp.bfloat16
i32 = jnp.int32


def round_up(value, unit):
    return -(-value // unit) * unit


def iota(shape, axis):
    return lax.broadcasted_iota(i32, shape, axis)


def params():
    return pltpu.CompilerParams(vmem_limit_bytes=VMEM_LIMIT)


def cost(flops, moved):
    return pl.CostEstimate(flops=int(flops), bytes_accessed=int(moved), transcendentals=0)


def pack_kernel(me_ref, routes_ref, weight_ref, grads_ref, saved_ref, select_ref, target_ref, *packed_refs, cap):
    ids = routes_ref[...]
    experts = len(packed_refs)
    count = ids.shape[1]
    width = grads_ref.shape[1]
    hits = iota((round_up(experts, 8), count), 0) == ids
    before = (iota((count, count), 0) < iota((count, count), 1)).astype(bf16)
    earlier = jnp.dot(hits.astype(f32).astype(bf16), before, preferred_element_type=f32)
    slot = jnp.sum(jnp.where(hits, earlier, 0.0), axis=0, keepdims=True)
    target = (ids ^ me_ref[0]) * cap + slot.astype(i32)
    chosen = iota((experts * cap, count), 0) == target
    select = chosen.astype(f32).astype(bf16)
    select_ref[...] = chosen.astype(f32)
    target_ref[...] = target.astype(f32)
    grads = jnp.dot(select, grads_ref[...], preferred_element_type=f32).astype(bf16)
    saved = jnp.dot(select, saved_ref[...], preferred_element_type=f32).astype(bf16)
    weight = jnp.sum(jnp.where(chosen, weight_ref[...].astype(f32), 0.0), axis=1, keepdims=True)
    weight = jnp.broadcast_to(weight, (experts * cap, LANES)).astype(bf16)
    for k, packed_ref in enumerate(packed_refs):
        span = slice(k * cap, (k + 1) * cap)
        packed_ref[:, :width] = grads[span]
        packed_ref[:, width:-LANES] = saved[span]
        packed_ref[:, -LANES:] = weight[span]


def window_kernel(position_ref, target_ref, tokens_ref, *refs, per, lead):
    out_refs, held = refs[:-1], refs[-1]
    parts, count, width = held.shape
    diagonal = iota((count, count), 0) == iota((count, count), 1)
    column = jnp.sum(jnp.where(diagonal, target_ref[...], 0.0), axis=1, keepdims=True)
    note = jnp.broadcast_to(column, (count, width)).astype(bf16)
    lane = iota((count, width), 1)
    for j in range(parts):
        start = per * j - lead
        if start < 0:
            blank = jnp.zeros((count, -start), bf16)
            piece = jnp.concatenate([blank, tokens_ref[:, : start + width]], axis=1)
        else:
            piece = tokens_ref[:, start : start + width]
        held[j] = jnp.where(lane == 0, note, piece)
    for d, out_ref in enumerate(out_refs):
        out_ref[...] = held[position_ref[0] ^ d]


def compact_kernel(position_ref, *refs, parts):
    window_refs, out_refs = refs[:parts], refs[parts:]
    count = window_refs[0].shape[0]
    experts, cap = len(out_refs), out_refs[0].shape[1]
    diagonal = iota((count, count), 0) == iota((count, count), 1)
    slots = iota((experts * cap, count), 0)
    for d, window_ref in enumerate(window_refs):
        block = window_ref[...]
        column = block[:, 0:1].astype(f32)
        target = jnp.sum(jnp.where(diagonal, column, 0.0), axis=0, keepdims=True).astype(i32)
        select = (slots == target).astype(f32).astype(bf16)
        rows = jnp.dot(select, block, preferred_element_type=f32).astype(bf16)
        for k, out_ref in enumerate(out_refs):
            out_ref[position_ref[0] ^ d] = rows[k * cap : (k + 1) * cap]


def turn_kernel(*refs):
    row_refs, out_ref = refs[:-1], refs[-1]
    parts, _, width = row_refs[0].shape
    kept = out_ref.shape[1]
    for i in range(parts):
        slab = jnp.concatenate([ref[i] for ref in row_refs], axis=0)
        out_ref[i] = slab.T[width - kept :, :]


def row_kernel(position_ref, *refs, experts, pieces, halves, chips):
    arrived_refs, refs = refs[:experts], refs[experts:]
    down_refs, refs = refs[:pieces], refs[pieces:]
    gate_ref, up_ref, refs = refs[0], refs[1], refs[2:]
    score_refs, (down, sems) = refs[:experts], refs[experts:]
    hidden, width = down.shape
    cap = score_refs[0].shape[0]
    loads = []
    if pieces == 1:
        loads.append(pltpu.make_async_copy(down_refs[0], down, sems.at[0]))
    else:
        size = hidden // pieces
        for n, down_ref in enumerate(down_refs):
            k, other, half = n // (2 * halves), n // halves % 2, n % halves
            slab = lax.rem(position_ref[0] + 2 * (chips - k), 2 * chips) ^ other
            at = pl.multiple_of((slab * halves + half) * size, 16)
            loads.append(pltpu.make_async_copy(down_ref, down.at[pl.ds(at, size)], sems.at[n]))
    for load in loads:
        load.start()
    arrived = jnp.concatenate([ref[...] for ref in arrived_refs], axis=0)
    gate = arrived[:, width : width + hidden].astype(f32)
    up = arrived[:, width + hidden : width + 2 * hidden].astype(f32)
    weight = arrived[:, width + 2 * hidden :].astype(f32)[:, 0:1]
    sig = jax.nn.sigmoid(gate)
    for load in loads:
        load.wait()
    back = lax.dot_general(arrived[:, :width], down[...], (((1,), (1,)), ((), ())), preferred_element_type=f32)
    scores = jnp.sum(gate * sig * up * back, axis=1, keepdims=True)
    for k, score_ref in enumerate(score_refs):
        score_ref[...] = jnp.broadcast_to(scores[k * cap : (k + 1) * cap], (cap, LANES))
    scaled = weight * back
    gate_ref[...] = (scaled * up * sig * (1.0 + gate * (1.0 - sig))).astype(bf16)
    up_ref[...] = (scaled * gate * sig).astype(bf16)


def router_kernel(select_ref, *refs):
    score_refs, out_ref = refs[:-1], refs[-1]
    scores = jnp.concatenate([ref[...] for ref in score_refs], axis=0)
    out_ref[...] = jnp.sum(jnp.where(select_ref[...] > 0.5, scores, 0.0), axis=0, keepdims=True)


def slab_sum(total, turned_ref, slabs, joined_refs, at, step):
    for slab, joined_ref in zip(slabs, joined_refs):
        piece = jnp.dot(turned_ref[slab], joined_ref[:, at : at + step], preferred_element_type=f32)
        piece = piece.astype(bf16).astype(f32)
        total = piece if total is None else total + piece
    return total


def slabs_of(position, first, count, chips):
    own = [lax.rem(position + 2 * (chips - k), 2 * chips) for k in range(first, first + count)]
    return [slab ^ other for slab in own for other in (0, 1)]


def early_kernel(position_ref, turned_ref, *refs, chips):
    joined_refs, sum_ref = refs[:-1], refs[-1]
    slabs = slabs_of(position_ref[0], 0, chips - 1, chips)
    hidden = joined_refs[0].shape[1]
    step = 2 * LANES
    for half in range(2):
        for at in range(0, hidden, step):
            total = slab_sum(None, turned_ref, slabs, joined_refs[half::2], at, step)
            sum_ref[:, half * hidden + at : half * hidden + at + step] = total


def adam(grad, old, first, second):
    first_new = beta_one * first + (1.0 - beta_one) * grad
    second_new = beta_two * second + (1.0 - beta_two) * grad * grad
    update = (first_new * (1.0 / (1.0 - beta_one**adam_step))) / (
        jnp.sqrt(second_new * (1.0 / (1.0 - beta_two**adam_step))) + adam_eps
    )
    return old - learn_rate * (update + decay_rate * old), first_new, second_new


def final_kernel(
    position_ref,
    offsets_ref,
    turned_ref,
    early_ref,
    heads_ref,
    gate_own,
    up_own,
    gate_other,
    up_other,
    master_any,
    first_any,
    second_any,
    out_master,
    out_first,
    out_second,
    weight_ref,
    sums,
    old,
    first,
    second,
    new_old,
    new_first,
    new_second,
    head_new,
    placed,
    sems,
    *,
    even_size,
    head_rows,
    chips,
):
    kept, columns = early_ref.shape
    per = weight_ref.shape[0]
    lines = columns // LANES
    before = (kept - per) * lines
    bucket_rows = old.shape[0]
    flat_rows = even_size // LANES
    loads = [
        pltpu.make_async_copy(source, target, sems.at[n])
        for n, (source, target) in enumerate(((master_any, old), (first_any, first), (second_any, second)))
    ]
    for load in loads:
        load.start()

    position = position_ref[0]
    start = offsets_ref[position]
    finish = offsets_ref[position + 1]
    shift = position * even_size - start
    next_shift = (position + 1) * even_size - finish
    length = finish - start
    whole, part = shift // LANES, shift % LANES
    next_whole, next_part = next_shift // LANES, next_shift % LANES

    step = 2 * LANES
    slabs = slabs_of(position, chips - 1, 1, chips)
    for half, joined_refs in enumerate(((gate_own, gate_other), (up_own, up_other))):
        for at in range(0, columns // 2, step):
            begin = half * columns // 2 + at
            total = slab_sum(early_ref[:, begin : begin + step], turned_ref, slabs, joined_refs, at, step)
            for c in range(step // LANES):
                sums[pl.ds(begin // LANES + c, kept, stride=lines), :] = total[:, c * LANES : (c + 1) * LANES]

    for load in loads:
        load.wait()

    def slots_of(row, count, by_rows, by_lanes):
        base = row + before - by_rows
        lane = iota((count, LANES), 1)
        here, above = sums[pl.ds(base, count), :], sums[pl.ds(base - 1, count), :]
        return pltpu.roll(jnp.where(lane < LANES - by_lanes, here, above), by_lanes, 1)

    def update(row, count):
        span = pl.ds(row, count)
        grad = slots_of(row, count, whole, part)
        inside = (row + iota((count, LANES), 0)) * LANES + iota((count, LANES), 1) < length
        grad = jnp.where(inside, grad, 0.0)
        a, b, c = adam(grad, old[span, :], first[span, :], second[span, :])
        new_old[span, :] = jnp.where(inside, a, 0.0)
        new_first[span, :] = jnp.where(inside, b, 0.0)
        new_second[span, :] = jnp.where(inside, c, 0.0)

    def full(n, carry):
        update(pl.multiple_of(n * CHUNK, 8), CHUNK)
        return carry

    lax.fori_loop(0, bucket_rows // CHUNK, full, 0)
    if bucket_rows % CHUNK:
        update(bucket_rows // CHUNK * CHUNK, bucket_rows % CHUNK)
    stores = [
        pltpu.make_async_copy(source, target, sems.at[3 + n])
        for n, (source, target) in enumerate(
            ((new_old.at[pl.ds(0, bucket_rows)], out_master), (new_first, out_first), (new_second, out_second))
        )
    ]
    for store in stores:
        store.start()

    grad = slots_of(flat_rows, head_rows, next_whole, next_part)
    head_new[pl.ds(head_rows, head_rows), :] = adam(grad, heads_ref[0], heads_ref[1], heads_ref[2])[0]

    def back_from(source, row, count, by_rows, by_lanes):
        lane = iota((count, LANES), 1)
        here, below = source[pl.ds(row + by_rows, count), :], source[pl.ds(row + by_rows + 1, count), :]
        return pltpu.roll(jnp.where(lane >= by_lanes, here, below), LANES - by_lanes, 1)

    def place(n, carry):
        row = pl.multiple_of(n * CHUNK, 8)
        placed[pl.ds(row, CHUNK), :] = back_from(new_old, row, CHUNK, whole, part)
        return carry

    lax.fori_loop(0, flat_rows // CHUNK, place, 0)
    if flat_rows % CHUNK:
        row = flat_rows // CHUNK * CHUNK
        placed[pl.ds(row, flat_rows % CHUNK), :] = back_from(new_old, row, flat_rows % CHUNK, whole, part)
    tail = flat_rows - head_rows
    own = placed[pl.ds(tail, head_rows), :]
    other = back_from(head_new, 0, head_rows, next_whole, next_part)
    flat = (tail + iota((head_rows, LANES), 0)) * LANES + iota((head_rows, LANES), 1)
    placed[pl.ds(tail, head_rows), :] = jnp.where(flat < even_size - next_shift, own, other)
    for c in range(lines):
        weight_ref[:, c * LANES : (c + 1) * LANES] = placed[pl.ds(c, per, stride=lines), :].astype(bf16)

    for store in stores:
        store.wait()


def vmem():
    return pl.BlockSpec(memory_space=pltpu.VMEM)


def anywhere():
    return pl.BlockSpec(memory_space=pl.ANY)


def smem():
    return pl.BlockSpec(memory_space=pltpu.SMEM)


def call(kernel, outs, scalars, args, name, flops=0, moved=0, scratch=()):
    many = isinstance(outs, (list, tuple))
    return pl.pallas_call(
        kernel,
        out_shape=outs,
        in_specs=[smem()] * len(scalars) + [vmem()] * len(args),
        out_specs=[vmem()] * len(outs) if many else vmem(),
        scratch_shapes=scratch,
        compiler_params=params(),
        cost_estimate=cost(flops, moved),
        name=name,
    )(*scalars, *args)


def struct(shape, kind):
    return jax.ShapeDtypeStruct(shape, kind)


def shards(
    tokens,
    out_grad,
    gate_up,
    route_weight,
    routes,
    down_weight,
    master,
    moment_one,
    moment_two,
    offsets,
):
    token_count, model_width = tokens.shape
    columns = gate_up.shape[2]
    hidden = columns // 2
    bucket_cap = master.shape[2]
    groups = lax.axis_size("expert")
    parts = lax.axis_size("dp")
    experts = groups * master.shape[0]
    cap = 2 * token_count // experts
    rows = experts * cap
    per = model_width // parts
    even_size = per * columns
    margin = bucket_cap - even_size
    extra = round_up(-(-margin // columns), 16)
    width = round_up(per + extra + 1, LANES)
    kept = per + extra
    lines = columns // LANES
    bucket_rows = bucket_cap // LANES
    head_rows = round_up(margin // LANES, 8)

    chips = parts // 2
    position = lax.axis_index("dp").astype(i32).reshape(1)
    me = lax.axis_index("expert").astype(i32).reshape(1)

    def onward(block):
        return lax.ppermute(block, "dp", [(i, (i + 2) % parts) for i in range(parts)])

    def swapped(block):
        return lax.ppermute(block, "dp", [(i, i ^ 1) for i in range(parts)])

    def line_gather(blocks):
        held = [blocks]
        for _ in range(chips - 1):
            held.append([onward(block) for block in held[-1]])
        return held, [[swapped(block) for block in step] for step in held]

    def exchanged(blocks, axis, size):
        return [blocks[0]] + [
            lax.ppermute(blocks[k], axis, [(i, i ^ k) for i in range(size)]) for k in range(1, size)
        ]

    down_rows = down_weight.shape[1]
    if down_rows % 32 == 0:
        halves = 2
        size = down_rows // halves
        held, other = line_gather([down_weight[0, h * size : (h + 1) * size] for h in range(halves)])
        down = [block for pair in zip(held, other) for step in pair for block in step]
        last_down = held[-1][-1]
    else:
        halves = 1
        down = [lax.all_gather(down_weight, "dp", axis=1, tiled=True)[0]]
        last_down = down[0]

    wide = model_width + columns + LANES
    select, target, *packed = call(
        functools.partial(pack_kernel, cap=cap),
        [struct((rows, token_count), f32), struct((1, token_count), f32)] + [struct((cap, wide), bf16)] * experts,
        (me,),
        (
            routes.reshape(1, token_count),
            route_weight.reshape(1, token_count),
            out_grad,
            gate_up.reshape(token_count, columns),
        ),
        "pack",
        moved=6_000_000,
    )
    arrived = exchanged(packed, "expert", experts)
    heads = jnp.concatenate([master, moment_one, moment_two], axis=0)[:, 0, : head_rows * LANES]
    heads = lax.ppermute(heads, "dp", [(i + 1, i) for i in range(parts - 1)])
    heads = heads.reshape(3, head_rows, LANES)
    windows = call(
        functools.partial(window_kernel, per=per, lead=width - per),
        [struct((token_count, width), bf16)] * parts,
        (position,),
        (target, tokens),
        "window",
        moved=2_000_000,
        scratch=[pltpu.VMEM((parts, token_count, width), bf16)],
    )
    gate, up, *scores = pl.pallas_call(
        functools.partial(row_kernel, experts=experts, pieces=len(down), halves=halves, chips=chips),
        out_shape=[struct((rows, hidden), bf16)] * 2 + [struct((cap, LANES), f32)] * experts,
        in_specs=[smem()] + [vmem()] * experts + [anywhere()] * len(down),
        out_specs=[vmem()] * (2 + experts),
        scratch_shapes=[
            pltpu.VMEM((hidden, model_width), bf16),
            pltpu.SemaphoreType.DMA((len(down),)),
        ],
        compiler_params=params(),
        cost_estimate=cost(2 * rows * model_width * hidden, 8_000_000),
        name="rows",
    )(position, *arrived, *down)
    held, other = line_gather([gate, up])
    windows, _ = lax.optimization_barrier((windows, last_down))
    windows = exchanged(windows, "dp", parts)
    compacted = call(
        functools.partial(compact_kernel, parts=parts),
        [struct((parts, cap, width), bf16)] * experts,
        (position,),
        windows,
        "compact",
        moved=3_000_000,
    )
    compacted = exchanged(compacted, "expert", experts)
    turned = call(
        turn_kernel,
        struct((parts, kept, rows), bf16),
        (),
        compacted,
        "turn",
        moved=3_000_000,
    )
    early = call(
        functools.partial(early_kernel, chips=chips),
        struct((kept, columns), f32),
        (position,),
        [turned] + [block for pair in zip(held[:-1], other[:-1]) for step in pair for block in step],
        "early",
        flops=2 * (parts - 2) * rows * kept * columns,
        moved=8_000_000,
    )
    scores = exchanged(scores, "expert", experts)
    router_grad = call(
        router_kernel,
        struct((1, token_count), f32),
        (),
        [select] + scores,
        "router",
        moved=300_000,
    )
    state = struct((bucket_rows, LANES), f32)
    kernel = functools.partial(final_kernel, even_size=even_size, head_rows=head_rows, chips=chips)
    flat_rows = even_size // LANES
    new_master, new_one, new_two, new_weight = pl.pallas_call(
        kernel,
        out_shape=[state, state, state, struct((per, columns), bf16)],
        in_specs=[smem()] * 2 + [vmem()] * 7 + [anywhere()] * 3,
        out_specs=[anywhere(), anywhere(), anywhere(), vmem()],
        scratch_shapes=[
            pltpu.VMEM((round_up(kept * lines + head_rows + 8, 8), LANES), f32),
            pltpu.VMEM((bucket_rows, LANES), f32),
            pltpu.VMEM((bucket_rows, LANES), f32),
            pltpu.VMEM((bucket_rows, LANES), f32),
            pltpu.VMEM((round_up(flat_rows + head_rows + 8, 8), LANES), f32),
            pltpu.VMEM((bucket_rows, LANES), f32),
            pltpu.VMEM((bucket_rows, LANES), f32),
            pltpu.VMEM((3 * head_rows + 8, LANES), f32),
            pltpu.VMEM((flat_rows, LANES), f32),
            pltpu.SemaphoreType.DMA((6,)),
        ],
        compiler_params=params(),
        cost_estimate=cost(4 * rows * kept * columns, 25_000_000),
        name="final",
    )(
        position,
        offsets,
        turned,
        early,
        heads,
        *held[-1],
        *other[-1],
        master.reshape(bucket_rows, LANES),
        moment_one.reshape(bucket_rows, LANES),
        moment_two.reshape(bucket_rows, LANES),
    )
    return (
        new_master.reshape(1, 1, bucket_cap),
        new_one.reshape(1, 1, bucket_cap),
        new_two.reshape(1, 1, bucket_cap),
        new_weight[None],
        router_grad.reshape(token_count, 1),
    )


def solution(mesh):
    placed = (
        P(("dp", "expert"), None),
        P(("dp", "expert"), None),
        P(("dp", "expert"), None, None),
        P(("dp", "expert"), None),
        P(("dp", "expert"), None),
        P("expert", "dp", None),
        P("expert", "dp", None),
        P("expert", "dp", None),
        P("expert", "dp", None),
        P(),
    )
    return jax.shard_map(
        shards,
        mesh=mesh,
        in_specs=placed,
        out_specs=(
            P("expert", "dp", None),
            P("expert", "dp", None),
            P("expert", "dp", None),
            P("expert", "dp", None),
            P(("dp", "expert"), None),
        ),
        check_vma=False,
    )
```

```python
import functools

import jax
import jax.numpy as jnp
from jax import lax
from jax.experimental import pallas as pl
from jax.experimental.pallas import tpu as pltpu
from jax.sharding import PartitionSpec as P

beta_one = 0.9
beta_two = 0.95
learn_rate = 0.001
decay_rate = 0.1
adam_eps = 1e-08
adam_step = 20.0

LANES = 128
CHUNK = 120

f32 = jnp.float32
bf16 = jnp.bfloat16
i32 = jnp.int32


def round_up(value, unit):
    return -(-value // unit) * unit


def iota(shape, axis):
    return lax.broadcasted_iota(i32, shape, axis)


def params(mib):
    return pltpu.CompilerParams(vmem_limit_bytes=mib * 1024 * 1024)


def cost(flops, moved):
    return pl.CostEstimate(flops=int(flops), bytes_accessed=int(moved), transcendentals=0)


def pack_kernel(me_ref, routes_ref, weight_ref, grads_ref, saved_ref, select_ref, target_ref, *packed_refs, cap):
    ids = routes_ref[...]
    experts = len(packed_refs)
    count = ids.shape[1]
    width = grads_ref.shape[1]
    hits = iota((round_up(experts, 8), count), 0) == ids
    before = (iota((count, count), 0) < iota((count, count), 1)).astype(bf16)
    earlier = jnp.dot(hits.astype(f32).astype(bf16), before, preferred_element_type=f32)
    slot = jnp.sum(jnp.where(hits, earlier, 0.0), axis=0, keepdims=True)
    target = (ids ^ me_ref[0]) * cap + slot.astype(i32)
    chosen = iota((experts * cap, count), 0) == target
    select = chosen.astype(f32).astype(bf16)
    select_ref[...] = chosen.astype(f32)
    target_ref[...] = target.astype(f32)
    grads = jnp.dot(select, grads_ref[...], preferred_element_type=f32).astype(bf16)
    saved = jnp.dot(select, saved_ref[...], preferred_element_type=f32).astype(bf16)
    weight = jnp.sum(jnp.where(chosen, weight_ref[...].astype(f32), 0.0), axis=1, keepdims=True)
    weight = jnp.broadcast_to(weight, (experts * cap, LANES)).astype(bf16)
    for k, packed_ref in enumerate(packed_refs):
        span = slice(k * cap, (k + 1) * cap)
        packed_ref[:, :width] = grads[span]
        packed_ref[:, width:-LANES] = saved[span]
        packed_ref[:, -LANES:] = weight[span]


def window_kernel(target_ref, tokens_ref, out_ref, *, per, lead):
    parts, count, width = out_ref.shape
    diagonal = iota((count, count), 0) == iota((count, count), 1)
    column = jnp.sum(jnp.where(diagonal, target_ref[...], 0.0), axis=1, keepdims=True)
    note = jnp.broadcast_to(column, (count, width)).astype(bf16)
    lane = iota((count, width), 1)
    for j in range(parts):
        start = per * j - lead
        if start < 0:
            blank = jnp.zeros((count, -start), bf16)
            piece = jnp.concatenate([blank, tokens_ref[:, : start + width]], axis=1)
        else:
            piece = tokens_ref[:, start : start + width]
        out_ref[j] = jnp.where(lane == 0, note, piece)


def compact_kernel(me_ref, windows_ref, out_ref):
    parts, count, width = windows_ref.shape
    experts, _, cap, _ = out_ref.shape
    diagonal = iota((count, count), 0) == iota((count, count), 1)
    slots = iota((experts * cap, count), 0)
    for i in range(parts):
        block = windows_ref[i]
        column = block[:, 0:1].astype(f32)
        target = jnp.sum(jnp.where(diagonal, column, 0.0), axis=0, keepdims=True).astype(i32)
        select = (slots == target).astype(f32).astype(bf16)
        rows = jnp.dot(select, block, preferred_element_type=f32).astype(bf16)
        for k in range(experts):
            out_ref[me_ref[0] ^ k, i] = rows[k * cap : (k + 1) * cap]


def turn_kernel(me_ref, rows_ref, out_ref):
    experts, parts, _, width = rows_ref.shape
    kept = out_ref.shape[1]
    for i in range(parts):
        slab = jnp.concatenate([rows_ref[me_ref[0] ^ k, i] for k in range(experts)], axis=0)
        out_ref[i] = slab.T[width - kept :, :]


def factor_kernel(*refs):
    arrived_refs, (grads_ref, gate_ref, up_ref, score_ref) = refs[:-4], refs[-4:]
    cap = arrived_refs[0].shape[0]
    width, hidden = grads_ref.shape[1], gate_ref.shape[1]
    for k, arrived_ref in enumerate(arrived_refs):
        span = slice(k * cap, (k + 1) * cap)
        grads_ref[span, :] = arrived_ref[:, :width]
        gate = arrived_ref[:, width : width + hidden].astype(f32)
        up = arrived_ref[:, width + hidden : width + 2 * hidden].astype(f32)
        weight = arrived_ref[:, width + 2 * hidden :].astype(f32)[:, 0:1]
        sig = jax.nn.sigmoid(gate)
        act = gate * sig
        score_ref[span, :] = act * up
        up_ref[span, :] = weight * act
        gate_ref[span, :] = weight * (up * sig * (1.0 + gate * (1.0 - sig)))


def row_kernel(position_ref, me_ref, grads_ref, gate_factor, up_factor, score_factor, *refs, chips):
    down_refs, (gate_ref, up_ref, joined_ref, scores_ref, down, sems) = refs[:-6], refs[-6:]
    pieces = len(down_refs)
    hidden = down.shape[0]
    size = hidden // pieces
    loads = []
    for n, down_ref in enumerate(down_refs):
        if pieces == 1:
            loads.append(pltpu.make_async_copy(down_ref, down, sems.at[0]))
        else:
            slab = lax.rem(position_ref[0] + 2 * (chips - n // 2), 2 * chips) ^ (n % 2)
            at = pl.multiple_of(slab * size, 16)
            loads.append(pltpu.make_async_copy(down_ref, down.at[pl.ds(at, size)], sems.at[n]))
    for load in loads:
        load.start()
    for load in loads:
        load.wait()
    scores = None
    step = 2 * LANES
    for at in range(0, hidden, step):
        span = slice(at, at + step)
        back = lax.dot_general(
            grads_ref[...], down[span, :], (((1,), (1,)), ((), ())), preferred_element_type=f32
        )
        part = jnp.sum(score_factor[:, span] * back, axis=1, keepdims=True)
        scores = part if scores is None else scores + part
        gate = (gate_factor[:, span] * back).astype(bf16)
        up = (up_factor[:, span] * back).astype(bf16)
        gate_ref[:, span] = gate
        up_ref[:, span] = up
        joined_ref[:, span] = gate
        joined_ref[:, hidden + at : hidden + at + step] = up
    experts, cap, _ = scores_ref.shape
    for k in range(experts):
        scores_ref[me_ref[0] ^ k] = jnp.broadcast_to(scores[k * cap : (k + 1) * cap], (cap, LANES))


def router_kernel(me_ref, select_ref, scores_ref, out_ref):
    experts = scores_ref.shape[0]
    scores = jnp.concatenate([scores_ref[me_ref[0] ^ k] for k in range(experts)], axis=0)
    out_ref[...] = jnp.sum(jnp.where(select_ref[...] > 0.5, scores, 0.0), axis=0, keepdims=True)


def slab_sum(total, turned_ref, slabs, joined):
    for slab, (ref, at, step) in zip(slabs, joined):
        piece = jnp.dot(turned_ref[slab], ref[:, at : at + step], preferred_element_type=f32)
        piece = piece.astype(bf16).astype(f32)
        total = piece if total is None else total + piece
    return total


def slabs_of(position, steps, chips):
    own = [lax.rem(position + 2 * (chips - k), 2 * chips) for k in steps]
    return [slab ^ other for slab in own for other in (0, 1)]


def early_kernel(position_ref, turned_ref, *refs, steps, chips):
    refs, sum_ref = list(refs[:-1]), refs[-1]
    hidden = sum_ref.shape[1] // 2
    step = 2 * LANES
    slabs = slabs_of(position_ref[0], steps, chips)
    lists = ([], [])
    for k in steps:
        for other in range(2):
            whole = refs.pop(0) if k == 0 else None
            for half in range(2):
                lists[half].append((whole, half * hidden) if k == 0 else (refs.pop(0), 0))
    base = refs[0] if refs else None
    for half in range(2):
        for at in range(0, hidden, step):
            span = slice(half * hidden + at, half * hidden + at + step)
            joined = [(ref, first + at, step) for ref, first in lists[half]]
            total = None if base is None else base[:, span]
            sum_ref[:, span] = slab_sum(total, turned_ref, slabs, joined)


def adam(grad, old, first, second):
    first_new = beta_one * first + (1.0 - beta_one) * grad
    second_new = beta_two * second + (1.0 - beta_two) * grad * grad
    below = jnp.sqrt(second_new * (1.0 / (1.0 - beta_two**adam_step))) + adam_eps
    update = first_new * (learn_rate / (1.0 - beta_one**adam_step)) / below
    return old * (1.0 - learn_rate * decay_rate) - update, first_new, second_new


def final_kernel(
    position_ref,
    offsets_ref,
    turned_ref,
    early_ref,
    heads_ref,
    gate_own,
    up_own,
    gate_other,
    up_other,
    old,
    first,
    second,
    out_master,
    out_first,
    out_second,
    weight_ref,
    sums,
    moved,
    new_old,
    new_first,
    new_second,
    head_new,
    sems,
    *,
    even_size,
    head_rows,
    chips,
):
    kept, columns = early_ref.shape
    hidden = columns // 2
    per = weight_ref.shape[0]
    lines = columns // LANES
    before = (kept - per) * lines
    bucket_rows = old.shape[0]
    flat_rows = even_size // LANES
    position = position_ref[0]
    start = offsets_ref[position]
    finish = offsets_ref[position + 1]
    shift = position * even_size - start
    next_shift = (position + 1) * even_size - finish
    length = finish - start
    whole, part = shift // LANES, shift % LANES
    odd = whole % 8
    next_whole, next_part = next_shift // LANES, next_shift % LANES

    step = 2 * LANES
    slabs = slabs_of(position, [chips - 1], chips)
    for half, refs in enumerate(((gate_own, gate_other), (up_own, up_other))):
        for at in range(0, hidden, step):
            begin = half * hidden + at
            total = slab_sum(
                early_ref[:, begin : begin + step], turned_ref, slabs, [(ref, at, step) for ref in refs]
            )
            for c in range(step // LANES):
                block = total[:, c * LANES : (c + 1) * LANES]
                line = begin // LANES + c
                block = pltpu.roll(block, part, 1)
                sums[pl.ds(odd + line, kept, stride=lines), :] = block
                moved[pl.ds(odd + line + 1, kept, stride=lines), :] = block

    def slots_of(row, count):
        at = pl.multiple_of(row + before - (whole - odd), 8)
        lane = iota((count, LANES), 1)
        return jnp.where(lane >= part, sums[pl.ds(at, count), :], moved[pl.ds(at, count), :])

    def update(row, count):
        span = pl.ds(row, count)
        a, b, c = adam(slots_of(row, count), old[span, :], first[span, :], second[span, :])
        new_old[span, :], new_first[span, :], new_second[span, :] = a, b, c

    def masked(row, count):
        span = pl.ds(row, count)
        inside = (row + iota((count, LANES), 0)) * LANES + iota((count, LANES), 1) < length
        grad = jnp.where(inside, slots_of(row, count), 0.0)
        a, b, c = adam(grad, old[span, :], first[span, :], second[span, :])
        new_old[span, :] = jnp.where(inside, a, 0.0)
        new_first[span, :] = jnp.where(inside, b, 0.0)
        new_second[span, :] = jnp.where(inside, c, 0.0)

    def send(begin, count, slot):
        span = pl.ds(begin, count)
        stores = [
            pltpu.make_async_copy(source.at[span], target.at[span], sems.at[slot, n])
            for n, (source, target) in enumerate(
                ((new_old, out_master), (new_first, out_first), (new_second, out_second))
            )
        ]
        for store in stores:
            store.start()
        return stores

    def chunk(n, carry):
        update(pl.multiple_of(n * CHUNK, 8), CHUNK)
        return carry

    safe = (flat_rows - head_rows) // CHUNK
    third = -(-safe // 3)
    stores = []
    for slot, begin in enumerate(range(0, safe, third)):
        end = min(begin + third, safe)
        lax.fori_loop(begin, end, chunk, 0)
        stores += send(begin * CHUNK, (end - begin) * CHUNK, slot)
    for row in range(safe * CHUNK, bucket_rows, CHUNK):
        masked(row, min(CHUNK, bucket_rows - row))
    stores += send(safe * CHUNK, bucket_rows - safe * CHUNK, 3)

    def next_slots():
        lane = iota((head_rows, LANES), 1)
        base = flat_rows + before - next_whole + odd
        here = pltpu.roll(sums[pl.ds(base, head_rows), :], (LANES - part) % LANES, 1)
        above = pltpu.roll(sums[pl.ds(base - 1, head_rows), :], (LANES - part) % LANES, 1)
        return pltpu.roll(jnp.where(lane < LANES - next_part, here, above), next_part, 1)

    edge = round_up(-(-head_rows // lines), 16)
    head_new[pl.ds(edge * lines, head_rows), :] = adam(next_slots(), heads_ref[0], heads_ref[1], heads_ref[2])[0]

    flat_row = iota((edge, LANES), 0) + (per - edge)
    for c in range(lines):
        lane = iota((per, LANES), 1)
        here = new_old[pl.ds(c + whole, per, stride=lines), :]
        below = new_old[pl.ds(c + whole + 1, per, stride=lines), :]
        own = pltpu.roll(jnp.where(lane >= part, here, below), (LANES - part) % LANES, 1)
        base = c + next_whole
        lane = iota((edge, LANES), 1)
        here = head_new[pl.ds(base, edge, stride=lines), :]
        below = head_new[pl.ds(base + 1, edge, stride=lines), :]
        other = pltpu.roll(jnp.where(lane >= next_part, here, below), (LANES - next_part) % LANES, 1)
        flat = (flat_row * lines + c) * LANES + lane
        last = jnp.where(flat < even_size - next_shift, own[per - edge :], other)
        out = slice(c * LANES, (c + 1) * LANES)
        if per > edge:
            weight_ref[: per - edge, out] = own[: per - edge].astype(bf16)
        weight_ref[per - edge :, out] = last.astype(bf16)

    for store in stores:
        store.wait()


def vmem():
    return pl.BlockSpec(memory_space=pltpu.VMEM)


def anywhere():
    return pl.BlockSpec(memory_space=pl.ANY)


def smem():
    return pl.BlockSpec(memory_space=pltpu.SMEM)


def call(kernel, outs, scalars, args, name, mib, flops=0, moved=0):
    many = isinstance(outs, (list, tuple))
    return pl.pallas_call(
        kernel,
        out_shape=outs,
        in_specs=[smem()] * len(scalars) + [vmem()] * len(args),
        out_specs=[vmem()] * len(outs) if many else vmem(),
        compiler_params=params(mib),
        cost_estimate=cost(flops, moved),
        name=name,
    )(*scalars, *args)


def struct(shape, kind):
    return jax.ShapeDtypeStruct(shape, kind)


def shards(
    tokens,
    out_grad,
    gate_up,
    route_weight,
    routes,
    down_weight,
    master,
    moment_one,
    moment_two,
    offsets,
):
    token_count, model_width = tokens.shape
    columns = gate_up.shape[2]
    hidden = columns // 2
    bucket_cap = master.shape[2]
    groups = lax.axis_size("expert")
    parts = lax.axis_size("dp")
    experts = groups * master.shape[0]
    cap = 2 * token_count // experts
    rows = experts * cap
    per = model_width // parts
    even_size = per * columns
    margin = bucket_cap - even_size
    extra = round_up(-(-margin // columns), 16)
    width = round_up(per + extra + 1, LANES)
    kept = per + extra
    lines = columns // LANES
    bucket_rows = bucket_cap // LANES
    head_rows = round_up(margin // LANES, 8)

    chips = parts // 2
    position = lax.axis_index("dp").astype(i32).reshape(1)
    me = lax.axis_index("expert").astype(i32).reshape(1)

    def onward(block):
        return lax.ppermute(block, "dp", [(i, (i + 2) % parts) for i in range(parts)])

    def swapped(block):
        return lax.ppermute(block, "dp", [(i, i ^ 1) for i in range(parts)])

    def exchanged(block, axis):
        return lax.all_to_all(block, axis, split_axis=0, concat_axis=0, tiled=True)

    def tied(*values):
        return lax.optimization_barrier(values)

    down_rows = down_weight.shape[1]
    if down_rows % 16 == 0:
        held = [down_weight[0]]
        for _ in range(chips - 1):
            held.append(onward(held[-1]))
        down = [piece for block in held for piece in (block, swapped(block))]
        last_down = held[-1]
    else:
        down = [lax.all_gather(down_weight, "dp", axis=1, tiled=True)[0]]
        last_down = down[0]

    wide = model_width + columns + LANES
    select, target, *packed = call(
        functools.partial(pack_kernel, cap=cap),
        [struct((rows, token_count), f32), struct((1, token_count), f32)] + [struct((cap, wide), bf16)] * experts,
        (me,),
        (
            routes.reshape(1, token_count),
            route_weight.reshape(1, token_count),
            out_grad,
            gate_up.reshape(token_count, columns),
        ),
        "pack",
        16,
        moved=6_000_000,
    )
    arrived = packed[:1] + [
        lax.ppermute(packed[k], "expert", [(i, i ^ k) for i in range(experts)]) for k in range(1, experts)
    ]
    windows = call(
        functools.partial(window_kernel, per=per, lead=width - per),
        struct((parts, token_count, width), bf16),
        (),
        (target, tokens),
        "window",
        12,
        moved=2_000_000,
    )
    factors = call(
        factor_kernel,
        [struct((rows, model_width), bf16)] + [struct((rows, hidden), f32)] * 3,
        (),
        arrived,
        "factors",
        20,
        moved=6_000_000,
    )
    windows, last_down = tied(windows, last_down)
    windows = exchanged(windows, "dp")
    if len(down) > 1:
        down[-2] = last_down
    gate, up, joined, scores = pl.pallas_call(
        functools.partial(row_kernel, chips=chips),
        out_shape=[struct((rows, hidden), bf16)] * 2
        + [struct((rows, columns), bf16), struct((experts, cap, LANES), f32)],
        in_specs=[smem()] * 2 + [vmem()] * 4 + [anywhere()] * len(down),
        out_specs=[vmem()] * 4,
        scratch_shapes=[
            pltpu.VMEM((hidden, model_width), bf16),
            pltpu.SemaphoreType.DMA((len(down),)),
        ],
        compiler_params=params(24),
        cost_estimate=cost(2 * rows * model_width * hidden, 8_000_000),
        name="rows",
    )(position, me, *factors, *down)

    halves = [gate, up]
    steps = [[joined, swapped(joined)]]
    compacted = call(
        compact_kernel,
        struct((experts, parts, cap, width), bf16),
        (me,),
        (windows,),
        "compact",
        12,
        moved=3_000_000,
    )
    heads = jnp.concatenate([master, moment_one, moment_two], axis=0)[:, 0, : head_rows * LANES]
    heads, _ = tied(heads, gate)
    heads = lax.ppermute(heads, "dp", [(i + 1, i) for i in range(parts - 1)])
    heads = heads.reshape(3, head_rows, LANES)
    turned = call(
        turn_kernel,
        struct((parts, kept, rows), bf16),
        (me,),
        (exchanged(compacted, "expert"),),
        "turn",
        12,
        moved=3_000_000,
    )
    router_grad = call(
        router_kernel,
        struct((1, token_count), f32),
        (me,),
        [select, exchanged(scores, "expert")],
        "router",
        4,
        moved=300_000,
    )

    def early(name, at, pieces, sum_before):
        return call(
            functools.partial(early_kernel, steps=at, chips=chips),
            struct((kept, columns), f32),
            (position,),
            [turned] + pieces + sum_before,
            name,
            24,
            flops=4 * len(at) * rows * kept * columns,
            moved=8_000_000,
        )

    total = []
    for k in range(1, chips):
        halves = [onward(half) for half in halves]
        if k == 1:
            halves[0], compacted_tied, heads = tied(halves[0], compacted, heads)
        elif k == chips - 1:
            total = [early("early%d" % k, [k - 1], steps.pop(), total)]
            halves[0], total[0] = tied(halves[0], total[0])
        else:
            pieces = steps.pop()
            if k == 2:
                pieces = steps.pop() + pieces
            total = [early("early%d" % k, [0, 1] if k == 2 else [k - 1], pieces, total)]
            halves[0], halves[1], total[0], router_grad = tied(halves[0], halves[1], total[0], router_grad)
        steps.append(halves + [swapped(half) for half in halves])
    last = steps.pop()
    state = struct((bucket_rows, LANES), f32)
    flat_rows = even_size // LANES
    sum_rows = round_up(kept * lines + head_rows + 32, 8)
    edge = round_up(-(-head_rows // lines), 16)
    new_master, new_one, new_two, new_weight = pl.pallas_call(
        functools.partial(final_kernel, even_size=even_size, head_rows=head_rows, chips=chips),
        out_shape=[state, state, state, struct((per, columns), bf16)],
        in_specs=[smem()] * 2 + [vmem()] * 10,
        out_specs=[anywhere(), anywhere(), anywhere(), vmem()],
        scratch_shapes=[
            pltpu.VMEM((sum_rows, LANES), f32),
            pltpu.VMEM((sum_rows, LANES), f32),
            pltpu.VMEM((round_up(flat_rows + head_rows + 32, 8), LANES), f32),
            pltpu.VMEM((bucket_rows, LANES), f32),
            pltpu.VMEM((bucket_rows, LANES), f32),
            pltpu.VMEM((edge * lines + 2 * head_rows + 32, LANES), f32),
            pltpu.SemaphoreType.DMA((4, 3)),
        ],
        compiler_params=params(32),
        cost_estimate=cost(4 * rows * kept * columns, 25_000_000),
        name="final",
    )(
        position,
        offsets,
        turned,
        total[0],
        heads,
        *last,
        master.reshape(bucket_rows, LANES),
        moment_one.reshape(bucket_rows, LANES),
        moment_two.reshape(bucket_rows, LANES),
    )
    return (
        new_master.reshape(1, 1, bucket_cap),
        new_one.reshape(1, 1, bucket_cap),
        new_two.reshape(1, 1, bucket_cap),
        new_weight[None],
        router_grad.reshape(token_count, 1),
    )


def solution(mesh):
    placed = (
        P(("dp", "expert"), None),
        P(("dp", "expert"), None),
        P(("dp", "expert"), None, None),
        P(("dp", "expert"), None),
        P(("dp", "expert"), None),
        P("expert", "dp", None),
        P("expert", "dp", None),
        P("expert", "dp", None),
        P("expert", "dp", None),
        P(),
    )
    return jax.shard_map(
        shards,
        mesh=mesh,
        in_specs=placed,
        out_specs=(
            P("expert", "dp", None),
            P("expert", "dp", None),
            P("expert", "dp", None),
            P("expert", "dp", None),
            P(("dp", "expert"), None),
        ),
        check_vma=False,
    )
```

```python
import functools

import jax
import jax.numpy as jnp
from jax import lax
from jax.experimental import pallas as pl
from jax.experimental.pallas import tpu as pltpu
from jax.sharding import PartitionSpec as P

beta_one = 0.9
beta_two = 0.95
learn_rate = 0.001
decay_rate = 0.1
adam_eps = 1e-08
adam_step = 20.0

LANES = 128
CHUNK = 120

f32 = jnp.float32
bf16 = jnp.bfloat16
i32 = jnp.int32


def round_up(value, unit):
    return -(-value // unit) * unit


def iota(shape, axis):
    return lax.broadcasted_iota(i32, shape, axis)


def params(mib):
    return pltpu.CompilerParams(vmem_limit_bytes=mib * 1024 * 1024)


def cost(flops, moved):
    return pl.CostEstimate(flops=int(flops), bytes_accessed=int(moved), transcendentals=0)


def pack_kernel(me_ref, routes_ref, weight_ref, grads_ref, saved_ref, select_ref, target_ref, *packed_refs, cap):
    ids = routes_ref[...]
    experts = len(packed_refs)
    count = ids.shape[1]
    width = grads_ref.shape[1]
    hits = iota((round_up(experts, 8), count), 0) == ids
    before = (iota((count, count), 0) < iota((count, count), 1)).astype(bf16)
    earlier = jnp.dot(hits.astype(f32).astype(bf16), before, preferred_element_type=f32)
    slot = jnp.sum(jnp.where(hits, earlier, 0.0), axis=0, keepdims=True)
    target = (ids ^ me_ref[0]) * cap + slot.astype(i32)
    chosen = iota((experts * cap, count), 0) == target
    select = chosen.astype(f32).astype(bf16)
    select_ref[...] = chosen.astype(f32)
    target_ref[...] = target.astype(f32)
    grads = jnp.dot(select, grads_ref[...], preferred_element_type=f32).astype(bf16)
    saved = jnp.dot(select, saved_ref[...], preferred_element_type=f32).astype(bf16)
    weight = jnp.sum(jnp.where(chosen, weight_ref[...].astype(f32), 0.0), axis=1, keepdims=True)
    weight = jnp.broadcast_to(weight, (experts * cap, LANES)).astype(bf16)
    for k, packed_ref in enumerate(packed_refs):
        span = slice(k * cap, (k + 1) * cap)
        packed_ref[:, :width] = grads[span]
        packed_ref[:, width:-LANES] = saved[span]
        packed_ref[:, -LANES:] = weight[span]


def window_kernel(target_ref, tokens_ref, out_ref, *, per, lead):
    parts, count, width = out_ref.shape
    diagonal = iota((count, count), 0) == iota((count, count), 1)
    column = jnp.sum(jnp.where(diagonal, target_ref[...], 0.0), axis=1, keepdims=True)
    note = jnp.broadcast_to(column, (count, width)).astype(bf16)
    lane = iota((count, width), 1)
    for j in range(parts):
        start = per * j - lead
        if start < 0:
            blank = jnp.zeros((count, -start), bf16)
            piece = jnp.concatenate([blank, tokens_ref[:, : start + width]], axis=1)
        else:
            piece = tokens_ref[:, start : start + width]
        out_ref[j] = jnp.where(lane == 0, note, piece)


def compact_kernel(me_ref, windows_ref, out_ref):
    parts, count, width = windows_ref.shape
    experts, _, cap, _ = out_ref.shape
    diagonal = iota((count, count), 0) == iota((count, count), 1)
    slots = iota((experts * cap, count), 0)
    for i in range(parts):
        block = windows_ref[i]
        column = block[:, 0:1].astype(f32)
        target = jnp.sum(jnp.where(diagonal, column, 0.0), axis=0, keepdims=True).astype(i32)
        select = (slots == target).astype(f32).astype(bf16)
        rows = jnp.dot(select, block, preferred_element_type=f32).astype(bf16)
        for k in range(experts):
            out_ref[me_ref[0] ^ k, i] = rows[k * cap : (k + 1) * cap]


def turn_kernel(me_ref, rows_ref, out_ref):
    experts, parts, _, width = rows_ref.shape
    kept = out_ref.shape[1]
    for i in range(parts):
        slab = jnp.concatenate([rows_ref[me_ref[0] ^ k, i] for k in range(experts)], axis=0)
        out_ref[i] = slab.T[width - kept :, :]


def factor_kernel(*refs):
    arrived_refs, (grads_ref, gate_ref, up_ref, score_ref) = refs[:-4], refs[-4:]
    cap = arrived_refs[0].shape[0]
    width, hidden = grads_ref.shape[1], gate_ref.shape[1]
    for k, arrived_ref in enumerate(arrived_refs):
        span = slice(k * cap, (k + 1) * cap)
        grads_ref[span, :] = arrived_ref[:, :width]
        gate = arrived_ref[:, width : width + hidden].astype(f32)
        up = arrived_ref[:, width + hidden : width + 2 * hidden].astype(f32)
        weight = arrived_ref[:, width + 2 * hidden :].astype(f32)[:, 0:1]
        sig = jax.nn.sigmoid(gate)
        act = gate * sig
        score_ref[span, :] = act * up
        up_ref[span, :] = weight * act
        gate_ref[span, :] = weight * (up * sig * (1.0 + gate * (1.0 - sig)))


def row_kernel(position_ref, me_ref, grads_ref, gate_factor, up_factor, score_factor, *refs, chips, places):
    down_refs, (gate_ref, up_ref, joined_ref, scores_ref, down, sems) = refs[:-6], refs[-6:]
    hidden = down.shape[0]
    loads = []
    for n, down_ref in enumerate(down_refs):
        size = down_ref.shape[0]
        if size == hidden:
            at = 0
        else:
            k, other, half = places[n]
            slab = lax.rem(position_ref[0] + 2 * (chips - k), 2 * chips) ^ other
            at = pl.multiple_of(slab * (hidden // (2 * chips)) + half * size, 16)
        loads.append(pltpu.make_async_copy(down_ref, down.at[pl.ds(at, size)], sems.at[n]))
    for load in loads:
        load.start()
    for load in loads:
        load.wait()
    scores = None
    step = 2 * LANES
    for at in range(0, hidden, step):
        span = slice(at, at + step)
        back = lax.dot_general(
            grads_ref[...], down[span, :], (((1,), (1,)), ((), ())), preferred_element_type=f32
        )
        part = jnp.sum(score_factor[:, span] * back, axis=1, keepdims=True)
        scores = part if scores is None else scores + part
        gate = (gate_factor[:, span] * back).astype(bf16)
        up = (up_factor[:, span] * back).astype(bf16)
        gate_ref[:, span] = gate
        up_ref[:, span] = up
        joined_ref[:, span] = gate
        joined_ref[:, hidden + at : hidden + at + step] = up
    experts, cap, _ = scores_ref.shape
    for k in range(experts):
        scores_ref[me_ref[0] ^ k] = jnp.broadcast_to(scores[k * cap : (k + 1) * cap], (cap, LANES))


def router_kernel(me_ref, select_ref, scores_ref, out_ref):
    experts = scores_ref.shape[0]
    scores = jnp.concatenate([scores_ref[me_ref[0] ^ k] for k in range(experts)], axis=0)
    out_ref[...] = jnp.sum(jnp.where(select_ref[...] > 0.5, scores, 0.0), axis=0, keepdims=True)


def slab_sum(total, turned_ref, slabs, joined):
    for slab, (ref, at, step) in zip(slabs, joined):
        piece = jnp.dot(turned_ref[slab], ref[:, at : at + step], preferred_element_type=f32)
        piece = piece.astype(bf16).astype(f32)
        total = piece if total is None else total + piece
    return total


def slabs_of(position, steps, chips):
    own = [lax.rem(position + 2 * (chips - k), 2 * chips) for k in steps]
    return [slab ^ other for slab in own for other in (0, 1)]


def early_kernel(position_ref, turned_ref, *refs, steps, chips):
    refs, sum_ref = list(refs[:-1]), refs[-1]
    hidden = sum_ref.shape[1] // 2
    step = 2 * LANES
    slabs = slabs_of(position_ref[0], steps, chips)
    lists = ([], [])
    for k in steps:
        for other in range(2):
            whole = refs.pop(0) if k == 0 else None
            for half in range(2):
                lists[half].append((whole, half * hidden) if k == 0 else (refs.pop(0), 0))
    base = refs[0] if refs else None
    for half in range(2):
        for at in range(0, hidden, step):
            span = slice(half * hidden + at, half * hidden + at + step)
            joined = [(ref, first + at, step) for ref, first in lists[half]]
            total = None if base is None else base[:, span]
            sum_ref[:, span] = slab_sum(total, turned_ref, slabs, joined)


def adam(grad, old, first, second):
    first_new = beta_one * first + (1.0 - beta_one) * grad
    second_new = beta_two * second + (1.0 - beta_two) * grad * grad
    below = jnp.sqrt(second_new * (1.0 / (1.0 - beta_two**adam_step))) + adam_eps
    update = first_new * (learn_rate / (1.0 - beta_one**adam_step)) / below
    return old * (1.0 - learn_rate * decay_rate) - update, first_new, second_new


def final_kernel(
    position_ref,
    offsets_ref,
    turned_ref,
    early_ref,
    heads_ref,
    gate_own,
    up_own,
    gate_other,
    up_other,
    old,
    first,
    second,
    out_master,
    out_first,
    out_second,
    weight_ref,
    sums,
    moved,
    new_old,
    new_first,
    new_second,
    head_new,
    sems,
    *,
    even_size,
    head_rows,
    chips,
):
    kept, columns = early_ref.shape
    hidden = columns // 2
    per = weight_ref.shape[0]
    lines = columns // LANES
    before = (kept - per) * lines
    bucket_rows = old.shape[0]
    flat_rows = even_size // LANES
    position = position_ref[0]
    start = offsets_ref[position]
    finish = offsets_ref[position + 1]
    shift = position * even_size - start
    next_shift = (position + 1) * even_size - finish
    length = finish - start
    whole, part = shift // LANES, shift % LANES
    odd = whole % 8
    next_whole, next_part = next_shift // LANES, next_shift % LANES

    step = 2 * LANES
    slabs = slabs_of(position, [chips - 1], chips)
    for half, refs in enumerate(((gate_own, gate_other), (up_own, up_other))):
        for at in range(0, hidden, step):
            begin = half * hidden + at
            total = slab_sum(
                early_ref[:, begin : begin + step], turned_ref, slabs, [(ref, at, step) for ref in refs]
            )
            for c in range(step // LANES):
                block = total[:, c * LANES : (c + 1) * LANES]
                line = begin // LANES + c
                block = pltpu.roll(block, part, 1)
                sums[pl.ds(odd + line, kept, stride=lines), :] = block
                moved[pl.ds(odd + line + 1, kept, stride=lines), :] = block

    def slots_of(row, count):
        at = pl.multiple_of(row + before - (whole - odd), 8)
        lane = iota((count, LANES), 1)
        return jnp.where(lane >= part, sums[pl.ds(at, count), :], moved[pl.ds(at, count), :])

    def update(row, count):
        span = pl.ds(row, count)
        a, b, c = adam(slots_of(row, count), old[span, :], first[span, :], second[span, :])
        new_old[span, :], new_first[span, :], new_second[span, :] = a, b, c

    def masked(row, count):
        span = pl.ds(row, count)
        inside = (row + iota((count, LANES), 0)) * LANES + iota((count, LANES), 1) < length
        grad = jnp.where(inside, slots_of(row, count), 0.0)
        a, b, c = adam(grad, old[span, :], first[span, :], second[span, :])
        new_old[span, :] = jnp.where(inside, a, 0.0)
        new_first[span, :] = jnp.where(inside, b, 0.0)
        new_second[span, :] = jnp.where(inside, c, 0.0)

    def send(begin, count, slot):
        span = pl.ds(begin, count)
        stores = [
            pltpu.make_async_copy(source.at[span], target.at[span], sems.at[slot, n])
            for n, (source, target) in enumerate(
                ((new_old, out_master), (new_first, out_first), (new_second, out_second))
            )
        ]
        for store in stores:
            store.start()
        return stores

    def chunk(n, carry):
        update(pl.multiple_of(n * CHUNK, 8), CHUNK)
        return carry

    safe = (flat_rows - head_rows) // CHUNK
    third = -(-safe // 3)
    stores = []
    for slot, begin in enumerate(range(0, safe, third)):
        end = min(begin + third, safe)
        lax.fori_loop(begin, end, chunk, 0)
        stores += send(begin * CHUNK, (end - begin) * CHUNK, slot)
    for row in range(safe * CHUNK, bucket_rows, CHUNK):
        masked(row, min(CHUNK, bucket_rows - row))
    stores += send(safe * CHUNK, bucket_rows - safe * CHUNK, 3)

    def next_slots():
        lane = iota((head_rows, LANES), 1)
        base = flat_rows + before - next_whole + odd
        here = pltpu.roll(sums[pl.ds(base, head_rows), :], (LANES - part) % LANES, 1)
        above = pltpu.roll(sums[pl.ds(base - 1, head_rows), :], (LANES - part) % LANES, 1)
        return pltpu.roll(jnp.where(lane < LANES - next_part, here, above), next_part, 1)

    edge = round_up(-(-head_rows // lines), 16)
    head_new[pl.ds(edge * lines, head_rows), :] = adam(next_slots(), heads_ref[0], heads_ref[1], heads_ref[2])[0]

    flat_row = iota((edge, LANES), 0) + (per - edge)
    for c in range(lines):
        lane = iota((per, LANES), 1)
        here = new_old[pl.ds(c + whole, per, stride=lines), :]
        below = new_old[pl.ds(c + whole + 1, per, stride=lines), :]
        own = pltpu.roll(jnp.where(lane >= part, here, below), (LANES - part) % LANES, 1)
        base = c + next_whole
        lane = iota((edge, LANES), 1)
        here = head_new[pl.ds(base, edge, stride=lines), :]
        below = head_new[pl.ds(base + 1, edge, stride=lines), :]
        other = pltpu.roll(jnp.where(lane >= next_part, here, below), (LANES - next_part) % LANES, 1)
        flat = (flat_row * lines + c) * LANES + lane
        last = jnp.where(flat < even_size - next_shift, own[per - edge :], other)
        out = slice(c * LANES, (c + 1) * LANES)
        if per > edge:
            weight_ref[: per - edge, out] = own[: per - edge].astype(bf16)
        weight_ref[per - edge :, out] = last.astype(bf16)

    for store in stores:
        store.wait()


def vmem():
    return pl.BlockSpec(memory_space=pltpu.VMEM)


def anywhere():
    return pl.BlockSpec(memory_space=pl.ANY)


def hbm():
    return pl.BlockSpec(memory_space=pltpu.HBM)


def smem():
    return pl.BlockSpec(memory_space=pltpu.SMEM)


def call(kernel, outs, scalars, args, name, mib, flops=0, moved=0):
    many = isinstance(outs, (list, tuple))
    return pl.pallas_call(
        kernel,
        out_shape=outs,
        in_specs=[smem()] * len(scalars) + [vmem()] * len(args),
        out_specs=[vmem()] * len(outs) if many else vmem(),
        compiler_params=params(mib),
        cost_estimate=cost(flops, moved),
        name=name,
    )(*scalars, *args)


def struct(shape, kind):
    return jax.ShapeDtypeStruct(shape, kind)


def shards(
    tokens,
    out_grad,
    gate_up,
    route_weight,
    routes,
    down_weight,
    master,
    moment_one,
    moment_two,
    offsets,
):
    token_count, model_width = tokens.shape
    columns = gate_up.shape[2]
    hidden = columns // 2
    bucket_cap = master.shape[2]
    groups = lax.axis_size("expert")
    parts = lax.axis_size("dp")
    experts = groups * master.shape[0]
    cap = 2 * token_count // experts
    rows = experts * cap
    per = model_width // parts
    even_size = per * columns
    margin = bucket_cap - even_size
    extra = round_up(-(-margin // columns), 16)
    width = round_up(per + extra + 1, LANES)
    kept = per + extra
    lines = columns // LANES
    bucket_rows = bucket_cap // LANES
    head_rows = round_up(margin // LANES, 8)

    chips = parts // 2
    position = lax.axis_index("dp").astype(i32).reshape(1)
    me = lax.axis_index("expert").astype(i32).reshape(1)

    def onward(block):
        return lax.ppermute(block, "dp", [(i, (i + 2) % parts) for i in range(parts)])

    def swapped(block):
        return lax.ppermute(block, "dp", [(i, i ^ 1) for i in range(parts)])

    def exchanged(block, axis):
        return lax.all_to_all(block, axis, split_axis=0, concat_axis=0, tiled=True)

    def tied(*values):
        return lax.optimization_barrier(values)

    wide = model_width + columns + LANES
    select, target, *packed = call(
        functools.partial(pack_kernel, cap=cap),
        [struct((rows, token_count), f32), struct((1, token_count), f32)] + [struct((cap, wide), bf16)] * experts,
        (me,),
        (
            routes.reshape(1, token_count),
            route_weight.reshape(1, token_count),
            out_grad,
            gate_up.reshape(token_count, columns),
        ),
        "pack",
        16,
        moved=6_000_000,
    )
    arrived = packed[:1] + [
        lax.ppermute(packed[k], "expert", [(i, i ^ k) for i in range(experts)]) for k in range(1, experts)
    ]
    windows = call(
        functools.partial(window_kernel, per=per, lead=width - per),
        struct((parts, token_count, width), bf16),
        (),
        (target, tokens),
        "window",
        12,
        moved=2_000_000,
    )
    down_rows = down_weight.shape[1]
    if down_rows % 32 == 0:
        size = down_rows // 2
        held = [[down_weight[0, :size], down_weight[0, size:]]]
        for k in range(1, chips):
            if k == 2:
                held[-1][0], windows = tied(held[-1][0], windows, *packed)[:2]
            held.append([onward(block) for block in held[-1]])
        windows, held[-1][0] = tied(windows, held[-1][0])
        whole, held[:-1], arrived = tied(down_weight[0], held[:-1], arrived)
        down = [whole, swapped(whole)]
        places = [(0, 0, 0), (0, 1, 0)]
        for k in range(1, chips):
            down += held[k] + [swapped(block) for block in held[k]]
            places += [(k, 0, 0), (k, 0, 1), (k, 1, 0), (k, 1, 1)]
    else:
        down = [lax.all_gather(down_weight, "dp", axis=1, tiled=True)[0]]
        windows, down[0] = tied(windows, down[0])
        places = None
    windows = exchanged(windows, "dp")
    factors = call(
        factor_kernel,
        [struct((rows, model_width), bf16)] + [struct((rows, hidden), f32)] * 3,
        (),
        arrived,
        "factors",
        20,
        moved=6_000_000,
    )
    gate, up, joined, scores = pl.pallas_call(
        functools.partial(row_kernel, chips=chips, places=places),
        out_shape=[struct((rows, hidden), bf16)] * 2
        + [struct((rows, columns), bf16), struct((experts, cap, LANES), f32)],
        in_specs=[smem()] * 2 + [vmem()] * 4 + [hbm()] * len(down),
        out_specs=[vmem()] * 4,
        scratch_shapes=[
            pltpu.VMEM((hidden, model_width), bf16),
            pltpu.SemaphoreType.DMA((len(down),)),
        ],
        compiler_params=params(24),
        cost_estimate=cost(2 * rows * model_width * hidden, 8_000_000),
        name="rows",
    )(position, me, *factors, *down)

    halves = [gate, up]
    steps = [[joined, swapped(joined)]]
    compacted = call(
        compact_kernel,
        struct((experts, parts, cap, width), bf16),
        (me,),
        (windows,),
        "compact",
        12,
        moved=3_000_000,
    )
    heads = jnp.concatenate([master, moment_one, moment_two], axis=0)[:, 0, : head_rows * LANES]
    first_step = [onward(half) for half in halves]
    first_step[0], heads, scores = tied(first_step[0], heads, scores)
    heads = lax.ppermute(heads, "dp", [(i + 1, i) for i in range(parts - 1)])
    heads = heads.reshape(3, head_rows, LANES)
    turned = call(
        turn_kernel,
        struct((parts, kept, rows), bf16),
        (me,),
        (exchanged(compacted, "expert"),),
        "turn",
        12,
        moved=3_000_000,
    )
    router_grad = call(
        router_kernel,
        struct((1, token_count), f32),
        (me,),
        [select, exchanged(scores, "expert")],
        "router",
        4,
        moved=300_000,
    )

    def early(name, at, pieces, sum_before):
        return call(
            functools.partial(early_kernel, steps=at, chips=chips),
            struct((kept, columns), f32),
            (position,),
            [turned] + pieces + sum_before,
            name,
            24,
            flops=4 * len(at) * rows * kept * columns,
            moved=8_000_000,
        )

    total = []
    for k in range(1, chips):
        halves = [onward(half) for half in halves] if k > 1 else first_step
        if k == 1:
            halves[0], compacted = tied(halves[0], compacted)
        elif k == 2:
            halves[1], turned = tied(halves[1], turned)
        else:
            pieces = steps.pop()
            if k == 3:
                first = early("early1", [0, 1], steps.pop(0) + steps.pop(0), [])
                halves[0], first, router_grad, heads = tied(halves[0], first, router_grad, heads)
                total = [first]
            total = [early("early%d" % (k - 1), [k - 1], pieces, total)]
            halves[1], total[0] = tied(halves[1], total[0])
        steps.append(halves + [swapped(half) for half in halves])
    last = steps.pop()
    state = struct((bucket_rows, LANES), f32)
    flat_rows = even_size // LANES
    sum_rows = round_up(kept * lines + head_rows + 32, 8)
    edge = round_up(-(-head_rows // lines), 16)
    new_master, new_one, new_two, new_weight = pl.pallas_call(
        functools.partial(final_kernel, even_size=even_size, head_rows=head_rows, chips=chips),
        out_shape=[state, state, state, struct((per, columns), bf16)],
        in_specs=[smem()] * 2 + [vmem()] * 10,
        out_specs=[anywhere(), anywhere(), anywhere(), vmem()],
        scratch_shapes=[
            pltpu.VMEM((sum_rows, LANES), f32),
            pltpu.VMEM((sum_rows, LANES), f32),
            pltpu.VMEM((round_up(flat_rows + head_rows + 32, 8), LANES), f32),
            pltpu.VMEM((bucket_rows, LANES), f32),
            pltpu.VMEM((bucket_rows, LANES), f32),
            pltpu.VMEM((edge * lines + 2 * head_rows + 32, LANES), f32),
            pltpu.SemaphoreType.DMA((4, 3)),
        ],
        compiler_params=params(32),
        cost_estimate=cost(4 * rows * kept * columns, 25_000_000),
        name="final",
    )(
        position,
        offsets,
        turned,
        total[0],
        heads,
        *last,
        master.reshape(bucket_rows, LANES),
        moment_one.reshape(bucket_rows, LANES),
        moment_two.reshape(bucket_rows, LANES),
    )
    return (
        new_master.reshape(1, 1, bucket_cap),
        new_one.reshape(1, 1, bucket_cap),
        new_two.reshape(1, 1, bucket_cap),
        new_weight[None],
        router_grad.reshape(token_count, 1),
    )


def solution(mesh):
    placed = (
        P(("dp", "expert"), None),
        P(("dp", "expert"), None),
        P(("dp", "expert"), None, None),
        P(("dp", "expert"), None),
        P(("dp", "expert"), None),
        P("expert", "dp", None),
        P("expert", "dp", None),
        P("expert", "dp", None),
        P("expert", "dp", None),
        P(),
    )
    return jax.shard_map(
        shards,
        mesh=mesh,
        in_specs=placed,
        out_specs=(
            P("expert", "dp", None),
            P("expert", "dp", None),
            P("expert", "dp", None),
            P("expert", "dp", None),
            P(("dp", "expert"), None),
        ),
        check_vma=False,
    )
```

```python
import functools

import jax
import jax.numpy as jnp
from jax import lax
from jax.experimental import pallas as pl
from jax.experimental.pallas import tpu as pltpu
from jax.sharding import PartitionSpec as P

beta_one = 0.9
beta_two = 0.95
learn_rate = 0.001
decay_rate = 0.1
adam_eps = 1e-08
adam_step = 20.0

LANES = 128
CHUNK = 120

f32 = jnp.float32
bf16 = jnp.bfloat16
i32 = jnp.int32


def round_up(value, unit):
    return -(-value // unit) * unit


def iota(shape, axis):
    return lax.broadcasted_iota(i32, shape, axis)


def params(mib):
    return pltpu.CompilerParams(vmem_limit_bytes=mib * 1024 * 1024)


def cost(flops, moved):
    return pl.CostEstimate(flops=int(flops), bytes_accessed=int(moved), transcendentals=0)


def pack_kernel(routes_ref, weight_ref, grads_ref, saved_ref, select_ref, target_ref, packed_ref):
    ids = routes_ref[...]
    experts, cap, _ = packed_ref.shape
    count = ids.shape[1]
    width = grads_ref.shape[1]
    hits = iota((round_up(experts, 8), count), 0) == ids
    before = (iota((count, count), 0) < iota((count, count), 1)).astype(bf16)
    earlier = jnp.dot(hits.astype(f32).astype(bf16), before, preferred_element_type=f32)
    slot = jnp.sum(jnp.where(hits, earlier, 0.0), axis=0, keepdims=True)
    target = ids * cap + slot.astype(i32)
    chosen = iota((experts * cap, count), 0) == target
    select = chosen.astype(f32).astype(bf16)
    select_ref[...] = chosen.astype(f32)
    target_ref[...] = target.astype(f32)
    grads = jnp.dot(select, grads_ref[...], preferred_element_type=f32).astype(bf16)
    saved = jnp.dot(select, saved_ref[...], preferred_element_type=f32).astype(bf16)
    weight = jnp.sum(jnp.where(chosen, weight_ref[...].astype(f32), 0.0), axis=1, keepdims=True)
    weight = jnp.broadcast_to(weight, (experts * cap, LANES)).astype(bf16)
    for k in range(experts):
        span = slice(k * cap, (k + 1) * cap)
        packed_ref[k, :, :width] = grads[span]
        packed_ref[k, :, width:-LANES] = saved[span]
        packed_ref[k, :, -LANES:] = weight[span]


def window_kernel(target_ref, tokens_ref, out_ref, *, per, lead):
    parts, count, width = out_ref.shape
    diagonal = iota((count, count), 0) == iota((count, count), 1)
    column = jnp.sum(jnp.where(diagonal, target_ref[...], 0.0), axis=1, keepdims=True)
    note = jnp.broadcast_to(column, (count, width)).astype(bf16)
    lane = iota((count, width), 1)
    for j in range(parts):
        start = per * j - lead
        if start < 0:
            blank = jnp.zeros((count, -start), bf16)
            piece = jnp.concatenate([blank, tokens_ref[:, : start + width]], axis=1)
        else:
            piece = tokens_ref[:, start : start + width]
        out_ref[j] = jnp.where(lane == 0, note, piece)


def compact_kernel(position_ref, windows_ref, scores_ref, out_ref):
    parts, count, width = windows_ref.shape
    experts, _, cap, _ = out_ref.shape
    diagonal = iota((count, count), 0) == iota((count, count), 1)
    slots = iota((experts * cap, count), 0)
    for i in range(parts):
        block = windows_ref[i]
        column = block[:, 0:1].astype(f32)
        target = jnp.sum(jnp.where(diagonal, column, 0.0), axis=0, keepdims=True).astype(i32)
        select = (slots == target).astype(f32).astype(bf16)
        rows = jnp.dot(select, block, preferred_element_type=f32).astype(bf16)
        for k in range(experts):
            out_ref[k, i] = rows[k * cap : (k + 1) * cap]
    lane = iota((cap, LANES), 1)
    for k in range(experts):
        rest = scores_ref[k * cap : (k + 1) * cap, :]
        first = out_ref[k, position_ref[0], :, :LANES]
        for c in range(3):
            part = rest.astype(bf16)
            rest = rest - part.astype(f32)
            first = jnp.where(lane == 1 + c, part, first)
        out_ref[k, position_ref[0], :, :LANES] = first


def turn_kernel(rows_ref, out_ref):
    experts, parts, _, width = rows_ref.shape
    kept = out_ref.shape[1]
    for i in range(parts):
        slab = jnp.concatenate([rows_ref[k, i] for k in range(experts)], axis=0)
        out_ref[i] = slab.T[width - kept :, :]


def factor_kernel(arrived_ref, grads_ref, gate_ref, up_ref, score_ref):
    width, hidden = grads_ref.shape[1], gate_ref.shape[1]
    grads_ref[...] = arrived_ref[:, :width]
    gate = arrived_ref[:, width : width + hidden].astype(f32)
    up = arrived_ref[:, width + hidden : width + 2 * hidden].astype(f32)
    weight = arrived_ref[:, width + 2 * hidden :].astype(f32)[:, 0:1]
    sig = jax.nn.sigmoid(gate)
    act = gate * sig
    score_ref[...] = act * up
    up_ref[...] = weight * act
    gate_ref[...] = weight * (up * sig * (1.0 + gate * (1.0 - sig)))


def row_kernel(position_ref, grads_ref, gate_factor, up_factor, score_factor, *refs, chips):
    down_refs, (gate_ref, up_ref, joined_ref, scores_ref, down, sems) = refs[:-6], refs[-6:]
    hidden = down.shape[0]
    loads = []
    for n, down_ref in enumerate(down_refs):
        size = down_ref.shape[0]
        if size == hidden:
            at = 0
        else:
            slab = lax.rem(position_ref[0] + 2 * (chips - n // 2), 2 * chips) ^ (n % 2)
            at = pl.multiple_of(slab * size, 16)
        loads.append(pltpu.make_async_copy(down_ref, down.at[pl.ds(at, size)], sems.at[n]))
    for load in loads:
        load.start()
    for load in loads:
        load.wait()
    scores = None
    step = 2 * LANES
    for at in range(0, hidden, step):
        span = slice(at, at + step)
        back = lax.dot_general(
            grads_ref[...], down[span, :], (((1,), (1,)), ((), ())), preferred_element_type=f32
        )
        part = jnp.sum(score_factor[:, span] * back, axis=1, keepdims=True)
        scores = part if scores is None else scores + part
        gate = (gate_factor[:, span] * back).astype(bf16)
        up = (up_factor[:, span] * back).astype(bf16)
        gate_ref[:, span] = gate
        up_ref[:, span] = up
        joined_ref[:, span] = gate
        joined_ref[:, hidden + at : hidden + at + step] = up
    scores_ref[...] = jnp.broadcast_to(scores, scores_ref.shape)


def router_kernel(position_ref, select_ref, rows_ref, out_ref):
    experts = rows_ref.shape[0]
    own = [rows_ref[k, position_ref[0], :, :LANES] for k in range(experts)]
    parts = jnp.concatenate(own, axis=0).astype(f32)
    scores = (parts[:, 1:2] + parts[:, 2:3]) + parts[:, 3:4]
    out_ref[...] = jnp.sum(jnp.where(select_ref[...] > 0.5, scores, 0.0), axis=0, keepdims=True)


def head_kernel(master_any, first_any, second_any, out_ref, sems):
    count = out_ref.shape[1]
    copies = [
        pltpu.make_async_copy(source.at[pl.ds(0, count)], out_ref.at[n], sems.at[n])
        for n, source in enumerate((master_any, first_any, second_any))
    ]
    for copy in copies:
        copy.start()
    for copy in copies:
        copy.wait()


def slab_sum(total, turned_ref, slabs, joined):
    for slab, (ref, at, step) in zip(slabs, joined):
        piece = jnp.dot(turned_ref[slab], ref[:, at : at + step], preferred_element_type=f32)
        piece = piece.astype(bf16).astype(f32)
        total = piece if total is None else total + piece
    return total


def slabs_of(position, steps, chips):
    own = [lax.rem(position + 2 * (chips - k), 2 * chips) for k in steps]
    return [slab ^ other for slab in own for other in (0, 1)]


def early_kernel(position_ref, turned_ref, *refs, steps, chips):
    refs, sum_ref = list(refs[:-1]), refs[-1]
    hidden = sum_ref.shape[1] // 2
    step = 2 * LANES
    slabs = slabs_of(position_ref[0], steps, chips)
    lists = ([], [])
    for k in steps:
        for other in range(2):
            whole = refs.pop(0) if k == 0 else None
            for half in range(2):
                lists[half].append((whole, half * hidden) if k == 0 else (refs.pop(0), 0))
    base = refs[0] if refs else None
    for half in range(2):
        for at in range(0, hidden, step):
            span = slice(half * hidden + at, half * hidden + at + step)
            joined = [(ref, first + at, step) for ref, first in lists[half]]
            total = None if base is None else base[:, span]
            sum_ref[:, span] = slab_sum(total, turned_ref, slabs, joined)


def adam(grad, old, first, second):
    first_new = beta_one * first + (1.0 - beta_one) * grad
    second_new = beta_two * second + (1.0 - beta_two) * grad * grad
    below = jnp.sqrt(second_new * (1.0 / (1.0 - beta_two**adam_step))) + adam_eps
    update = first_new * (learn_rate / (1.0 - beta_one**adam_step)) / below
    return old * (1.0 - learn_rate * decay_rate) - update, first_new, second_new


def final_kernel(
    position_ref,
    offsets_ref,
    turned_ref,
    early_ref,
    heads_ref,
    gate_own,
    up_own,
    gate_other,
    up_other,
    old,
    first,
    second,
    out_master,
    out_first,
    out_second,
    weight_ref,
    sums,
    moved,
    new_old,
    new_first,
    new_second,
    head_new,
    sems,
    *,
    even_size,
    head_rows,
    chips,
):
    kept, columns = early_ref.shape
    hidden = columns // 2
    per = weight_ref.shape[0]
    lines = columns // LANES
    before = (kept - per) * lines
    bucket_rows = old.shape[0]
    flat_rows = even_size // LANES
    position = position_ref[0]
    start = offsets_ref[position]
    finish = offsets_ref[position + 1]
    shift = position * even_size - start
    next_shift = (position + 1) * even_size - finish
    length = finish - start
    whole, part = shift // LANES, shift % LANES
    odd = whole % 8
    next_whole, next_part = next_shift // LANES, next_shift % LANES

    step = 2 * LANES
    slabs = slabs_of(position, [chips - 1], chips)
    for half, refs in enumerate(((gate_own, gate_other), (up_own, up_other))):
        for at in range(0, hidden, step):
            begin = half * hidden + at
            total = slab_sum(
                early_ref[:, begin : begin + step], turned_ref, slabs, [(ref, at, step) for ref in refs]
            )
            for c in range(step // LANES):
                block = total[:, c * LANES : (c + 1) * LANES]
                line = begin // LANES + c
                block = pltpu.roll(block, part, 1)
                sums[pl.ds(odd + line, kept, stride=lines), :] = block
                moved[pl.ds(odd + line + 1, kept, stride=lines), :] = block

    def slots_of(row, count):
        at = pl.multiple_of(row + before - (whole - odd), 8)
        lane = iota((count, LANES), 1)
        return jnp.where(lane >= part, sums[pl.ds(at, count), :], moved[pl.ds(at, count), :])

    def update(row, count):
        span = pl.ds(row, count)
        a, b, c = adam(slots_of(row, count), old[span, :], first[span, :], second[span, :])
        new_old[span, :], new_first[span, :], new_second[span, :] = a, b, c

    def masked(row, count):
        span = pl.ds(row, count)
        inside = (row + iota((count, LANES), 0)) * LANES + iota((count, LANES), 1) < length
        grad = jnp.where(inside, slots_of(row, count), 0.0)
        a, b, c = adam(grad, old[span, :], first[span, :], second[span, :])
        new_old[span, :] = jnp.where(inside, a, 0.0)
        new_first[span, :] = jnp.where(inside, b, 0.0)
        new_second[span, :] = jnp.where(inside, c, 0.0)

    def send(begin, count, slot):
        span = pl.ds(begin, count)
        stores = [
            pltpu.make_async_copy(source.at[span], target.at[span], sems.at[slot, n])
            for n, (source, target) in enumerate(
                ((new_old, out_master), (new_first, out_first), (new_second, out_second))
            )
        ]
        for store in stores:
            store.start()
        return stores

    def chunk(n, carry):
        update(pl.multiple_of(n * CHUNK, 8), CHUNK)
        return carry

    safe = (flat_rows - head_rows) // CHUNK
    third = -(-safe // 3)
    stores = []
    for slot, begin in enumerate(range(0, safe, third)):
        end = min(begin + third, safe)
        lax.fori_loop(begin, end, chunk, 0)
        stores += send(begin * CHUNK, (end - begin) * CHUNK, slot)
    for row in range(safe * CHUNK, bucket_rows, CHUNK):
        masked(row, min(CHUNK, bucket_rows - row))
    stores += send(safe * CHUNK, bucket_rows - safe * CHUNK, 3)

    def next_slots():
        lane = iota((head_rows, LANES), 1)
        base = flat_rows + before - next_whole + odd
        here = pltpu.roll(sums[pl.ds(base, head_rows), :], (LANES - part) % LANES, 1)
        above = pltpu.roll(sums[pl.ds(base - 1, head_rows), :], (LANES - part) % LANES, 1)
        return pltpu.roll(jnp.where(lane < LANES - next_part, here, above), next_part, 1)

    edge = round_up(-(-head_rows // lines), 16)
    head_new[pl.ds(edge * lines, head_rows), :] = adam(next_slots(), heads_ref[0], heads_ref[1], heads_ref[2])[0]

    flat_row = iota((edge, LANES), 0) + (per - edge)
    for c in range(lines):
        lane = iota((per, LANES), 1)
        here = new_old[pl.ds(c + whole, per, stride=lines), :]
        below = new_old[pl.ds(c + whole + 1, per, stride=lines), :]
        own = pltpu.roll(jnp.where(lane >= part, here, below), (LANES - part) % LANES, 1)
        base = c + next_whole
        lane = iota((edge, LANES), 1)
        here = head_new[pl.ds(base, edge, stride=lines), :]
        below = head_new[pl.ds(base + 1, edge, stride=lines), :]
        other = pltpu.roll(jnp.where(lane >= next_part, here, below), (LANES - next_part) % LANES, 1)
        flat = (flat_row * lines + c) * LANES + lane
        last = jnp.where(flat < even_size - next_shift, own[per - edge :], other)
        out = slice(c * LANES, (c + 1) * LANES)
        if per > edge:
            weight_ref[: per - edge, out] = own[: per - edge].astype(bf16)
        weight_ref[per - edge :, out] = last.astype(bf16)

    for store in stores:
        store.wait()


def vmem():
    return pl.BlockSpec(memory_space=pltpu.VMEM)


def anywhere():
    return pl.BlockSpec(memory_space=pl.ANY)


def hbm():
    return pl.BlockSpec(memory_space=pltpu.HBM)


def smem():
    return pl.BlockSpec(memory_space=pltpu.SMEM)


def call(kernel, outs, scalars, args, name, mib, flops=0, moved=0):
    many = isinstance(outs, (list, tuple))
    return pl.pallas_call(
        kernel,
        out_shape=outs,
        in_specs=[smem()] * len(scalars) + [vmem()] * len(args),
        out_specs=[vmem()] * len(outs) if many else vmem(),
        compiler_params=params(mib),
        cost_estimate=cost(flops, moved),
        name=name,
    )(*scalars, *args)


def struct(shape, kind):
    return jax.ShapeDtypeStruct(shape, kind)


def shards(
    tokens,
    out_grad,
    gate_up,
    route_weight,
    routes,
    down_weight,
    master,
    moment_one,
    moment_two,
    offsets,
):
    token_count, model_width = tokens.shape
    columns = gate_up.shape[2]
    hidden = columns // 2
    bucket_cap = master.shape[2]
    groups = lax.axis_size("expert")
    parts = lax.axis_size("dp")
    experts = groups * master.shape[0]
    cap = 2 * token_count // experts
    rows = experts * cap
    per = model_width // parts
    even_size = per * columns
    margin = bucket_cap - even_size
    extra = round_up(-(-margin // columns), 16)
    width = round_up(per + extra + 4, LANES)
    kept = per + extra
    lines = columns // LANES
    bucket_rows = bucket_cap // LANES
    head_rows = round_up(margin // LANES, 8)

    chips = parts // 2
    position = lax.axis_index("dp").astype(i32).reshape(1)
    state = struct((bucket_rows, LANES), f32)
    old, first, second = (array.reshape(bucket_rows, LANES) for array in (master, moment_one, moment_two))

    def onward(block):
        return lax.ppermute(block, "dp", [(i, (i + 2) % parts) for i in range(parts)])

    def swapped(block):
        return lax.ppermute(block, "dp", [(i, i ^ 1) for i in range(parts)])

    def exchanged(block, axis):
        return lax.all_to_all(block, axis, split_axis=0, concat_axis=0, tiled=True)

    def tied(*values):
        return lax.optimization_barrier(values)

    wide = model_width + columns + LANES
    select, target, packed = call(
        pack_kernel,
        [
            struct((rows, token_count), f32),
            struct((1, token_count), f32),
            struct((experts, cap, wide), bf16),
        ],
        (),
        (
            routes.reshape(1, token_count),
            route_weight.reshape(1, token_count),
            out_grad,
            gate_up.reshape(token_count, columns),
        ),
        "pack",
        16,
        moved=6_000_000,
    )
    arrived = exchanged(packed, "expert").reshape(rows, wide)
    windows = call(
        functools.partial(window_kernel, per=per, lead=width - per),
        struct((parts, token_count, width), bf16),
        (),
        (target, tokens),
        "window",
        12,
        moved=2_000_000,
    )
    heads = pl.pallas_call(
        head_kernel,
        out_shape=struct((3, head_rows, LANES), f32),
        in_specs=[hbm()] * 3,
        out_specs=vmem(),
        scratch_shapes=[pltpu.SemaphoreType.DMA((3,))],
        compiler_params=params(4),
        cost_estimate=cost(0, 400_000),
        name="heads",
    )(old, first, second)
    if down_weight.shape[1] % 16 == 0:
        held = [down_weight[0]]
        for k in range(1, chips):
            block = held[-1]
            if k == 2:
                block, windows, heads, _ = tied(block, windows, heads, packed)
                heads = lax.ppermute(heads, "dp", [(i + 1, i) for i in range(parts - 1)])
            held.append(onward(block))
        windows, held[-1] = tied(windows, held[-1])
        down = [piece for block in held for piece in (block, swapped(block))]
    else:
        heads = lax.ppermute(heads, "dp", [(i + 1, i) for i in range(parts - 1)])
        down = [lax.all_gather(down_weight, "dp", axis=1, tiled=True)[0]]
        windows, down[0] = tied(windows, down[0])
    windows = exchanged(windows, "dp")
    arrived, heads = tied(arrived, heads)
    factors = call(
        factor_kernel,
        [struct((rows, model_width), bf16)] + [struct((rows, hidden), f32)] * 3,
        (),
        (arrived,),
        "factors",
        20,
        moved=6_000_000,
    )
    gate, up, joined, scores = pl.pallas_call(
        functools.partial(row_kernel, chips=chips),
        out_shape=[struct((rows, hidden), bf16)] * 2
        + [struct((rows, columns), bf16), struct((rows, LANES), f32)],
        in_specs=[smem()] + [vmem()] * 4 + [anywhere()] * len(down),
        out_specs=[vmem()] * 4,
        scratch_shapes=[
            pltpu.VMEM((hidden, model_width), bf16),
            pltpu.SemaphoreType.DMA((len(down),)),
        ],
        compiler_params=params(24),
        cost_estimate=cost(2 * rows * model_width * hidden, 8_000_000),
        name="rows",
    )(position, *factors, *down)

    halves = [gate, up]
    steps = [[joined, swapped(joined)]]
    compacted = call(
        compact_kernel,
        struct((experts, parts, cap, width), bf16),
        (position,),
        (windows, scores),
        "compact",
        12,
        moved=3_000_000,
    )
    compacted_rows = exchanged(compacted, "expert")
    turned = call(
        turn_kernel,
        struct((parts, kept, rows), bf16),
        (),
        (compacted_rows,),
        "turn",
        12,
        moved=3_000_000,
    )
    router_grad = call(
        router_kernel,
        struct((1, token_count), f32),
        (position,),
        (select, compacted_rows),
        "router",
        4,
        moved=300_000,
    )

    def early(name, at, pieces, sum_before):
        return call(
            functools.partial(early_kernel, steps=at, chips=chips),
            struct((kept, columns), f32),
            (position,),
            [turned] + pieces + sum_before,
            name,
            24,
            flops=4 * len(at) * rows * kept * columns,
            moved=8_000_000,
        )

    total = []
    for k in range(1, chips):
        halves = [onward(half) for half in halves]
        if k == 1:
            halves[0], compacted = tied(halves[0], compacted)
        elif k > 2:
            pieces = steps.pop()
            if k == 3:
                begun = early("early1", [0, 1], steps.pop(0) + steps.pop(0), [])
                halves[0], begun, router_grad = tied(halves[0], begun, router_grad)
                total = [begun]
            total = [early("early%d" % (k - 1), [k - 1], pieces, total)]
            halves[1], total[0] = tied(halves[1], total[0])
        steps.append(halves + [swapped(half) for half in halves])
    last = steps.pop()
    flat_rows = even_size // LANES
    sum_rows = round_up(kept * lines + head_rows + 32, 8)
    edge = round_up(-(-head_rows // lines), 16)
    new_master, new_one, new_two, new_weight = pl.pallas_call(
        functools.partial(final_kernel, even_size=even_size, head_rows=head_rows, chips=chips),
        out_shape=[state, state, state, struct((per, columns), bf16)],
        in_specs=[smem()] * 2 + [vmem()] * 10,
        out_specs=[anywhere(), anywhere(), anywhere(), vmem()],
        scratch_shapes=[
            pltpu.VMEM((sum_rows, LANES), f32),
            pltpu.VMEM((sum_rows, LANES), f32),
            pltpu.VMEM((round_up(flat_rows + head_rows + 32, 8), LANES), f32),
            pltpu.VMEM((bucket_rows, LANES), f32),
            pltpu.VMEM((bucket_rows, LANES), f32),
            pltpu.VMEM((edge * lines + 2 * head_rows + 32, LANES), f32),
            pltpu.SemaphoreType.DMA((4, 3)),
        ],
        compiler_params=params(32),
        cost_estimate=cost(4 * rows * kept * columns, 25_000_000),
        name="final",
    )(
        position,
        offsets,
        turned,
        total[0],
        heads,
        *last,
        old,
        first,
        second,
    )
    return (
        new_master.reshape(1, 1, bucket_cap),
        new_one.reshape(1, 1, bucket_cap),
        new_two.reshape(1, 1, bucket_cap),
        new_weight[None],
        router_grad.reshape(token_count, 1),
    )


def solution(mesh):
    placed = (
        P(("dp", "expert"), None),
        P(("dp", "expert"), None),
        P(("dp", "expert"), None, None),
        P(("dp", "expert"), None),
        P(("dp", "expert"), None),
        P("expert", "dp", None),
        P("expert", "dp", None),
        P("expert", "dp", None),
        P("expert", "dp", None),
        P(),
    )
    return jax.shard_map(
        shards,
        mesh=mesh,
        in_specs=placed,
        out_specs=(
            P("expert", "dp", None),
            P("expert", "dp", None),
            P("expert", "dp", None),
            P("expert", "dp", None),
            P(("dp", "expert"), None),
        ),
        check_vma=False,
    )
```

```python
import functools

import jax
import jax.numpy as jnp
from jax import lax
from jax.experimental import pallas as pl
from jax.experimental.pallas import tpu as pltpu
from jax.sharding import PartitionSpec as P

beta_one = 0.9
beta_two = 0.95
learn_rate = 0.001
decay_rate = 0.1
adam_eps = 1e-08
adam_step = 20.0

LANES = 128
CHUNK = 120

f32 = jnp.float32
bf16 = jnp.bfloat16
i32 = jnp.int32


def round_up(value, unit):
    return -(-value // unit) * unit


def iota(shape, axis):
    return lax.broadcasted_iota(i32, shape, axis)


def params(mib):
    return pltpu.CompilerParams(vmem_limit_bytes=mib * 1024 * 1024)


def cost(flops, moved):
    return pl.CostEstimate(flops=int(flops), bytes_accessed=int(moved), transcendentals=0)


def pack_kernel(routes_ref, weight_ref, grads_ref, saved_ref, select_ref, target_ref, packed_ref):
    ids = routes_ref[...]
    experts, cap, _ = packed_ref.shape
    count = ids.shape[1]
    width = grads_ref.shape[1]
    hits = iota((round_up(experts, 8), count), 0) == ids
    before = (iota((count, count), 0) < iota((count, count), 1)).astype(bf16)
    earlier = jnp.dot(hits.astype(f32).astype(bf16), before, preferred_element_type=f32)
    slot = jnp.sum(jnp.where(hits, earlier, 0.0), axis=0, keepdims=True)
    target = ids * cap + slot.astype(i32)
    chosen = iota((experts * cap, count), 0) == target
    select = chosen.astype(f32).astype(bf16)
    select_ref[...] = chosen.astype(f32)
    target_ref[...] = target.astype(f32)
    grads = jnp.dot(select, grads_ref[...], preferred_element_type=f32).astype(bf16)
    saved = jnp.dot(select, saved_ref[...], preferred_element_type=f32).astype(bf16)
    weight = jnp.sum(jnp.where(chosen, weight_ref[...].astype(f32), 0.0), axis=1, keepdims=True)
    weight = jnp.broadcast_to(weight, (experts * cap, LANES)).astype(bf16)
    for k in range(experts):
        span = slice(k * cap, (k + 1) * cap)
        packed_ref[k, :, :width] = grads[span]
        packed_ref[k, :, width:-LANES] = saved[span]
        packed_ref[k, :, -LANES:] = weight[span]


def window_kernel(target_ref, tokens_ref, out_ref, *, per, lead):
    parts, count, width = out_ref.shape
    diagonal = iota((count, count), 0) == iota((count, count), 1)
    column = jnp.sum(jnp.where(diagonal, target_ref[...], 0.0), axis=1, keepdims=True)
    note = jnp.broadcast_to(column, (count, width)).astype(bf16)
    lane = iota((count, width), 1)
    for j in range(parts):
        start = per * j - lead
        if start < 0:
            blank = jnp.zeros((count, -start), bf16)
            piece = jnp.concatenate([blank, tokens_ref[:, : start + width]], axis=1)
        else:
            piece = tokens_ref[:, start : start + width]
        out_ref[j] = jnp.where(lane == 0, note, piece)


def compact_kernel(position_ref, windows_ref, scores_ref, out_ref):
    parts, count, width = windows_ref.shape
    experts, _, cap, _ = out_ref.shape
    diagonal = iota((count, count), 0) == iota((count, count), 1)
    slots = iota((experts * cap, count), 0)
    for i in range(parts):
        block = windows_ref[i]
        column = block[:, 0:1].astype(f32)
        target = jnp.sum(jnp.where(diagonal, column, 0.0), axis=0, keepdims=True).astype(i32)
        select = (slots == target).astype(f32).astype(bf16)
        rows = jnp.dot(select, block, preferred_element_type=f32).astype(bf16)
        for k in range(experts):
            out_ref[k, i] = rows[k * cap : (k + 1) * cap]
    lane = iota((cap, LANES), 1)
    for k in range(experts):
        rest = scores_ref[k * cap : (k + 1) * cap, :]
        first = out_ref[k, position_ref[0], :, :LANES]
        for c in range(3):
            part = rest.astype(bf16)
            rest = rest - part.astype(f32)
            first = jnp.where(lane == 1 + c, part, first)
        out_ref[k, position_ref[0], :, :LANES] = first


def turn_kernel(rows_ref, out_ref):
    experts, parts, _, width = rows_ref.shape
    kept = out_ref.shape[1]
    for i in range(parts):
        slab = jnp.concatenate([rows_ref[k, i] for k in range(experts)], axis=0)
        out_ref[i] = slab.T[width - kept :, :]


def factor_kernel(arrived_ref, grads_ref, gate_ref, up_ref, score_ref):
    width, hidden = grads_ref.shape[1], gate_ref.shape[1]
    grads_ref[...] = arrived_ref[:, :width]
    gate = arrived_ref[:, width : width + hidden].astype(f32)
    up = arrived_ref[:, width + hidden : width + 2 * hidden].astype(f32)
    weight = arrived_ref[:, width + 2 * hidden :].astype(f32)[:, 0:1]
    sig = jax.nn.sigmoid(gate)
    act = gate * sig
    score_ref[...] = act * up
    up_ref[...] = weight * act
    gate_ref[...] = weight * (up * sig * (1.0 + gate * (1.0 - sig)))


def row_kernel(position_ref, grads_ref, gate_factor, up_factor, score_factor, *refs, chips):
    down_refs, (gate_ref, up_ref, joined_ref, scores_ref, down, sems) = refs[:-6], refs[-6:]
    hidden = down.shape[0]
    loads = []
    for n, down_ref in enumerate(down_refs):
        size = down_ref.shape[0]
        if size == hidden:
            at = 0
        else:
            slab = lax.rem(position_ref[0] + 2 * (chips - n // 2), 2 * chips) ^ (n % 2)
            at = pl.multiple_of(slab * size, 16)
        loads.append(pltpu.make_async_copy(down_ref, down.at[pl.ds(at, size)], sems.at[n]))
    for load in loads:
        load.start()
    for load in loads:
        load.wait()
    scores = None
    step = 2 * LANES
    for at in range(0, hidden, step):
        span = slice(at, at + step)
        back = lax.dot_general(
            grads_ref[...], down[span, :], (((1,), (1,)), ((), ())), preferred_element_type=f32
        )
        part = jnp.sum(score_factor[:, span] * back, axis=1, keepdims=True)
        scores = part if scores is None else scores + part
        gate = (gate_factor[:, span] * back).astype(bf16)
        up = (up_factor[:, span] * back).astype(bf16)
        gate_ref[:, span] = gate
        up_ref[:, span] = up
        joined_ref[:, span] = gate
        joined_ref[:, hidden + at : hidden + at + step] = up
    scores_ref[...] = jnp.broadcast_to(scores, scores_ref.shape)


def router_kernel(position_ref, select_ref, rows_ref, out_ref):
    experts = rows_ref.shape[0]
    own = [rows_ref[k, position_ref[0], :, :LANES] for k in range(experts)]
    parts = jnp.concatenate(own, axis=0).astype(f32)
    scores = (parts[:, 1:2] + parts[:, 2:3]) + parts[:, 3:4]
    out_ref[...] = jnp.sum(jnp.where(select_ref[...] > 0.5, scores, 0.0), axis=0, keepdims=True)


def head_kernel(master_any, first_any, second_any, out_ref, sems):
    count = out_ref.shape[1]
    copies = [
        pltpu.make_async_copy(source.at[pl.ds(0, count)], out_ref.at[n], sems.at[n])
        for n, source in enumerate((master_any, first_any, second_any))
    ]
    for copy in copies:
        copy.start()
    for copy in copies:
        copy.wait()


def slab_sum(total, turned_ref, slabs, joined):
    for slab, (ref, at, step) in zip(slabs, joined):
        piece = jnp.dot(turned_ref[slab], ref[:, at : at + step], preferred_element_type=f32)
        piece = piece.astype(bf16).astype(f32)
        total = piece if total is None else total + piece
    return total


def slabs_of(position, steps, chips):
    own = [lax.rem(position + 2 * (chips - k), 2 * chips) for k in steps]
    return [slab ^ other for slab in own for other in (0, 1)]


def early_kernel(position_ref, turned_ref, *refs, steps, chips):
    refs, sum_ref = list(refs[:-1]), refs[-1]
    hidden = sum_ref.shape[1] // 2
    step = 2 * LANES
    slabs = slabs_of(position_ref[0], steps, chips)
    lists = ([], [])
    for k in steps:
        for other in range(2):
            whole = refs.pop(0) if k == 0 else None
            for half in range(2):
                lists[half].append((whole, half * hidden) if k == 0 else (refs.pop(0), 0))
    base = refs[0] if refs else None
    for half in range(2):
        for at in range(0, hidden, step):
            span = slice(half * hidden + at, half * hidden + at + step)
            joined = [(ref, first + at, step) for ref, first in lists[half]]
            total = None if base is None else base[:, span]
            sum_ref[:, span] = slab_sum(total, turned_ref, slabs, joined)


def adam(grad, old, first, second):
    first_new = beta_one * first + (1.0 - beta_one) * grad
    second_new = beta_two * second + (1.0 - beta_two) * grad * grad
    below = jnp.sqrt(second_new * (1.0 / (1.0 - beta_two**adam_step))) + adam_eps
    update = first_new * (learn_rate / (1.0 - beta_one**adam_step)) / below
    return old * (1.0 - learn_rate * decay_rate) - update, first_new, second_new


def final_kernel(
    position_ref,
    offsets_ref,
    turned_ref,
    early_ref,
    heads_ref,
    gate_own,
    up_own,
    gate_other,
    up_other,
    old,
    first,
    second,
    out_master,
    out_first,
    out_second,
    weight_ref,
    sums,
    moved,
    new_old,
    new_first,
    new_second,
    head_new,
    sems,
    *,
    even_size,
    head_rows,
    chips,
):
    kept, columns = early_ref.shape
    hidden = columns // 2
    per = weight_ref.shape[0]
    lines = columns // LANES
    before = (kept - per) * lines
    bucket_rows = old.shape[0]
    flat_rows = even_size // LANES
    position = position_ref[0]
    start = offsets_ref[position]
    finish = offsets_ref[position + 1]
    shift = position * even_size - start
    next_shift = (position + 1) * even_size - finish
    length = finish - start
    whole, part = shift // LANES, shift % LANES
    odd = whole % 8
    next_whole, next_part = next_shift // LANES, next_shift % LANES

    step = 2 * LANES
    slabs = slabs_of(position, [chips - 1], chips)
    for half, refs in enumerate(((gate_own, gate_other), (up_own, up_other))):
        for at in range(0, hidden, step):
            begin = half * hidden + at
            total = slab_sum(
                early_ref[:, begin : begin + step], turned_ref, slabs, [(ref, at, step) for ref in refs]
            )
            for c in range(step // LANES):
                block = total[:, c * LANES : (c + 1) * LANES]
                line = begin // LANES + c
                block = pltpu.roll(block, part, 1)
                sums[pl.ds(odd + line, kept, stride=lines), :] = block
                moved[pl.ds(odd + line + 1, kept, stride=lines), :] = block

    def slots_of(row, count):
        at = pl.multiple_of(row + before - (whole - odd), 8)
        lane = iota((count, LANES), 1)
        return jnp.where(lane >= part, sums[pl.ds(at, count), :], moved[pl.ds(at, count), :])

    def update(row, count):
        span = pl.ds(row, count)
        a, b, c = adam(slots_of(row, count), old[span, :], first[span, :], second[span, :])
        new_old[span, :], new_first[span, :], new_second[span, :] = a, b, c

    def masked(row, count):
        span = pl.ds(row, count)
        inside = (row + iota((count, LANES), 0)) * LANES + iota((count, LANES), 1) < length
        grad = jnp.where(inside, slots_of(row, count), 0.0)
        a, b, c = adam(grad, old[span, :], first[span, :], second[span, :])
        new_old[span, :] = jnp.where(inside, a, 0.0)
        new_first[span, :] = jnp.where(inside, b, 0.0)
        new_second[span, :] = jnp.where(inside, c, 0.0)

    def send(begin, count, slot):
        span = pl.ds(begin, count)
        stores = [
            pltpu.make_async_copy(source.at[span], target.at[span], sems.at[slot, n])
            for n, (source, target) in enumerate(
                ((new_old, out_master), (new_first, out_first), (new_second, out_second))
            )
        ]
        for store in stores:
            store.start()
        return stores

    def chunk(n, carry):
        update(pl.multiple_of(n * CHUNK, 8), CHUNK)
        return carry

    safe = (flat_rows - head_rows) // CHUNK
    third = -(-safe // 3)
    stores = []
    for slot, begin in enumerate(range(0, safe, third)):
        end = min(begin + third, safe)
        lax.fori_loop(begin, end, chunk, 0)
        stores += send(begin * CHUNK, (end - begin) * CHUNK, slot)
    for row in range(safe * CHUNK, bucket_rows, CHUNK):
        masked(row, min(CHUNK, bucket_rows - row))
    stores += send(safe * CHUNK, bucket_rows - safe * CHUNK, 3)

    def next_slots():
        lane = iota((head_rows, LANES), 1)
        base = flat_rows + before - next_whole + odd
        here = pltpu.roll(sums[pl.ds(base, head_rows), :], (LANES - part) % LANES, 1)
        above = pltpu.roll(sums[pl.ds(base - 1, head_rows), :], (LANES - part) % LANES, 1)
        return pltpu.roll(jnp.where(lane < LANES - next_part, here, above), next_part, 1)

    edge = round_up(-(-head_rows // lines), 16)
    head_new[pl.ds(edge * lines, head_rows), :] = adam(next_slots(), heads_ref[0], heads_ref[1], heads_ref[2])[0]

    flat_row = iota((edge, LANES), 0) + (per - edge)
    for c in range(lines):
        lane = iota((per, LANES), 1)
        here = new_old[pl.ds(c + whole, per, stride=lines), :]
        below = new_old[pl.ds(c + whole + 1, per, stride=lines), :]
        own = pltpu.roll(jnp.where(lane >= part, here, below), (LANES - part) % LANES, 1)
        base = c + next_whole
        lane = iota((edge, LANES), 1)
        here = head_new[pl.ds(base, edge, stride=lines), :]
        below = head_new[pl.ds(base + 1, edge, stride=lines), :]
        other = pltpu.roll(jnp.where(lane >= next_part, here, below), (LANES - next_part) % LANES, 1)
        flat = (flat_row * lines + c) * LANES + lane
        last = jnp.where(flat < even_size - next_shift, own[per - edge :], other)
        out = slice(c * LANES, (c + 1) * LANES)
        if per > edge:
            weight_ref[: per - edge, out] = own[: per - edge].astype(bf16)
        weight_ref[per - edge :, out] = last.astype(bf16)

    for store in stores:
        store.wait()


def vmem():
    return pl.BlockSpec(memory_space=pltpu.VMEM)


def anywhere():
    return pl.BlockSpec(memory_space=pl.ANY)


def hbm():
    return pl.BlockSpec(memory_space=pltpu.HBM)


def smem():
    return pl.BlockSpec(memory_space=pltpu.SMEM)


def call(kernel, outs, scalars, args, name, mib, flops=0, moved=0):
    many = isinstance(outs, (list, tuple))
    return pl.pallas_call(
        kernel,
        out_shape=outs,
        in_specs=[smem()] * len(scalars) + [vmem()] * len(args),
        out_specs=[vmem()] * len(outs) if many else vmem(),
        compiler_params=params(mib),
        cost_estimate=cost(flops, moved),
        name=name,
    )(*scalars, *args)


def struct(shape, kind):
    return jax.ShapeDtypeStruct(shape, kind)


def shards(
    tokens,
    out_grad,
    gate_up,
    route_weight,
    routes,
    down_weight,
    master,
    moment_one,
    moment_two,
    offsets,
):
    token_count, model_width = tokens.shape
    columns = gate_up.shape[2]
    hidden = columns // 2
    bucket_cap = master.shape[2]
    groups = lax.axis_size("expert")
    parts = lax.axis_size("dp")
    experts = groups * master.shape[0]
    cap = 2 * token_count // experts
    rows = experts * cap
    per = model_width // parts
    even_size = per * columns
    margin = bucket_cap - even_size
    extra = round_up(-(-margin // columns), 16)
    width = round_up(per + extra + 4, LANES)
    kept = per + extra
    lines = columns // LANES
    bucket_rows = bucket_cap // LANES
    head_rows = round_up(margin // LANES, 8)

    chips = parts // 2
    position = lax.axis_index("dp").astype(i32).reshape(1)
    state = struct((bucket_rows, LANES), f32)
    old, first, second = (array.reshape(bucket_rows, LANES) for array in (master, moment_one, moment_two))

    def onward(block):
        return lax.ppermute(block, "dp", [(i, (i + 2) % parts) for i in range(parts)])

    def swapped(block):
        return lax.ppermute(block, "dp", [(i, i ^ 1) for i in range(parts)])

    def exchanged(block, axis):
        return lax.all_to_all(block, axis, split_axis=0, concat_axis=0, tiled=True)

    def tied(*values):
        return lax.optimization_barrier(values)

    wide = model_width + columns + LANES
    select, target, packed = call(
        pack_kernel,
        [
            struct((rows, token_count), f32),
            struct((1, token_count), f32),
            struct((experts, cap, wide), bf16),
        ],
        (),
        (
            routes.reshape(1, token_count),
            route_weight.reshape(1, token_count),
            out_grad,
            gate_up.reshape(token_count, columns),
        ),
        "pack",
        16,
        moved=6_000_000,
    )
    windows = call(
        functools.partial(window_kernel, per=per, lead=width - per),
        struct((parts, token_count, width), bf16),
        (),
        (target, tokens),
        "window",
        12,
        moved=2_000_000,
    )
    heads = pl.pallas_call(
        head_kernel,
        out_shape=struct((3, head_rows, LANES), f32),
        in_specs=[hbm()] * 3,
        out_specs=vmem(),
        scratch_shapes=[pltpu.SemaphoreType.DMA((3,))],
        compiler_params=params(4),
        cost_estimate=cost(0, 400_000),
        name="heads",
    )(old, first, second)
    heads = lax.ppermute(heads, "dp", [(i + 1, i) for i in range(parts - 1)])
    if down_weight.shape[1] % 16 == 0:
        held, other = [down_weight[0]], [swapped(down_weight[0])]
        for k in range(1, chips):
            arrival = onward(held[-1])
            if k == 1:
                arrival, packed, windows, heads = tied(arrival, packed, windows, heads)
            elif k == chips - 2:
                arrival, windows, other = tied(arrival, windows, other)
            else:
                arrival, other = tied(arrival, other)
            held.append(arrival)
            other.append(swapped(arrival))
        down = [piece for pair in zip(held, other) for piece in pair]
    else:
        down = [lax.all_gather(down_weight, "dp", axis=1, tiled=True)[0]]
        windows, down[0] = tied(windows, down[0])
    arrived = exchanged(packed, "expert").reshape(rows, wide)
    windows = exchanged(windows, "dp")
    factors = call(
        factor_kernel,
        [struct((rows, model_width), bf16)] + [struct((rows, hidden), f32)] * 3,
        (),
        (arrived,),
        "factors",
        20,
        moved=6_000_000,
    )
    gate, up, joined, scores = pl.pallas_call(
        functools.partial(row_kernel, chips=chips),
        out_shape=[struct((rows, hidden), bf16)] * 2
        + [struct((rows, columns), bf16), struct((rows, LANES), f32)],
        in_specs=[smem()] + [vmem()] * 4 + [anywhere()] * len(down),
        out_specs=[vmem()] * 4,
        scratch_shapes=[
            pltpu.VMEM((hidden, model_width), bf16),
            pltpu.SemaphoreType.DMA((len(down),)),
        ],
        compiler_params=params(24),
        cost_estimate=cost(2 * rows * model_width * hidden, 8_000_000),
        name="rows",
    )(position, *factors, *down)

    halves = [gate, up]
    steps = [[joined, swapped(joined)]]
    first_step = [onward(half) for half in halves]
    first_step[0], windows, scores = tied(first_step[0], windows, scores)
    compacted = call(
        compact_kernel,
        struct((experts, parts, cap, width), bf16),
        (position,),
        (windows, scores),
        "compact",
        12,
        moved=3_000_000,
    )
    compacted_rows = exchanged(compacted, "expert")
    turned = call(
        turn_kernel,
        struct((parts, kept, rows), bf16),
        (),
        (compacted_rows,),
        "turn",
        12,
        moved=3_000_000,
    )
    router_grad = call(
        router_kernel,
        struct((1, token_count), f32),
        (position,),
        (select, compacted_rows),
        "router",
        4,
        moved=300_000,
    )

    def early(name, at, pieces, sum_before):
        return call(
            functools.partial(early_kernel, steps=at, chips=chips),
            struct((kept, columns), f32),
            (position,),
            [turned] + pieces + sum_before,
            name,
            24,
            flops=4 * len(at) * rows * kept * columns,
            moved=8_000_000,
        )

    total = []
    for k in range(1, chips):
        halves = [onward(half) for half in halves] if k > 1 else first_step
        if k > 2:
            pieces = steps.pop()
            if k == 3:
                begun = early("early1", [0, 1], steps.pop(0) + steps.pop(0), [])
                halves[0], begun, router_grad = tied(halves[0], begun, router_grad)
                total = [begun]
            total = [early("early%d" % (k - 1), [k - 1], pieces, total)]
            halves[1], total[0] = tied(halves[1], total[0])
        steps.append(halves + [swapped(half) for half in halves])
    last = steps.pop()
    flat_rows = even_size // LANES
    sum_rows = round_up(kept * lines + head_rows + 32, 8)
    edge = round_up(-(-head_rows // lines), 16)
    new_master, new_one, new_two, new_weight = pl.pallas_call(
        functools.partial(final_kernel, even_size=even_size, head_rows=head_rows, chips=chips),
        out_shape=[state, state, state, struct((per, columns), bf16)],
        in_specs=[smem()] * 2 + [vmem()] * 10,
        out_specs=[anywhere(), anywhere(), anywhere(), vmem()],
        scratch_shapes=[
            pltpu.VMEM((sum_rows, LANES), f32),
            pltpu.VMEM((sum_rows, LANES), f32),
            pltpu.VMEM((round_up(flat_rows + head_rows + 32, 8), LANES), f32),
            pltpu.VMEM((bucket_rows, LANES), f32),
            pltpu.VMEM((bucket_rows, LANES), f32),
            pltpu.VMEM((edge * lines + 2 * head_rows + 32, LANES), f32),
            pltpu.SemaphoreType.DMA((4, 3)),
        ],
        compiler_params=params(32),
        cost_estimate=cost(4 * rows * kept * columns, 25_000_000),
        name="final",
    )(
        position,
        offsets,
        turned,
        total[0],
        heads,
        *last,
        old,
        first,
        second,
    )
    return (
        new_master.reshape(1, 1, bucket_cap),
        new_one.reshape(1, 1, bucket_cap),
        new_two.reshape(1, 1, bucket_cap),
        new_weight[None],
        router_grad.reshape(token_count, 1),
    )


def solution(mesh):
    placed = (
        P(("dp", "expert"), None),
        P(("dp", "expert"), None),
        P(("dp", "expert"), None, None),
        P(("dp", "expert"), None),
        P(("dp", "expert"), None),
        P("expert", "dp", None),
        P("expert", "dp", None),
        P("expert", "dp", None),
        P("expert", "dp", None),
        P(),
    )
    return jax.shard_map(
        shards,
        mesh=mesh,
        in_specs=placed,
        out_specs=(
            P("expert", "dp", None),
            P("expert", "dp", None),
            P("expert", "dp", None),
            P("expert", "dp", None),
            P(("dp", "expert"), None),
        ),
        check_vma=False,
    )
```

```python
import functools

import jax
import jax.numpy as jnp
from jax import lax
from jax.experimental import pallas as pl
from jax.experimental.pallas import tpu as pltpu
from jax.sharding import PartitionSpec as P

beta_one = 0.9
beta_two = 0.95
learn_rate = 0.001
decay_rate = 0.1
adam_eps = 1e-08
adam_step = 20.0

LANES = 128
CHUNK = 120

f32 = jnp.float32
bf16 = jnp.bfloat16
i32 = jnp.int32


def round_up(value, unit):
    return -(-value // unit) * unit


def iota(shape, axis):
    return lax.broadcasted_iota(i32, shape, axis)


def params(mib):
    return pltpu.CompilerParams(vmem_limit_bytes=mib * 1024 * 1024)


def cost(flops, moved):
    return pl.CostEstimate(flops=int(flops), bytes_accessed=int(moved), transcendentals=0)


def pack_kernel(
    routes_ref, weight_ref, grads_any, saved_any, select_ref, target_ref, packed_any, grads, saved, packed, sems
):
    loads = [
        pltpu.make_async_copy(grads_any, grads, sems.at[0]),
        pltpu.make_async_copy(saved_any, saved, sems.at[1]),
    ]
    for load in loads:
        load.start()
    ids = routes_ref[...]
    experts, cap, _ = packed.shape
    count = ids.shape[1]
    width = grads.shape[1]
    hits = iota((round_up(experts, 8), count), 0) == ids
    before = (iota((count, count), 0) < iota((count, count), 1)).astype(bf16)
    earlier = jnp.dot(hits.astype(f32).astype(bf16), before, preferred_element_type=f32)
    slot = jnp.sum(jnp.where(hits, earlier, 0.0), axis=0, keepdims=True)
    target = ids * cap + slot.astype(i32)
    chosen = iota((experts * cap, count), 0) == target
    select = chosen.astype(f32).astype(bf16)
    select_ref[...] = chosen.astype(f32)
    target_ref[...] = target.astype(f32)
    weight = jnp.sum(jnp.where(chosen, weight_ref[...].astype(f32), 0.0), axis=1, keepdims=True)
    weight = jnp.broadcast_to(weight, (experts * cap, LANES)).astype(bf16)
    for load in loads:
        load.wait()
    picked_grads = jnp.dot(select, grads[...], preferred_element_type=f32).astype(bf16)
    picked_saved = jnp.dot(select, saved[...], preferred_element_type=f32).astype(bf16)
    stores = []
    for k in range(experts):
        span = slice(k * cap, (k + 1) * cap)
        packed[k, :, :width] = picked_grads[span]
        packed[k, :, width:-LANES] = picked_saved[span]
        packed[k, :, -LANES:] = weight[span]
        stores.append(pltpu.make_async_copy(packed.at[k], packed_any.at[k], sems.at[2 + k]))
        stores[-1].start()
    for store in stores:
        store.wait()


def window_kernel(target_ref, tokens_ref, out_ref, *, per, lead):
    parts, count, width = out_ref.shape
    diagonal = iota((count, count), 0) == iota((count, count), 1)
    column = jnp.sum(jnp.where(diagonal, target_ref[...], 0.0), axis=1, keepdims=True)
    note = jnp.broadcast_to(column, (count, width)).astype(bf16)
    lane = iota((count, width), 1)
    for j in range(parts):
        start = per * j - lead
        if start < 0:
            blank = jnp.zeros((count, -start), bf16)
            piece = jnp.concatenate([blank, tokens_ref[:, : start + width]], axis=1)
        else:
            piece = tokens_ref[:, start : start + width]
        out_ref[j] = jnp.where(lane == 0, note, piece)


def compact_kernel(position_ref, windows_ref, scores_ref, out_ref):
    parts, count, width = windows_ref.shape
    experts, _, cap, _ = out_ref.shape
    diagonal = iota((count, count), 0) == iota((count, count), 1)
    slots = iota((experts * cap, count), 0)
    for i in range(parts):
        block = windows_ref[i]
        column = block[:, 0:1].astype(f32)
        target = jnp.sum(jnp.where(diagonal, column, 0.0), axis=0, keepdims=True).astype(i32)
        select = (slots == target).astype(f32).astype(bf16)
        rows = jnp.dot(select, block, preferred_element_type=f32).astype(bf16)
        for k in range(experts):
            out_ref[k, i] = rows[k * cap : (k + 1) * cap]
    lane = iota((cap, LANES), 1)
    for k in range(experts):
        rest = scores_ref[k * cap : (k + 1) * cap, :]
        first = out_ref[k, position_ref[0], :, :LANES]
        for c in range(3):
            part = rest.astype(bf16)
            rest = rest - part.astype(f32)
            first = jnp.where(lane == 1 + c, part, first)
        out_ref[k, position_ref[0], :, :LANES] = first


def turn_kernel(rows_ref, out_ref):
    experts, parts, _, width = rows_ref.shape
    kept = out_ref.shape[1]
    for i in range(parts):
        slab = jnp.concatenate([rows_ref[k, i] for k in range(experts)], axis=0)
        out_ref[i] = slab.T[width - kept :, :]


def factor_kernel(arrived_ref, grads_ref, gate_ref, up_ref, score_ref):
    width, hidden = grads_ref.shape[1], gate_ref.shape[1]
    grads_ref[...] = arrived_ref[:, :width]
    gate = arrived_ref[:, width : width + hidden].astype(f32)
    up = arrived_ref[:, width + hidden : width + 2 * hidden].astype(f32)
    weight = arrived_ref[:, width + 2 * hidden :].astype(f32)[:, 0:1]
    sig = jax.nn.sigmoid(gate)
    act = gate * sig
    score_ref[...] = act * up
    up_ref[...] = weight * act
    gate_ref[...] = weight * (up * sig * (1.0 + gate * (1.0 - sig)))


def row_kernel(position_ref, grads_ref, gate_factor, up_factor, score_factor, *refs, chips):
    down_refs, refs = refs[:-8], refs[-8:]
    gate_any, up_any, joined_ref, scores_ref, gate_half, up_half, down, sems = refs
    hidden = down.shape[0]
    loads = []
    for n, down_ref in enumerate(down_refs):
        size = down_ref.shape[0]
        if size == hidden:
            at = 0
        else:
            slab = lax.rem(position_ref[0] + 2 * (chips - n // 2), 2 * chips) ^ (n % 2)
            at = pl.multiple_of(slab * size, 16)
        loads.append(pltpu.make_async_copy(down_ref, down.at[pl.ds(at, size)], sems.at[n]))
    for load in loads:
        load.start()
    for load in loads:
        load.wait()
    scores = None
    step = 2 * LANES
    stores = []
    for at in range(0, hidden, step):
        span = slice(at, at + step)
        back = lax.dot_general(
            grads_ref[...], down[span, :], (((1,), (1,)), ((), ())), preferred_element_type=f32
        )
        part = jnp.sum(score_factor[:, span] * back, axis=1, keepdims=True)
        scores = part if scores is None else scores + part
        gate = (gate_factor[:, span] * back).astype(bf16)
        up = (up_factor[:, span] * back).astype(bf16)
        gate_half[:, span] = gate
        up_half[:, span] = up
        joined_ref[:, span] = gate
        joined_ref[:, hidden + at : hidden + at + step] = up
        for half, (source, target) in enumerate(((gate_half, gate_any), (up_half, up_any))):
            sem = sems.at[len(down_refs) + 2 * (at // step) + half]
            stores.append(pltpu.make_async_copy(source.at[:, span], target.at[:, span], sem))
            stores[-1].start()
    scores_ref[...] = jnp.broadcast_to(scores, scores_ref.shape)
    for store in stores:
        store.wait()


def router_kernel(position_ref, select_ref, rows_ref, out_ref):
    experts = rows_ref.shape[0]
    own = [rows_ref[k, position_ref[0], :, :LANES] for k in range(experts)]
    parts = jnp.concatenate(own, axis=0).astype(f32)
    scores = (parts[:, 1:2] + parts[:, 2:3]) + parts[:, 3:4]
    out_ref[...] = jnp.sum(jnp.where(select_ref[...] > 0.5, scores, 0.0), axis=0, keepdims=True)


def head_kernel(master_any, first_any, second_any, out_ref, sems):
    count = out_ref.shape[1]
    copies = [
        pltpu.make_async_copy(source.at[pl.ds(0, count)], out_ref.at[n], sems.at[n])
        for n, source in enumerate((master_any, first_any, second_any))
    ]
    for copy in copies:
        copy.start()
    for copy in copies:
        copy.wait()


def slab_sum(total, turned_ref, slabs, joined):
    for slab, (ref, at, step) in zip(slabs, joined):
        piece = jnp.dot(turned_ref[slab], ref[:, at : at + step], preferred_element_type=f32)
        piece = piece.astype(bf16).astype(f32)
        total = piece if total is None else total + piece
    return total


def slabs_of(position, steps, chips):
    own = [lax.rem(position + 2 * (chips - k), 2 * chips) for k in steps]
    return [slab ^ other for slab in own for other in (0, 1)]


def early_kernel(position_ref, turned_ref, *refs, steps, chips):
    refs, sum_ref = list(refs[:-1]), refs[-1]
    hidden = sum_ref.shape[1] // 2
    step = 2 * LANES
    slabs = slabs_of(position_ref[0], steps, chips)
    lists = ([], [])
    for k in steps:
        for other in range(2):
            whole = refs.pop(0) if k == 0 else None
            for half in range(2):
                lists[half].append((whole, half * hidden) if k == 0 else (refs.pop(0), 0))
    base = refs[0] if refs else None
    for half in range(2):
        for at in range(0, hidden, step):
            span = slice(half * hidden + at, half * hidden + at + step)
            joined = [(ref, first + at, step) for ref, first in lists[half]]
            total = None if base is None else base[:, span]
            sum_ref[:, span] = slab_sum(total, turned_ref, slabs, joined)


def adam(grad, old, first, second):
    first_new = beta_one * first + (1.0 - beta_one) * grad
    second_new = beta_two * second + (1.0 - beta_two) * grad * grad
    below = jnp.sqrt(second_new * (1.0 / (1.0 - beta_two**adam_step))) + adam_eps
    update = first_new * (learn_rate / (1.0 - beta_one**adam_step)) / below
    return old * (1.0 - learn_rate * decay_rate) - update, first_new, second_new


def final_kernel(
    position_ref,
    offsets_ref,
    turned_ref,
    early_ref,
    heads_ref,
    gate_own,
    up_own,
    gate_other,
    up_other,
    old,
    first,
    second,
    out_master,
    out_first,
    out_second,
    weight_ref,
    sums,
    moved,
    new_old,
    new_first,
    new_second,
    head_new,
    sems,
    *,
    even_size,
    head_rows,
    chips,
):
    kept, columns = early_ref.shape
    hidden = columns // 2
    per = weight_ref.shape[0]
    lines = columns // LANES
    before = (kept - per) * lines
    bucket_rows = old.shape[0]
    flat_rows = even_size // LANES
    position = position_ref[0]
    start = offsets_ref[position]
    finish = offsets_ref[position + 1]
    shift = position * even_size - start
    next_shift = (position + 1) * even_size - finish
    length = finish - start
    whole, part = shift // LANES, shift % LANES
    odd = whole % 8
    next_whole, next_part = next_shift // LANES, next_shift % LANES

    step = 2 * LANES
    slabs = slabs_of(position, [chips - 1], chips)
    for half, refs in enumerate(((gate_own, gate_other), (up_own, up_other))):
        for at in range(0, hidden, step):
            begin = half * hidden + at
            total = slab_sum(
                early_ref[:, begin : begin + step], turned_ref, slabs, [(ref, at, step) for ref in refs]
            )
            for c in range(step // LANES):
                block = total[:, c * LANES : (c + 1) * LANES]
                line = begin // LANES + c
                block = pltpu.roll(block, part, 1)
                sums[pl.ds(odd + line, kept, stride=lines), :] = block
                moved[pl.ds(odd + line + 1, kept, stride=lines), :] = block

    def slots_of(row, count):
        at = pl.multiple_of(row + before - (whole - odd), 8)
        lane = iota((count, LANES), 1)
        return jnp.where(lane >= part, sums[pl.ds(at, count), :], moved[pl.ds(at, count), :])

    def update(row, count):
        span = pl.ds(row, count)
        a, b, c = adam(slots_of(row, count), old[span, :], first[span, :], second[span, :])
        new_old[span, :], new_first[span, :], new_second[span, :] = a, b, c

    def masked(row, count):
        span = pl.ds(row, count)
        inside = (row + iota((count, LANES), 0)) * LANES + iota((count, LANES), 1) < length
        grad = jnp.where(inside, slots_of(row, count), 0.0)
        a, b, c = adam(grad, old[span, :], first[span, :], second[span, :])
        new_old[span, :] = jnp.where(inside, a, 0.0)
        new_first[span, :] = jnp.where(inside, b, 0.0)
        new_second[span, :] = jnp.where(inside, c, 0.0)

    def send(begin, count, slot):
        span = pl.ds(begin, count)
        stores = [
            pltpu.make_async_copy(source.at[span], target.at[span], sems.at[slot, n])
            for n, (source, target) in enumerate(
                ((new_old, out_master), (new_first, out_first), (new_second, out_second))
            )
        ]
        for store in stores:
            store.start()
        return stores

    def chunk(n, carry):
        update(pl.multiple_of(n * CHUNK, 8), CHUNK)
        return carry

    safe = (flat_rows - head_rows) // CHUNK
    third = -(-safe // 3)
    stores = []
    for slot, begin in enumerate(range(0, safe, third)):
        end = min(begin + third, safe)
        lax.fori_loop(begin, end, chunk, 0)
        stores += send(begin * CHUNK, (end - begin) * CHUNK, slot)
    for row in range(safe * CHUNK, bucket_rows, CHUNK):
        masked(row, min(CHUNK, bucket_rows - row))
    stores += send(safe * CHUNK, bucket_rows - safe * CHUNK, 3)

    def next_slots():
        lane = iota((head_rows, LANES), 1)
        base = flat_rows + before - next_whole + odd
        here = pltpu.roll(sums[pl.ds(base, head_rows), :], (LANES - part) % LANES, 1)
        above = pltpu.roll(sums[pl.ds(base - 1, head_rows), :], (LANES - part) % LANES, 1)
        return pltpu.roll(jnp.where(lane < LANES - next_part, here, above), next_part, 1)

    edge = round_up(-(-head_rows // lines), 16)
    head_new[pl.ds(edge * lines, head_rows), :] = adam(next_slots(), heads_ref[0], heads_ref[1], heads_ref[2])[0]

    flat_row = iota((edge, LANES), 0) + (per - edge)
    for c in range(lines):
        lane = iota((per, LANES), 1)
        here = new_old[pl.ds(c + whole, per, stride=lines), :]
        below = new_old[pl.ds(c + whole + 1, per, stride=lines), :]
        own = pltpu.roll(jnp.where(lane >= part, here, below), (LANES - part) % LANES, 1)
        base = c + next_whole
        lane = iota((edge, LANES), 1)
        here = head_new[pl.ds(base, edge, stride=lines), :]
        below = head_new[pl.ds(base + 1, edge, stride=lines), :]
        other = pltpu.roll(jnp.where(lane >= next_part, here, below), (LANES - next_part) % LANES, 1)
        flat = (flat_row * lines + c) * LANES + lane
        last = jnp.where(flat < even_size - next_shift, own[per - edge :], other)
        out = slice(c * LANES, (c + 1) * LANES)
        if per > edge:
            weight_ref[: per - edge, out] = own[: per - edge].astype(bf16)
        weight_ref[per - edge :, out] = last.astype(bf16)

    for store in stores:
        store.wait()


def vmem():
    return pl.BlockSpec(memory_space=pltpu.VMEM)


def anywhere():
    return pl.BlockSpec(memory_space=pl.ANY)


def hbm():
    return pl.BlockSpec(memory_space=pltpu.HBM)


def smem():
    return pl.BlockSpec(memory_space=pltpu.SMEM)


def call(kernel, outs, scalars, args, name, mib, flops=0, moved=0):
    many = isinstance(outs, (list, tuple))
    return pl.pallas_call(
        kernel,
        out_shape=outs,
        in_specs=[smem()] * len(scalars) + [vmem()] * len(args),
        out_specs=[vmem()] * len(outs) if many else vmem(),
        compiler_params=params(mib),
        cost_estimate=cost(flops, moved),
        name=name,
    )(*scalars, *args)


def struct(shape, kind):
    return jax.ShapeDtypeStruct(shape, kind)


def shards(
    tokens,
    out_grad,
    gate_up,
    route_weight,
    routes,
    down_weight,
    master,
    moment_one,
    moment_two,
    offsets,
):
    token_count, model_width = tokens.shape
    columns = gate_up.shape[2]
    hidden = columns // 2
    bucket_cap = master.shape[2]
    groups = lax.axis_size("expert")
    parts = lax.axis_size("dp")
    experts = groups * master.shape[0]
    cap = 2 * token_count // experts
    rows = experts * cap
    per = model_width // parts
    even_size = per * columns
    margin = bucket_cap - even_size
    extra = round_up(-(-margin // columns), 16)
    width = round_up(per + extra + 4, LANES)
    kept = per + extra
    lines = columns // LANES
    bucket_rows = bucket_cap // LANES
    head_rows = round_up(margin // LANES, 8)

    chips = parts // 2
    position = lax.axis_index("dp").astype(i32).reshape(1)
    state = struct((bucket_rows, LANES), f32)
    old, first, second = (array.reshape(bucket_rows, LANES) for array in (master, moment_one, moment_two))

    def onward(block):
        return lax.ppermute(block, "dp", [(i, (i + 2) % parts) for i in range(parts)])

    def swapped(block):
        return lax.ppermute(block, "dp", [(i, i ^ 1) for i in range(parts)])

    def exchanged(block, axis):
        return lax.all_to_all(block, axis, split_axis=0, concat_axis=0, tiled=True)

    def tied(*values):
        return lax.optimization_barrier(values)

    wide = model_width + columns + LANES
    select, target, packed = pl.pallas_call(
        pack_kernel,
        out_shape=[
            struct((rows, token_count), f32),
            struct((1, token_count), f32),
            struct((experts, cap, wide), bf16),
        ],
        in_specs=[vmem(), vmem(), hbm(), hbm()],
        out_specs=[vmem(), vmem(), hbm()],
        scratch_shapes=[
            pltpu.VMEM((token_count, model_width), bf16),
            pltpu.VMEM((token_count, columns), bf16),
            pltpu.VMEM((experts, cap, wide), bf16),
            pltpu.SemaphoreType.DMA((2 + experts,)),
        ],
        compiler_params=params(16),
        cost_estimate=cost(0, 6_000_000),
        name="pack",
    )(
        routes.reshape(1, token_count),
        route_weight.reshape(1, token_count),
        out_grad,
        gate_up.reshape(token_count, columns),
    )
    windows = call(
        functools.partial(window_kernel, per=per, lead=width - per),
        struct((parts, token_count, width), bf16),
        (),
        (target, tokens),
        "window",
        12,
        moved=2_000_000,
    )
    heads = pl.pallas_call(
        head_kernel,
        out_shape=struct((3, head_rows, LANES), f32),
        in_specs=[hbm()] * 3,
        out_specs=vmem(),
        scratch_shapes=[pltpu.SemaphoreType.DMA((3,))],
        compiler_params=params(4),
        cost_estimate=cost(0, 400_000),
        name="heads",
    )(old, first, second)
    heads = lax.ppermute(heads, "dp", [(i + 1, i) for i in range(parts - 1)])
    if down_weight.shape[1] % 16 == 0:
        held, other = [down_weight[0]], [swapped(down_weight[0])]
        for k in range(1, chips):
            arrival = onward(held[-1])
            if k == 1:
                arrival, windows, heads = tied(arrival, windows, heads)
            else:
                arrival, other = tied(arrival, other)
            held.append(arrival)
            other.append(swapped(arrival))
            if k == chips - 2:
                windows, other[-1] = tied(windows, other[-1])
        down = [piece for pair in zip(held, other) for piece in pair]
    else:
        down = [lax.all_gather(down_weight, "dp", axis=1, tiled=True)[0]]
        windows, down[0] = tied(windows, down[0])
    arrived = exchanged(packed, "expert").reshape(rows, wide)
    windows = exchanged(windows, "dp")
    factors = call(
        factor_kernel,
        [struct((rows, model_width), bf16)] + [struct((rows, hidden), f32)] * 3,
        (),
        (arrived,),
        "factors",
        20,
        moved=6_000_000,
    )
    gate, up, joined, scores = pl.pallas_call(
        functools.partial(row_kernel, chips=chips),
        out_shape=[struct((rows, hidden), bf16)] * 2
        + [struct((rows, columns), bf16), struct((rows, LANES), f32)],
        in_specs=[smem()] + [vmem()] * 4 + [anywhere()] * len(down),
        out_specs=[hbm(), hbm(), vmem(), vmem()],
        scratch_shapes=[
            pltpu.VMEM((rows, hidden), bf16),
            pltpu.VMEM((rows, hidden), bf16),
            pltpu.VMEM((hidden, model_width), bf16),
            pltpu.SemaphoreType.DMA((len(down) + 2 * (hidden // (2 * LANES)),)),
        ],
        compiler_params=params(24),
        cost_estimate=cost(2 * rows * model_width * hidden, 8_000_000),
        name="rows",
    )(position, *factors, *down)

    halves = [gate, up]
    steps = [[joined, swapped(joined)]]
    first_step = [onward(half) for half in halves]
    first_step[0], windows, scores = tied(first_step[0], windows, scores)
    first_step = list(tied(*first_step))
    compacted = call(
        compact_kernel,
        struct((experts, parts, cap, width), bf16),
        (position,),
        (windows, scores),
        "compact",
        12,
        moved=3_000_000,
    )
    compacted_rows = exchanged(compacted, "expert")
    turned = call(
        turn_kernel,
        struct((parts, kept, rows), bf16),
        (),
        (compacted_rows,),
        "turn",
        12,
        moved=3_000_000,
    )
    router_grad = call(
        router_kernel,
        struct((1, token_count), f32),
        (position,),
        (select, compacted_rows),
        "router",
        4,
        moved=300_000,
    )

    def early(name, at, pieces, sum_before):
        return call(
            functools.partial(early_kernel, steps=at, chips=chips),
            struct((kept, columns), f32),
            (position,),
            [turned] + pieces + sum_before,
            name,
            24,
            flops=4 * len(at) * rows * kept * columns,
            moved=8_000_000,
        )

    total = []
    for k in range(1, chips):
        halves = [onward(half) for half in halves] if k > 1 else first_step
        if k > 2:
            pieces = steps.pop()
            if k == 3:
                begun = early("early1", [0, 1], steps.pop(0) + steps.pop(0), [])
                halves[0], begun, router_grad = tied(halves[0], begun, router_grad)
                total = [begun]
            total = [early("early%d" % (k - 1), [k - 1], pieces, total)]
            if k == chips - 1:
                sent = swapped(halves[0])
                halves[1], total[0], sent = tied(halves[1], total[0], sent)
                steps.append(halves + [sent, swapped(halves[1])])
                break
            halves[1], total[0] = tied(halves[1], total[0])
        steps.append(halves + [swapped(half) for half in halves])
    last = steps.pop()
    flat_rows = even_size // LANES
    sum_rows = round_up(kept * lines + head_rows + 32, 8)
    edge = round_up(-(-head_rows // lines), 16)
    new_master, new_one, new_two, new_weight = pl.pallas_call(
        functools.partial(final_kernel, even_size=even_size, head_rows=head_rows, chips=chips),
        out_shape=[state, state, state, struct((per, columns), bf16)],
        in_specs=[smem()] * 2 + [vmem()] * 10,
        out_specs=[anywhere(), anywhere(), anywhere(), vmem()],
        scratch_shapes=[
            pltpu.VMEM((sum_rows, LANES), f32),
            pltpu.VMEM((sum_rows, LANES), f32),
            pltpu.VMEM((round_up(flat_rows + head_rows + 32, 8), LANES), f32),
            pltpu.VMEM((bucket_rows, LANES), f32),
            pltpu.VMEM((bucket_rows, LANES), f32),
            pltpu.VMEM((edge * lines + 2 * head_rows + 32, LANES), f32),
            pltpu.SemaphoreType.DMA((4, 3)),
        ],
        compiler_params=params(32),
        cost_estimate=cost(4 * rows * kept * columns, 25_000_000),
        name="final",
    )(
        position,
        offsets,
        turned,
        total[0],
        heads,
        *last,
        old,
        first,
        second,
    )
    return (
        new_master.reshape(1, 1, bucket_cap),
        new_one.reshape(1, 1, bucket_cap),
        new_two.reshape(1, 1, bucket_cap),
        new_weight[None],
        router_grad.reshape(token_count, 1),
    )


def solution(mesh):
    placed = (
        P(("dp", "expert"), None),
        P(("dp", "expert"), None),
        P(("dp", "expert"), None, None),
        P(("dp", "expert"), None),
        P(("dp", "expert"), None),
        P("expert", "dp", None),
        P("expert", "dp", None),
        P("expert", "dp", None),
        P("expert", "dp", None),
        P(),
    )
    return jax.shard_map(
        shards,
        mesh=mesh,
        in_specs=placed,
        out_specs=(
            P("expert", "dp", None),
            P("expert", "dp", None),
            P("expert", "dp", None),
            P("expert", "dp", None),
            P(("dp", "expert"), None),
        ),
        check_vma=False,
    )
```

```python
import functools

import jax
import jax.numpy as jnp
from jax import lax
from jax.experimental import pallas as pl
from jax.experimental.pallas import tpu as pltpu
from jax.sharding import PartitionSpec as P

beta_one = 0.9
beta_two = 0.95
learn_rate = 0.001
decay_rate = 0.1
adam_eps = 1e-08
adam_step = 20.0

LANES = 128
CHUNK = 120

f32 = jnp.float32
bf16 = jnp.bfloat16
i32 = jnp.int32


def round_up(value, unit):
    return -(-value // unit) * unit


def iota(shape, axis):
    return lax.broadcasted_iota(i32, shape, axis)


def params(mib):
    return pltpu.CompilerParams(vmem_limit_bytes=mib * 1024 * 1024)


def cost(flops, moved):
    return pl.CostEstimate(flops=int(flops), bytes_accessed=int(moved), transcendentals=0)


def pack_kernel(
    routes_ref, weight_ref, grads_any, saved_any, select_ref, target_ref, packed_any, grads, saved, packed, sems
):
    loads = [
        pltpu.make_async_copy(grads_any, grads, sems.at[0]),
        pltpu.make_async_copy(saved_any, saved, sems.at[1]),
    ]
    for load in loads:
        load.start()
    ids = routes_ref[...]
    experts, cap, _ = packed.shape
    count = ids.shape[1]
    width = grads.shape[1]
    hits = iota((round_up(experts, 8), count), 0) == ids
    before = (iota((count, count), 0) < iota((count, count), 1)).astype(bf16)
    earlier = jnp.dot(hits.astype(f32).astype(bf16), before, preferred_element_type=f32)
    slot = jnp.sum(jnp.where(hits, earlier, 0.0), axis=0, keepdims=True)
    target = ids * cap + slot.astype(i32)
    chosen = iota((experts * cap, count), 0) == target
    select = chosen.astype(f32).astype(bf16)
    select_ref[...] = chosen.astype(f32)
    target_ref[...] = target.astype(f32)
    weight = jnp.sum(jnp.where(chosen, weight_ref[...].astype(f32), 0.0), axis=1, keepdims=True)
    weight = jnp.broadcast_to(weight, (experts * cap, LANES)).astype(bf16)
    for load in loads:
        load.wait()
    picked_grads = jnp.dot(select, grads[...], preferred_element_type=f32).astype(bf16)
    picked_saved = jnp.dot(select, saved[...], preferred_element_type=f32).astype(bf16)
    stores = []
    for k in range(experts):
        span = slice(k * cap, (k + 1) * cap)
        packed[k, :, :width] = picked_grads[span]
        packed[k, :, width:-LANES] = picked_saved[span]
        packed[k, :, -LANES:] = weight[span]
        stores.append(pltpu.make_async_copy(packed.at[k], packed_any.at[k], sems.at[2 + k]))
        stores[-1].start()
    for store in stores:
        store.wait()


def window_kernel(target_ref, tokens_ref, out_ref, *, per, lead):
    parts, count, width = out_ref.shape
    diagonal = iota((count, count), 0) == iota((count, count), 1)
    column = jnp.sum(jnp.where(diagonal, target_ref[...], 0.0), axis=1, keepdims=True)
    note = jnp.broadcast_to(column, (count, width)).astype(bf16)
    lane = iota((count, width), 1)
    for j in range(parts):
        start = per * j - lead
        if start < 0:
            blank = jnp.zeros((count, -start), bf16)
            piece = jnp.concatenate([blank, tokens_ref[:, : start + width]], axis=1)
        else:
            piece = tokens_ref[:, start : start + width]
        out_ref[j] = jnp.where(lane == 0, note, piece)


def compact_kernel(position_ref, windows_ref, scores_ref, out_ref):
    parts, count, width = windows_ref.shape
    experts, _, cap, _ = out_ref.shape
    diagonal = iota((count, count), 0) == iota((count, count), 1)
    slots = iota((experts * cap, count), 0)
    for i in range(parts):
        block = windows_ref[i]
        column = block[:, 0:1].astype(f32)
        target = jnp.sum(jnp.where(diagonal, column, 0.0), axis=0, keepdims=True).astype(i32)
        select = (slots == target).astype(f32).astype(bf16)
        rows = jnp.dot(select, block, preferred_element_type=f32).astype(bf16)
        for k in range(experts):
            out_ref[k, i] = rows[k * cap : (k + 1) * cap]
    lane = iota((cap, LANES), 1)
    for k in range(experts):
        rest = scores_ref[k * cap : (k + 1) * cap, :]
        first = out_ref[k, position_ref[0], :, :LANES]
        for c in range(3):
            part = rest.astype(bf16)
            rest = rest - part.astype(f32)
            first = jnp.where(lane == 1 + c, part, first)
        out_ref[k, position_ref[0], :, :LANES] = first


def turn_kernel(rows_ref, out_ref):
    experts, parts, _, width = rows_ref.shape
    kept = out_ref.shape[1]
    for i in range(parts):
        slab = jnp.concatenate([rows_ref[k, i] for k in range(experts)], axis=0)
        out_ref[i] = slab.T[width - kept :, :]


def factor_kernel(arrived_ref, grads_ref, gate_ref, up_ref, score_ref):
    width, hidden = grads_ref.shape[1], gate_ref.shape[1]
    grads_ref[...] = arrived_ref[:, :width]
    gate = arrived_ref[:, width : width + hidden].astype(f32)
    up = arrived_ref[:, width + hidden : width + 2 * hidden].astype(f32)
    weight = arrived_ref[:, width + 2 * hidden :].astype(f32)[:, 0:1]
    sig = jax.nn.sigmoid(gate)
    act = gate * sig
    score_ref[...] = act * up
    up_ref[...] = weight * act
    gate_ref[...] = weight * (up * sig * (1.0 + gate * (1.0 - sig)))


def row_kernel(position_ref, grads_ref, gate_factor, up_factor, score_factor, *refs, chips):
    down_refs, refs = refs[:-9], refs[-8:]
    gate_any, up_any, joined_ref, scores_ref, gate_half, up_half, down, sems = refs
    hidden = down.shape[0]
    loads = []
    for n, down_ref in enumerate(down_refs):
        size = down_ref.shape[0]
        if size == hidden:
            at = 0
        else:
            slab = lax.rem(position_ref[0] + 2 * (chips - n // 2), 2 * chips) ^ (n % 2)
            at = pl.multiple_of(slab * size, 16)
        loads.append(pltpu.make_async_copy(down_ref, down.at[pl.ds(at, size)], sems.at[n]))
    for load in loads:
        load.start()
    for load in loads:
        load.wait()
    scores = None
    step = 2 * LANES
    stores = []
    for at in range(0, hidden, step):
        span = slice(at, at + step)
        back = lax.dot_general(
            grads_ref[...], down[span, :], (((1,), (1,)), ((), ())), preferred_element_type=f32
        )
        part = jnp.sum(score_factor[:, span] * back, axis=1, keepdims=True)
        scores = part if scores is None else scores + part
        gate = (gate_factor[:, span] * back).astype(bf16)
        up = (up_factor[:, span] * back).astype(bf16)
        gate_half[:, span] = gate
        up_half[:, span] = up
        joined_ref[:, span] = gate
        joined_ref[:, hidden + at : hidden + at + step] = up
        for half, (source, target) in enumerate(((gate_half, gate_any), (up_half, up_any))):
            sem = sems.at[len(down_refs) + 2 * (at // step) + half]
            stores.append(pltpu.make_async_copy(source.at[:, span], target.at[:, span], sem))
            stores[-1].start()
    scores_ref[...] = jnp.broadcast_to(scores, scores_ref.shape)
    for store in stores:
        store.wait()


def router_kernel(position_ref, select_ref, rows_ref, out_ref):
    experts = rows_ref.shape[0]
    own = [rows_ref[k, position_ref[0], :, :LANES] for k in range(experts)]
    parts = jnp.concatenate(own, axis=0).astype(f32)
    scores = (parts[:, 1:2] + parts[:, 2:3]) + parts[:, 3:4]
    out_ref[...] = jnp.sum(jnp.where(select_ref[...] > 0.5, scores, 0.0), axis=0, keepdims=True)


def head_kernel(master_ref, first_ref, second_ref, out_ref):
    for n, source in enumerate((master_ref, first_ref, second_ref)):
        out_ref[n] = source[...]


def ready_kernel(*refs):
    refs[-1][...] = jnp.zeros(refs[-1].shape, f32)


def slab_sum(total, turned_ref, slabs, joined):
    for slab, (ref, at, step) in zip(slabs, joined):
        piece = jnp.dot(turned_ref[slab], ref[:, at : at + step], preferred_element_type=f32)
        piece = piece.astype(bf16).astype(f32)
        total = piece if total is None else total + piece
    return total


def slabs_of(position, steps, chips):
    own = [lax.rem(position + 2 * (chips - k), 2 * chips) for k in steps]
    return [slab ^ other for slab in own for other in (0, 1)]


def early_kernel(position_ref, turned_ref, *refs, steps, chips):
    refs, sum_ref = list(refs[:-1]), refs[-1]
    hidden = sum_ref.shape[1] // 2
    step = 2 * LANES
    slabs = slabs_of(position_ref[0], steps, chips)
    lists = ([], [])
    for k in steps:
        for other in range(2):
            whole = refs.pop(0) if k == 0 else None
            for half in range(2):
                lists[half].append((whole, half * hidden) if k == 0 else (refs.pop(0), 0))
    base = refs[0] if refs else None
    for half in range(2):
        for at in range(0, hidden, step):
            span = slice(half * hidden + at, half * hidden + at + step)
            joined = [(ref, first + at, step) for ref, first in lists[half]]
            total = None if base is None else base[:, span]
            sum_ref[:, span] = slab_sum(total, turned_ref, slabs, joined)


def adam(grad, old, first, second):
    first_new = beta_one * first + (1.0 - beta_one) * grad
    second_new = beta_two * second + (1.0 - beta_two) * grad * grad
    below = jnp.sqrt(second_new * (1.0 / (1.0 - beta_two**adam_step))) + adam_eps
    update = first_new * (learn_rate / (1.0 - beta_one**adam_step)) / below
    return old * (1.0 - learn_rate * decay_rate) - update, first_new, second_new


def final_kernel(
    position_ref,
    offsets_ref,
    turned_ref,
    early_ref,
    heads_ref,
    gate_own,
    up_own,
    gate_other,
    up_other,
    old,
    first,
    second,
    out_master,
    out_first,
    out_second,
    weight_ref,
    sums,
    moved,
    new_old,
    new_first,
    new_second,
    head_new,
    sems,
    *,
    even_size,
    head_rows,
    chips,
):
    kept, columns = early_ref.shape
    hidden = columns // 2
    per = weight_ref.shape[0]
    lines = columns // LANES
    before = (kept - per) * lines
    bucket_rows = old.shape[0]
    flat_rows = even_size // LANES
    position = position_ref[0]
    start = offsets_ref[position]
    finish = offsets_ref[position + 1]
    shift = position * even_size - start
    next_shift = (position + 1) * even_size - finish
    length = finish - start
    whole, part = shift // LANES, shift % LANES
    odd = whole % 8
    next_whole, next_part = next_shift // LANES, next_shift % LANES

    step = 2 * LANES
    slabs = slabs_of(position, [chips - 1], chips)
    for half, refs in enumerate(((gate_own, gate_other), (up_own, up_other))):
        for at in range(0, hidden, step):
            begin = half * hidden + at
            total = slab_sum(
                early_ref[:, begin : begin + step], turned_ref, slabs, [(ref, at, step) for ref in refs]
            )
            for c in range(step // LANES):
                block = total[:, c * LANES : (c + 1) * LANES]
                line = begin // LANES + c
                block = pltpu.roll(block, part, 1)
                sums[pl.ds(odd + line, kept, stride=lines), :] = block
                moved[pl.ds(odd + line + 1, kept, stride=lines), :] = block

    def slots_of(row, count):
        at = pl.multiple_of(row + before - (whole - odd), 8)
        lane = iota((count, LANES), 1)
        return jnp.where(lane >= part, sums[pl.ds(at, count), :], moved[pl.ds(at, count), :])

    def update(row, count):
        span = pl.ds(row, count)
        a, b, c = adam(slots_of(row, count), old[span, :], first[span, :], second[span, :])
        new_old[span, :], new_first[span, :], new_second[span, :] = a, b, c

    def masked(row, count):
        span = pl.ds(row, count)
        inside = (row + iota((count, LANES), 0)) * LANES + iota((count, LANES), 1) < length
        grad = jnp.where(inside, slots_of(row, count), 0.0)
        a, b, c = adam(grad, old[span, :], first[span, :], second[span, :])
        new_old[span, :] = jnp.where(inside, a, 0.0)
        new_first[span, :] = jnp.where(inside, b, 0.0)
        new_second[span, :] = jnp.where(inside, c, 0.0)

    def send(begin, count, slot):
        span = pl.ds(begin, count)
        stores = [
            pltpu.make_async_copy(source.at[span], target.at[span], sems.at[slot, n])
            for n, (source, target) in enumerate(
                ((new_old, out_master), (new_first, out_first), (new_second, out_second))
            )
        ]
        for store in stores:
            store.start()
        return stores

    def chunk(n, carry):
        update(pl.multiple_of(n * CHUNK, 8), CHUNK)
        return carry

    safe = (flat_rows - head_rows) // CHUNK
    third = -(-safe // 3)
    stores = []
    for slot, begin in enumerate(range(0, safe, third)):
        end = min(begin + third, safe)
        lax.fori_loop(begin, end, chunk, 0)
        stores += send(begin * CHUNK, (end - begin) * CHUNK, slot)
    for row in range(safe * CHUNK, bucket_rows, CHUNK):
        masked(row, min(CHUNK, bucket_rows - row))
    stores += send(safe * CHUNK, bucket_rows - safe * CHUNK, 3)

    def next_slots():
        lane = iota((head_rows, LANES), 1)
        base = flat_rows + before - next_whole + odd
        here = pltpu.roll(sums[pl.ds(base, head_rows), :], (LANES - part) % LANES, 1)
        above = pltpu.roll(sums[pl.ds(base - 1, head_rows), :], (LANES - part) % LANES, 1)
        return pltpu.roll(jnp.where(lane < LANES - next_part, here, above), next_part, 1)

    edge = round_up(-(-head_rows // lines), 16)
    head_new[pl.ds(edge * lines, head_rows), :] = adam(next_slots(), heads_ref[0], heads_ref[1], heads_ref[2])[0]

    flat_row = iota((edge, LANES), 0) + (per - edge)
    for c in range(lines):
        lane = iota((per, LANES), 1)
        here = new_old[pl.ds(c + whole, per, stride=lines), :]
        below = new_old[pl.ds(c + whole + 1, per, stride=lines), :]
        own = pltpu.roll(jnp.where(lane >= part, here, below), (LANES - part) % LANES, 1)
        base = c + next_whole
        lane = iota((edge, LANES), 1)
        here = head_new[pl.ds(base, edge, stride=lines), :]
        below = head_new[pl.ds(base + 1, edge, stride=lines), :]
        other = pltpu.roll(jnp.where(lane >= next_part, here, below), (LANES - next_part) % LANES, 1)
        flat = (flat_row * lines + c) * LANES + lane
        last = jnp.where(flat < even_size - next_shift, own[per - edge :], other)
        out = slice(c * LANES, (c + 1) * LANES)
        if per > edge:
            weight_ref[: per - edge, out] = own[: per - edge].astype(bf16)
        weight_ref[per - edge :, out] = last.astype(bf16)

    for store in stores:
        store.wait()


def vmem():
    return pl.BlockSpec(memory_space=pltpu.VMEM)


def anywhere():
    return pl.BlockSpec(memory_space=pl.ANY)


def hbm():
    return pl.BlockSpec(memory_space=pltpu.HBM)


def smem():
    return pl.BlockSpec(memory_space=pltpu.SMEM)


def call(kernel, outs, scalars, args, name, mib, flops=0, moved=0):
    many = isinstance(outs, (list, tuple))
    return pl.pallas_call(
        kernel,
        out_shape=outs,
        in_specs=[smem()] * len(scalars) + [vmem()] * len(args),
        out_specs=[vmem()] * len(outs) if many else vmem(),
        compiler_params=params(mib),
        cost_estimate=cost(flops, moved),
        name=name,
    )(*scalars, *args)


def struct(shape, kind):
    return jax.ShapeDtypeStruct(shape, kind)


def shards(
    tokens,
    out_grad,
    gate_up,
    route_weight,
    routes,
    down_weight,
    master,
    moment_one,
    moment_two,
    offsets,
):
    token_count, model_width = tokens.shape
    columns = gate_up.shape[2]
    hidden = columns // 2
    bucket_cap = master.shape[2]
    groups = lax.axis_size("expert")
    parts = lax.axis_size("dp")
    experts = groups * master.shape[0]
    cap = 2 * token_count // experts
    rows = experts * cap
    per = model_width // parts
    even_size = per * columns
    margin = bucket_cap - even_size
    extra = round_up(-(-margin // columns), 16)
    width = round_up(per + extra + 4, LANES)
    kept = per + extra
    lines = columns // LANES
    bucket_rows = bucket_cap // LANES
    head_rows = round_up(margin // LANES, 8)

    chips = parts // 2
    position = lax.axis_index("dp").astype(i32).reshape(1)
    state = struct((bucket_rows, LANES), f32)
    old, first, second = (array.reshape(bucket_rows, LANES) for array in (master, moment_one, moment_two))

    def onward(block):
        return lax.ppermute(block, "dp", [(i, (i + 2) % parts) for i in range(parts)])

    def swapped(block):
        return lax.ppermute(block, "dp", [(i, i ^ 1) for i in range(parts)])

    def exchanged(block, axis):
        return lax.all_to_all(block, axis, split_axis=0, concat_axis=0, tiled=True)

    def tied(*values):
        return lax.optimization_barrier(values)

    wide = model_width + columns + LANES
    select, target, packed = pl.pallas_call(
        pack_kernel,
        out_shape=[
            struct((rows, token_count), f32),
            struct((1, token_count), f32),
            struct((experts, cap, wide), bf16),
        ],
        in_specs=[vmem(), vmem(), hbm(), hbm()],
        out_specs=[vmem(), vmem(), hbm()],
        scratch_shapes=[
            pltpu.VMEM((token_count, model_width), bf16),
            pltpu.VMEM((token_count, columns), bf16),
            pltpu.VMEM((experts, cap, wide), bf16),
            pltpu.SemaphoreType.DMA((2 + experts,)),
        ],
        compiler_params=params(16),
        cost_estimate=cost(0, 6_000_000),
        name="pack",
    )(
        routes.reshape(1, token_count),
        route_weight.reshape(1, token_count),
        out_grad,
        gate_up.reshape(token_count, columns),
    )
    windows = call(
        functools.partial(window_kernel, per=per, lead=width - per),
        struct((parts, token_count, width), bf16),
        (),
        (target, tokens),
        "window",
        12,
        moved=2_000_000,
    )
    if down_weight.shape[1] % 16 == 0:
        held, other = [down_weight[0]], [swapped(down_weight[0])]
        for k in range(1, chips):
            arrival = onward(held[-1])
            if k > 1:
                arrival, other = tied(arrival, other)
            held.append(arrival)
            other.append(swapped(arrival))
            if k == chips - 2:
                windows, other[-1] = tied(windows, other[-1])
        down = [piece for pair in zip(held, other) for piece in pair]
    else:
        down = [lax.all_gather(down_weight, "dp", axis=1, tiled=True)[0]]
        windows, down[0] = tied(windows, down[0])
    arrived = exchanged(packed, "expert").reshape(rows, wide)
    windows = exchanged(windows, "dp")
    factors = call(
        factor_kernel,
        [struct((rows, model_width), bf16)] + [struct((rows, hidden), f32)] * 3,
        (),
        (arrived,),
        "factors",
        20,
        moved=6_000_000,
    )
    ready = pl.pallas_call(
        ready_kernel,
        out_shape=struct((8, LANES), f32),
        in_specs=[anywhere()],
        out_specs=vmem(),
        compiler_params=params(4),
        cost_estimate=cost(0, 18_000_000),
        name="ready",
    )(down[-1])
    gate, up, joined, scores = pl.pallas_call(
        functools.partial(row_kernel, chips=chips),
        out_shape=[struct((rows, hidden), bf16)] * 2
        + [struct((rows, columns), bf16), struct((rows, LANES), f32)],
        in_specs=[smem()] + [vmem()] * 4 + [anywhere()] * (len(down) + 1),
        out_specs=[hbm(), hbm(), vmem(), vmem()],
        scratch_shapes=[
            pltpu.VMEM((rows, hidden), bf16),
            pltpu.VMEM((rows, hidden), bf16),
            pltpu.VMEM((hidden, model_width), bf16),
            pltpu.SemaphoreType.DMA((len(down) + 2 * (hidden // (2 * LANES)),)),
        ],
        compiler_params=params(24),
        cost_estimate=cost(2 * rows * model_width * hidden, 8_000_000),
        name="rows",
    )(position, *factors, *down, ready)

    halves = [gate, up]
    steps = [[joined, swapped(joined)]]
    first_step = [onward(half) for half in halves]
    first_step[1], windows, scores, _ = tied(first_step[1], windows, scores, first_step[0])
    heads = pl.pallas_call(
        head_kernel,
        grid=(1,),
        out_shape=struct((3, head_rows, LANES), f32),
        in_specs=[pl.BlockSpec((head_rows, LANES), lambda i: (0, 0))] * 3,
        out_specs=pl.BlockSpec((3, head_rows, LANES), lambda i: (0, 0, 0)),
        cost_estimate=cost(0, 400_000),
        name="heads",
    )(old, first, second)
    heads, _ = tied(heads, first_step[1])
    heads = lax.ppermute(heads, "dp", [(i + 1, i) for i in range(parts - 1)])
    compacted = call(
        compact_kernel,
        struct((experts, parts, cap, width), bf16),
        (position,),
        (windows, scores),
        "compact",
        12,
        moved=3_000_000,
    )
    compacted_rows = exchanged(compacted, "expert")
    turned = call(
        turn_kernel,
        struct((parts, kept, rows), bf16),
        (),
        (compacted_rows,),
        "turn",
        12,
        moved=3_000_000,
    )
    router_grad = call(
        router_kernel,
        struct((1, token_count), f32),
        (position,),
        (select, compacted_rows),
        "router",
        4,
        moved=300_000,
    )

    def early(name, at, pieces, sum_before):
        return call(
            functools.partial(early_kernel, steps=at, chips=chips),
            struct((kept, columns), f32),
            (position,),
            [turned] + pieces + sum_before,
            name,
            24,
            flops=4 * len(at) * rows * kept * columns,
            moved=8_000_000,
        )

    total = []
    for k in range(1, chips):
        halves = [onward(half) for half in halves] if k > 1 else first_step
        if k > 2:
            pieces = steps.pop()
            if k == 3:
                begun = early("early1", [0, 1], steps.pop(0) + steps.pop(0), [])
                halves[0], begun, router_grad, heads = tied(halves[0], begun, router_grad, heads)
                total = [begun]
            total = [early("early%d" % (k - 1), [k - 1], pieces, total)]
            if k == chips - 1:
                sent = swapped(halves[0])
                halves[1], total[0], sent = tied(halves[1], total[0], sent)
                steps.append(halves + [sent, swapped(halves[1])])
                break
            halves[1], total[0] = tied(halves[1], total[0])
        steps.append(halves + [swapped(half) for half in halves])
    last = steps.pop()
    flat_rows = even_size // LANES
    sum_rows = round_up(kept * lines + head_rows + 32, 8)
    edge = round_up(-(-head_rows // lines), 16)
    new_master, new_one, new_two, new_weight = pl.pallas_call(
        functools.partial(final_kernel, even_size=even_size, head_rows=head_rows, chips=chips),
        out_shape=[state, state, state, struct((per, columns), bf16)],
        in_specs=[smem()] * 2 + [vmem()] * 10,
        out_specs=[anywhere(), anywhere(), anywhere(), vmem()],
        scratch_shapes=[
            pltpu.VMEM((sum_rows, LANES), f32),
            pltpu.VMEM((sum_rows, LANES), f32),
            pltpu.VMEM((round_up(flat_rows + head_rows + 32, 8), LANES), f32),
            pltpu.VMEM((bucket_rows, LANES), f32),
            pltpu.VMEM((bucket_rows, LANES), f32),
            pltpu.VMEM((edge * lines + 2 * head_rows + 32, LANES), f32),
            pltpu.SemaphoreType.DMA((4, 3)),
        ],
        compiler_params=params(32),
        cost_estimate=cost(4 * rows * kept * columns, 25_000_000),
        name="final",
    )(
        position,
        offsets,
        turned,
        total[0],
        heads,
        *last,
        old,
        first,
        second,
    )
    return (
        new_master.reshape(1, 1, bucket_cap),
        new_one.reshape(1, 1, bucket_cap),
        new_two.reshape(1, 1, bucket_cap),
        new_weight[None],
        router_grad.reshape(token_count, 1),
    )


def solution(mesh):
    placed = (
        P(("dp", "expert"), None),
        P(("dp", "expert"), None),
        P(("dp", "expert"), None, None),
        P(("dp", "expert"), None),
        P(("dp", "expert"), None),
        P("expert", "dp", None),
        P("expert", "dp", None),
        P("expert", "dp", None),
        P("expert", "dp", None),
        P(),
    )
    return jax.shard_map(
        shards,
        mesh=mesh,
        in_specs=placed,
        out_specs=(
            P("expert", "dp", None),
            P("expert", "dp", None),
            P("expert", "dp", None),
            P("expert", "dp", None),
            P(("dp", "expert"), None),
        ),
        check_vma=False,
    )
```

```python
import functools

import jax
import jax.numpy as jnp
from jax import lax
from jax.experimental import pallas as pl
from jax.experimental.pallas import tpu as pltpu
from jax.sharding import PartitionSpec as P

beta_one = 0.9
beta_two = 0.95
learn_rate = 0.001
decay_rate = 0.1
adam_eps = 1e-08
adam_step = 20.0

LANES = 128
CHUNK = 120

f32 = jnp.float32
bf16 = jnp.bfloat16
i32 = jnp.int32


def round_up(value, unit):
    return -(-value // unit) * unit


def iota(shape, axis):
    return lax.broadcasted_iota(i32, shape, axis)


def params(mib):
    return pltpu.CompilerParams(vmem_limit_bytes=mib * 1024 * 1024)


def cost(flops, moved):
    return pl.CostEstimate(flops=int(flops), bytes_accessed=int(moved), transcendentals=0)


def pack_kernel(
    routes_ref, weight_ref, grads_any, saved_any, select_ref, target_ref, packed_any, grads, saved, packed, sems
):
    loads = [
        pltpu.make_async_copy(grads_any, grads, sems.at[0]),
        pltpu.make_async_copy(saved_any, saved, sems.at[1]),
    ]
    for load in loads:
        load.start()
    ids = routes_ref[...]
    experts, cap, _ = packed.shape
    count = ids.shape[1]
    width = grads.shape[1]
    hits = iota((round_up(experts, 8), count), 0) == ids
    before = (iota((count, count), 0) < iota((count, count), 1)).astype(bf16)
    earlier = jnp.dot(hits.astype(f32).astype(bf16), before, preferred_element_type=f32)
    slot = jnp.sum(jnp.where(hits, earlier, 0.0), axis=0, keepdims=True)
    target = ids * cap + slot.astype(i32)
    chosen = iota((experts * cap, count), 0) == target
    select = chosen.astype(f32).astype(bf16)
    select_ref[...] = chosen.astype(f32)
    target_ref[...] = target.astype(f32)
    weight = jnp.sum(jnp.where(chosen, weight_ref[...].astype(f32), 0.0), axis=1, keepdims=True)
    weight = jnp.broadcast_to(weight, (experts * cap, LANES)).astype(bf16)
    for load in loads:
        load.wait()
    picked_grads = jnp.dot(select, grads[...], preferred_element_type=f32).astype(bf16)
    picked_saved = jnp.dot(select, saved[...], preferred_element_type=f32).astype(bf16)
    stores = []
    for k in range(experts):
        span = slice(k * cap, (k + 1) * cap)
        packed[k, :, :width] = picked_grads[span]
        packed[k, :, width:-LANES] = picked_saved[span]
        packed[k, :, -LANES:] = weight[span]
        stores.append(pltpu.make_async_copy(packed.at[k], packed_any.at[k], sems.at[2 + k]))
        stores[-1].start()
    for store in stores:
        store.wait()


def window_kernel(target_ref, tokens_ref, out_ref, *, per, lead):
    parts, count, width = out_ref.shape
    diagonal = iota((count, count), 0) == iota((count, count), 1)
    column = jnp.sum(jnp.where(diagonal, target_ref[...], 0.0), axis=1, keepdims=True)
    note = jnp.broadcast_to(column, (count, width)).astype(bf16)
    lane = iota((count, width), 1)
    for j in range(parts):
        start = per * j - lead
        if start < 0:
            blank = jnp.zeros((count, -start), bf16)
            piece = jnp.concatenate([blank, tokens_ref[:, : start + width]], axis=1)
        else:
            piece = tokens_ref[:, start : start + width]
        out_ref[j] = jnp.where(lane == 0, note, piece)


def compact_kernel(position_ref, windows_ref, scores_ref, out_ref):
    parts, count, width = windows_ref.shape
    experts, _, cap, _ = out_ref.shape
    diagonal = iota((count, count), 0) == iota((count, count), 1)
    slots = iota((experts * cap, count), 0)
    for i in range(parts):
        block = windows_ref[i]
        column = block[:, 0:1].astype(f32)
        target = jnp.sum(jnp.where(diagonal, column, 0.0), axis=0, keepdims=True).astype(i32)
        select = (slots == target).astype(f32).astype(bf16)
        rows = jnp.dot(select, block, preferred_element_type=f32).astype(bf16)
        for k in range(experts):
            out_ref[k, i] = rows[k * cap : (k + 1) * cap]
    lane = iota((cap, LANES), 1)
    for k in range(experts):
        rest = scores_ref[k * cap : (k + 1) * cap, :]
        first = out_ref[k, position_ref[0], :, :LANES]
        for c in range(3):
            part = rest.astype(bf16)
            rest = rest - part.astype(f32)
            first = jnp.where(lane == 1 + c, part, first)
        out_ref[k, position_ref[0], :, :LANES] = first


def turn_kernel(rows_ref, out_ref):
    experts, parts, _, width = rows_ref.shape
    kept = out_ref.shape[1]
    for i in range(parts):
        slab = jnp.concatenate([rows_ref[k, i] for k in range(experts)], axis=0)
        out_ref[i] = slab.T[width - kept :, :]


def factor_kernel(arrived_ref, grads_ref, gate_ref, up_ref, score_ref):
    width, hidden = grads_ref.shape[1], gate_ref.shape[1]
    grads_ref[...] = arrived_ref[:, :width]
    gate = arrived_ref[:, width : width + hidden].astype(f32)
    up = arrived_ref[:, width + hidden : width + 2 * hidden].astype(f32)
    weight = arrived_ref[:, width + 2 * hidden :].astype(f32)[:, 0:1]
    sig = jax.nn.sigmoid(gate)
    act = gate * sig
    score_ref[...] = act * up
    up_ref[...] = weight * act
    gate_ref[...] = weight * (up * sig * (1.0 + gate * (1.0 - sig)))


def row_kernel(position_ref, grads_ref, gate_factor, up_factor, score_factor, *refs, chips):
    down_refs, refs = refs[:-6], refs[-5:]
    joined_any, scores_ref, joined, down, sems = refs
    hidden = down.shape[0]
    loads = []
    for n, down_ref in enumerate(down_refs):
        size = down_ref.shape[0]
        if size == hidden:
            at = 0
        else:
            slab = lax.rem(position_ref[0] + 2 * (chips - n // 2), 2 * chips) ^ (n % 2)
            at = pl.multiple_of(slab * size, 16)
        loads.append(pltpu.make_async_copy(down_ref, down.at[pl.ds(at, size)], sems.at[n]))
    for load in loads:
        load.start()
    for load in loads:
        load.wait()
    scores = None
    step = 2 * LANES
    stores = []
    for at in range(0, hidden, step):
        span = slice(at, at + step)
        back = lax.dot_general(
            grads_ref[...], down[span, :], (((1,), (1,)), ((), ())), preferred_element_type=f32
        )
        part = jnp.sum(score_factor[:, span] * back, axis=1, keepdims=True)
        scores = part if scores is None else scores + part
        for half, factor in enumerate((gate_factor, up_factor)):
            out = slice(half * hidden + at, half * hidden + at + step)
            joined[:, out] = (factor[:, span] * back).astype(bf16)
            sem = sems.at[len(down_refs) + 2 * (at // step) + half]
            stores.append(pltpu.make_async_copy(joined.at[:, out], joined_any.at[:, out], sem))
            stores[-1].start()
    scores_ref[...] = jnp.broadcast_to(scores, scores_ref.shape)
    for store in stores:
        store.wait()


def router_kernel(position_ref, select_ref, rows_ref, out_ref):
    experts = rows_ref.shape[0]
    own = [rows_ref[k, position_ref[0], :, :LANES] for k in range(experts)]
    parts = jnp.concatenate(own, axis=0).astype(f32)
    scores = (parts[:, 1:2] + parts[:, 2:3]) + parts[:, 3:4]
    out_ref[...] = jnp.sum(jnp.where(select_ref[...] > 0.5, scores, 0.0), axis=0, keepdims=True)


def head_kernel(master_ref, first_ref, second_ref, out_ref):
    for n, source in enumerate((master_ref, first_ref, second_ref)):
        out_ref[n] = source[...]


def ready_kernel(*refs):
    refs[-1][...] = jnp.zeros(refs[-1].shape, f32)


def slab_sum(total, turned_ref, slabs, joined_refs, span):
    for slab, ref in zip(slabs, joined_refs):
        piece = jnp.dot(turned_ref[slab], ref[:, span], preferred_element_type=f32)
        piece = piece.astype(bf16).astype(f32)
        total = piece if total is None else total + piece
    return total


def slabs_of(position, steps, chips):
    own = [lax.rem(position + 2 * (chips - k), 2 * chips) for k in steps]
    return [slab ^ other for slab in own for other in (0, 1)]


def early_kernel(position_ref, turned_ref, *refs, steps, chips):
    joined_refs, base, sum_ref = refs[: 2 * len(steps)], refs[2 * len(steps) : -1], refs[-1]
    step = 2 * LANES
    slabs = slabs_of(position_ref[0], steps, chips)
    for at in range(0, sum_ref.shape[1], step):
        span = slice(at, at + step)
        total = base[0][:, span] if base else None
        sum_ref[:, span] = slab_sum(total, turned_ref, slabs, joined_refs, span)


def adam(grad, old, first, second):
    first_new = beta_one * first + (1.0 - beta_one) * grad
    second_new = beta_two * second + (1.0 - beta_two) * grad * grad
    below = jnp.sqrt(second_new * (1.0 / (1.0 - beta_two**adam_step))) + adam_eps
    update = first_new * (learn_rate / (1.0 - beta_one**adam_step)) / below
    return old * (1.0 - learn_rate * decay_rate) - update, first_new, second_new


def final_kernel(
    position_ref,
    offsets_ref,
    turned_ref,
    early_ref,
    heads_ref,
    own_ref,
    other_ref,
    old,
    first,
    second,
    out_master,
    out_first,
    out_second,
    weight_ref,
    sums,
    moved,
    new_old,
    new_first,
    new_second,
    head_new,
    sems,
    *,
    even_size,
    head_rows,
    chips,
):
    kept, columns = early_ref.shape
    per = weight_ref.shape[0]
    lines = columns // LANES
    before = (kept - per) * lines
    bucket_rows = old.shape[0]
    flat_rows = even_size // LANES
    position = position_ref[0]
    start = offsets_ref[position]
    finish = offsets_ref[position + 1]
    shift = position * even_size - start
    next_shift = (position + 1) * even_size - finish
    length = finish - start
    whole, part = shift // LANES, shift % LANES
    odd = whole % 8
    next_whole, next_part = next_shift // LANES, next_shift % LANES

    step = 2 * LANES
    slabs = slabs_of(position, [chips - 1], chips)
    for begin in range(0, columns, step):
        span = slice(begin, begin + step)
        total = slab_sum(early_ref[:, span], turned_ref, slabs, (own_ref, other_ref), span)
        for c in range(step // LANES):
            block = pltpu.roll(total[:, c * LANES : (c + 1) * LANES], part, 1)
            line = begin // LANES + c
            sums[pl.ds(odd + line, kept, stride=lines), :] = block
            moved[pl.ds(odd + line + 1, kept, stride=lines), :] = block

    def slots_of(row, count):
        at = pl.multiple_of(row + before - (whole - odd), 8)
        lane = iota((count, LANES), 1)
        return jnp.where(lane >= part, sums[pl.ds(at, count), :], moved[pl.ds(at, count), :])

    def update(row, count):
        span = pl.ds(row, count)
        a, b, c = adam(slots_of(row, count), old[span, :], first[span, :], second[span, :])
        new_old[span, :], new_first[span, :], new_second[span, :] = a, b, c

    def masked(row, count):
        span = pl.ds(row, count)
        inside = (row + iota((count, LANES), 0)) * LANES + iota((count, LANES), 1) < length
        grad = jnp.where(inside, slots_of(row, count), 0.0)
        a, b, c = adam(grad, old[span, :], first[span, :], second[span, :])
        new_old[span, :] = jnp.where(inside, a, 0.0)
        new_first[span, :] = jnp.where(inside, b, 0.0)
        new_second[span, :] = jnp.where(inside, c, 0.0)

    def send(begin, count, slot):
        span = pl.ds(begin, count)
        stores = [
            pltpu.make_async_copy(source.at[span], target.at[span], sems.at[slot, n])
            for n, (source, target) in enumerate(
                ((new_old, out_master), (new_first, out_first), (new_second, out_second))
            )
        ]
        for store in stores:
            store.start()
        return stores

    def chunk(n, carry):
        update(pl.multiple_of(n * CHUNK, 8), CHUNK)
        return carry

    safe = (flat_rows - head_rows) // CHUNK
    third = -(-safe // 3)
    stores = []
    for slot, begin in enumerate(range(0, safe, third)):
        end = min(begin + third, safe)
        lax.fori_loop(begin, end, chunk, 0)
        stores += send(begin * CHUNK, (end - begin) * CHUNK, slot)
    for row in range(safe * CHUNK, bucket_rows, CHUNK):
        masked(row, min(CHUNK, bucket_rows - row))
    stores += send(safe * CHUNK, bucket_rows - safe * CHUNK, 3)

    def next_slots():
        lane = iota((head_rows, LANES), 1)
        base = flat_rows + before - next_whole + odd
        here = pltpu.roll(sums[pl.ds(base, head_rows), :], (LANES - part) % LANES, 1)
        above = pltpu.roll(sums[pl.ds(base - 1, head_rows), :], (LANES - part) % LANES, 1)
        return pltpu.roll(jnp.where(lane < LANES - next_part, here, above), next_part, 1)

    edge = round_up(-(-head_rows // lines), 16)
    head_new[pl.ds(edge * lines, head_rows), :] = adam(next_slots(), heads_ref[0], heads_ref[1], heads_ref[2])[0]

    flat_row = iota((edge, LANES), 0) + (per - edge)
    for c in range(lines):
        lane = iota((per, LANES), 1)
        here = new_old[pl.ds(c + whole, per, stride=lines), :]
        below = new_old[pl.ds(c + whole + 1, per, stride=lines), :]
        own = pltpu.roll(jnp.where(lane >= part, here, below), (LANES - part) % LANES, 1)
        base = c + next_whole
        lane = iota((edge, LANES), 1)
        here = head_new[pl.ds(base, edge, stride=lines), :]
        below = head_new[pl.ds(base + 1, edge, stride=lines), :]
        other = pltpu.roll(jnp.where(lane >= next_part, here, below), (LANES - next_part) % LANES, 1)
        flat = (flat_row * lines + c) * LANES + lane
        last = jnp.where(flat < even_size - next_shift, own[per - edge :], other)
        out = slice(c * LANES, (c + 1) * LANES)
        if per > edge:
            weight_ref[: per - edge, out] = own[: per - edge].astype(bf16)
        weight_ref[per - edge :, out] = last.astype(bf16)

    for store in stores:
        store.wait()


def vmem():
    return pl.BlockSpec(memory_space=pltpu.VMEM)


def anywhere():
    return pl.BlockSpec(memory_space=pl.ANY)


def hbm():
    return pl.BlockSpec(memory_space=pltpu.HBM)


def smem():
    return pl.BlockSpec(memory_space=pltpu.SMEM)


def call(kernel, outs, scalars, args, name, mib, flops=0, moved=0):
    many = isinstance(outs, (list, tuple))
    return pl.pallas_call(
        kernel,
        out_shape=outs,
        in_specs=[smem()] * len(scalars) + [vmem()] * len(args),
        out_specs=[vmem()] * len(outs) if many else vmem(),
        compiler_params=params(mib),
        cost_estimate=cost(flops, moved),
        name=name,
    )(*scalars, *args)


def struct(shape, kind):
    return jax.ShapeDtypeStruct(shape, kind)


def shards(
    tokens,
    out_grad,
    gate_up,
    route_weight,
    routes,
    down_weight,
    master,
    moment_one,
    moment_two,
    offsets,
):
    token_count, model_width = tokens.shape
    columns = gate_up.shape[2]
    hidden = columns // 2
    bucket_cap = master.shape[2]
    groups = lax.axis_size("expert")
    parts = lax.axis_size("dp")
    experts = groups * master.shape[0]
    cap = 2 * token_count // experts
    rows = experts * cap
    per = model_width // parts
    even_size = per * columns
    margin = bucket_cap - even_size
    extra = round_up(-(-margin // columns), 16)
    width = round_up(per + extra + 4, LANES)
    kept = per + extra
    lines = columns // LANES
    bucket_rows = bucket_cap // LANES
    head_rows = round_up(margin // LANES, 8)

    chips = parts // 2
    position = lax.axis_index("dp").astype(i32).reshape(1)
    state = struct((bucket_rows, LANES), f32)
    old, first, second = (array.reshape(bucket_rows, LANES) for array in (master, moment_one, moment_two))

    def onward(block):
        return lax.ppermute(block, "dp", [(i, (i + 2) % parts) for i in range(parts)])

    def swapped(block):
        return lax.ppermute(block, "dp", [(i, i ^ 1) for i in range(parts)])

    def exchanged(block, axis):
        return lax.all_to_all(block, axis, split_axis=0, concat_axis=0, tiled=True)

    def tied(*values):
        return lax.optimization_barrier(values)

    wide = model_width + columns + LANES
    select, target, packed = pl.pallas_call(
        pack_kernel,
        out_shape=[
            struct((rows, token_count), f32),
            struct((1, token_count), f32),
            struct((experts, cap, wide), bf16),
        ],
        in_specs=[vmem(), vmem(), hbm(), hbm()],
        out_specs=[vmem(), vmem(), hbm()],
        scratch_shapes=[
            pltpu.VMEM((token_count, model_width), bf16),
            pltpu.VMEM((token_count, columns), bf16),
            pltpu.VMEM((experts, cap, wide), bf16),
            pltpu.SemaphoreType.DMA((2 + experts,)),
        ],
        compiler_params=params(16),
        cost_estimate=cost(0, 6_000_000),
        name="pack",
    )(
        routes.reshape(1, token_count),
        route_weight.reshape(1, token_count),
        out_grad,
        gate_up.reshape(token_count, columns),
    )
    windows = call(
        functools.partial(window_kernel, per=per, lead=width - per),
        struct((parts, token_count, width), bf16),
        (),
        (target, tokens),
        "window",
        12,
        moved=2_000_000,
    )
    if down_weight.shape[1] % 16 == 0:
        held, other = [down_weight[0]], [swapped(down_weight[0])]
        for k in range(1, chips):
            arrival = onward(held[-1])
            if k == 1:
                arrival, windows = tied(arrival, windows)
            else:
                arrival, other = tied(arrival, other)
            held.append(arrival)
            other.append(swapped(arrival))
            if k == chips - 1:
                windows, held[-1] = tied(windows, held[-1])
        down = [piece for pair in zip(held, other) for piece in pair]
    else:
        down = [lax.all_gather(down_weight, "dp", axis=1, tiled=True)[0]]
        windows, down[0] = tied(windows, down[0])
    arrived = exchanged(packed, "expert").reshape(rows, wide)
    windows = exchanged(windows, "dp")
    factors = call(
        factor_kernel,
        [struct((rows, model_width), bf16)] + [struct((rows, hidden), f32)] * 3,
        (),
        (arrived,),
        "factors",
        20,
        moved=6_000_000,
    )
    ready = pl.pallas_call(
        ready_kernel,
        out_shape=struct((8, LANES), f32),
        in_specs=[anywhere()],
        out_specs=vmem(),
        compiler_params=params(4),
        cost_estimate=cost(0, 18_000_000),
        name="ready",
    )(down[-1])
    joined, scores = pl.pallas_call(
        functools.partial(row_kernel, chips=chips),
        out_shape=[struct((rows, columns), bf16), struct((rows, LANES), f32)],
        in_specs=[smem()] + [vmem()] * 4 + [anywhere()] * (len(down) + 1),
        out_specs=[hbm(), vmem()],
        scratch_shapes=[
            pltpu.VMEM((rows, columns), bf16),
            pltpu.VMEM((hidden, model_width), bf16),
            pltpu.SemaphoreType.DMA((len(down) + 2 * (hidden // (2 * LANES)),)),
        ],
        compiler_params=params(24),
        cost_estimate=cost(2 * rows * model_width * hidden, 8_000_000),
        name="rows",
    )(position, *factors, *down, ready)

    steps = [[joined, swapped(joined)]]
    step_one = onward(joined)
    heads = pl.pallas_call(
        head_kernel,
        grid=(1,),
        out_shape=struct((3, head_rows, LANES), f32),
        in_specs=[pl.BlockSpec((head_rows, LANES), lambda i: (0, 0))] * 3,
        out_specs=pl.BlockSpec((3, head_rows, LANES), lambda i: (0, 0, 0)),
        cost_estimate=cost(0, 400_000),
        name="heads",
    )(old, first, second)
    heads, _ = tied(heads, step_one)
    heads = lax.ppermute(heads, "dp", [(i + 1, i) for i in range(parts - 1)])
    compacted = call(
        compact_kernel,
        struct((experts, parts, cap, width), bf16),
        (position,),
        (windows, scores),
        "compact",
        12,
        moved=3_000_000,
    )
    compacted_rows = exchanged(compacted, "expert")
    turned = call(
        turn_kernel,
        struct((parts, kept, rows), bf16),
        (),
        (compacted_rows,),
        "turn",
        12,
        moved=3_000_000,
    )
    router_grad = call(
        router_kernel,
        struct((1, token_count), f32),
        (position,),
        (select, compacted_rows),
        "router",
        4,
        moved=300_000,
    )

    def early(name, at, pieces, sum_before):
        return call(
            functools.partial(early_kernel, steps=at, chips=chips),
            struct((kept, columns), f32),
            (position,),
            [turned] + pieces + sum_before,
            name,
            24,
            flops=4 * len(at) * rows * kept * columns,
            moved=8_000_000,
        )

    total = []
    arrival = joined
    for k in range(1, chips):
        arrival = onward(arrival) if k > 1 else step_one
        if k > 2:
            pieces = steps.pop()
            if k == 3:
                begun = early("early1", [0, 1], steps.pop(0) + steps.pop(0), [])
                total = [begun]
            total = [early("early%d" % (k - 1), [k - 1], pieces, total)]
        if k == chips - 1:
            arrival, total[0], router_grad, heads = tied(arrival, total[0], router_grad, heads)
        steps.append([arrival, swapped(arrival)])
    last = steps.pop()
    flat_rows = even_size // LANES
    sum_rows = round_up(kept * lines + head_rows + 32, 8)
    edge = round_up(-(-head_rows // lines), 16)
    new_master, new_one, new_two, new_weight = pl.pallas_call(
        functools.partial(final_kernel, even_size=even_size, head_rows=head_rows, chips=chips),
        out_shape=[state, state, state, struct((per, columns), bf16)],
        in_specs=[smem()] * 2 + [vmem()] * 8,
        out_specs=[anywhere(), anywhere(), anywhere(), vmem()],
        scratch_shapes=[
            pltpu.VMEM((sum_rows, LANES), f32),
            pltpu.VMEM((sum_rows, LANES), f32),
            pltpu.VMEM((round_up(flat_rows + head_rows + 32, 8), LANES), f32),
            pltpu.VMEM((bucket_rows, LANES), f32),
            pltpu.VMEM((bucket_rows, LANES), f32),
            pltpu.VMEM((edge * lines + 2 * head_rows + 32, LANES), f32),
            pltpu.SemaphoreType.DMA((4, 3)),
        ],
        compiler_params=params(32),
        cost_estimate=cost(4 * rows * kept * columns, 25_000_000),
        name="final",
    )(
        position,
        offsets,
        turned,
        total[0],
        heads,
        *last,
        old,
        first,
        second,
    )
    return (
        new_master.reshape(1, 1, bucket_cap),
        new_one.reshape(1, 1, bucket_cap),
        new_two.reshape(1, 1, bucket_cap),
        new_weight[None],
        router_grad.reshape(token_count, 1),
    )


def solution(mesh):
    placed = (
        P(("dp", "expert"), None),
        P(("dp", "expert"), None),
        P(("dp", "expert"), None, None),
        P(("dp", "expert"), None),
        P(("dp", "expert"), None),
        P("expert", "dp", None),
        P("expert", "dp", None),
        P("expert", "dp", None),
        P("expert", "dp", None),
        P(),
    )
    return jax.shard_map(
        shards,
        mesh=mesh,
        in_specs=placed,
        out_specs=(
            P("expert", "dp", None),
            P("expert", "dp", None),
            P("expert", "dp", None),
            P("expert", "dp", None),
            P(("dp", "expert"), None),
        ),
        check_vma=False,
    )
```

```python
import functools

import jax
import jax.numpy as jnp
from jax import lax
from jax.experimental import pallas as pl
from jax.experimental.pallas import tpu as pltpu
from jax.sharding import PartitionSpec as P

beta_one = 0.9
beta_two = 0.95
learn_rate = 0.001
decay_rate = 0.1
adam_eps = 1e-08
adam_step = 20.0

LANES = 128
CHUNK = 120

f32 = jnp.float32
bf16 = jnp.bfloat16
i32 = jnp.int32


def round_up(value, unit):
    return -(-value // unit) * unit


def iota(shape, axis):
    return lax.broadcasted_iota(i32, shape, axis)


def params(mib):
    return pltpu.CompilerParams(vmem_limit_bytes=mib * 1024 * 1024)


def cost(flops, moved):
    return pl.CostEstimate(flops=int(flops), bytes_accessed=int(moved), transcendentals=0)


def pack_kernel(
    routes_ref, weight_ref, grads_any, saved_any, select_ref, target_ref, packed_any, grads, saved, packed, sems
):
    loads = [
        pltpu.make_async_copy(grads_any, grads, sems.at[0]),
        pltpu.make_async_copy(saved_any, saved, sems.at[1]),
    ]
    for load in loads:
        load.start()
    ids = routes_ref[...]
    experts, cap, _ = packed.shape
    count = ids.shape[1]
    width = grads.shape[1]
    hits = iota((round_up(experts, 8), count), 0) == ids
    before = (iota((count, count), 0) < iota((count, count), 1)).astype(bf16)
    earlier = jnp.dot(hits.astype(f32).astype(bf16), before, preferred_element_type=f32)
    slot = jnp.sum(jnp.where(hits, earlier, 0.0), axis=0, keepdims=True)
    target = ids * cap + slot.astype(i32)
    chosen = iota((experts * cap, count), 0) == target
    select = chosen.astype(f32).astype(bf16)
    select_ref[...] = chosen.astype(f32)
    target_ref[...] = target.astype(f32)
    weight = jnp.sum(jnp.where(chosen, weight_ref[...].astype(f32), 0.0), axis=1, keepdims=True)
    weight = jnp.broadcast_to(weight, (experts * cap, LANES)).astype(bf16)
    for load in loads:
        load.wait()
    picked_grads = jnp.dot(select, grads[...], preferred_element_type=f32).astype(bf16)
    picked_saved = jnp.dot(select, saved[...], preferred_element_type=f32).astype(bf16)
    stores = []
    for k in range(experts):
        span = slice(k * cap, (k + 1) * cap)
        packed[k, :, :width] = picked_grads[span]
        packed[k, :, width:-LANES] = picked_saved[span]
        packed[k, :, -LANES:] = weight[span]
        stores.append(pltpu.make_async_copy(packed.at[k], packed_any.at[k], sems.at[2 + k]))
        stores[-1].start()
    for store in stores:
        store.wait()


def window_kernel(target_ref, tokens_ref, out_ref, *, per, lead):
    parts, count, width = out_ref.shape
    diagonal = iota((count, count), 0) == iota((count, count), 1)
    column = jnp.sum(jnp.where(diagonal, target_ref[...], 0.0), axis=1, keepdims=True)
    note = jnp.broadcast_to(column, (count, width)).astype(bf16)
    lane = iota((count, width), 1)
    for j in range(parts):
        start = per * j - lead
        if start < 0:
            blank = jnp.zeros((count, -start), bf16)
            piece = jnp.concatenate([blank, tokens_ref[:, : start + width]], axis=1)
        else:
            piece = tokens_ref[:, start : start + width]
        out_ref[j] = jnp.where(lane == 0, note, piece)


def compact_kernel(position_ref, windows_ref, scores_ref, out_ref):
    parts, count, width = windows_ref.shape
    experts, _, cap, _ = out_ref.shape
    diagonal = iota((count, count), 0) == iota((count, count), 1)
    slots = iota((experts * cap, count), 0)
    for i in range(parts):
        block = windows_ref[i]
        column = block[:, 0:1].astype(f32)
        target = jnp.sum(jnp.where(diagonal, column, 0.0), axis=0, keepdims=True).astype(i32)
        select = (slots == target).astype(f32).astype(bf16)
        rows = jnp.dot(select, block, preferred_element_type=f32).astype(bf16)
        for k in range(experts):
            out_ref[k, i] = rows[k * cap : (k + 1) * cap]
    lane = iota((cap, LANES), 1)
    for k in range(experts):
        rest = scores_ref[k * cap : (k + 1) * cap, :]
        first = out_ref[k, position_ref[0], :, :LANES]
        for c in range(3):
            part = rest.astype(bf16)
            rest = rest - part.astype(f32)
            first = jnp.where(lane == 1 + c, part, first)
        out_ref[k, position_ref[0], :, :LANES] = first


def turn_kernel(rows_ref, out_ref):
    experts, parts, _, width = rows_ref.shape
    kept = out_ref.shape[1]
    for i in range(parts):
        slab = jnp.concatenate([rows_ref[k, i] for k in range(experts)], axis=0)
        out_ref[i] = slab.T[width - kept :, :]


def factor_kernel(arrived_ref, grads_ref, gate_ref, up_ref, score_ref):
    width, hidden = grads_ref.shape[1], gate_ref.shape[1]
    grads_ref[...] = arrived_ref[:, :width]
    gate = arrived_ref[:, width : width + hidden].astype(f32)
    up = arrived_ref[:, width + hidden : width + 2 * hidden].astype(f32)
    weight = arrived_ref[:, width + 2 * hidden :].astype(f32)[:, 0:1]
    sig = jax.nn.sigmoid(gate)
    act = gate * sig
    score_ref[...] = act * up
    up_ref[...] = weight * act
    gate_ref[...] = weight * (up * sig * (1.0 + gate * (1.0 - sig)))


def row_kernel(position_ref, grads_ref, gate_factor, up_factor, score_factor, *refs, chips, places):
    down_refs, refs = refs[:-6], refs[-5:]
    joined_any, scores_ref, joined, down, sems = refs
    hidden = down.shape[0]
    loads = []
    for n, down_ref in enumerate(down_refs):
        size = down_ref.shape[0]
        if size == hidden:
            at = 0
        else:
            k, other, half = places[n]
            slab = lax.rem(position_ref[0] + 2 * (chips - k), 2 * chips) ^ other
            at = pl.multiple_of(slab * (hidden // (2 * chips)) + half * size, 16)
        loads.append(pltpu.make_async_copy(down_ref, down.at[pl.ds(at, size)], sems.at[n]))
    for load in loads:
        load.start()
    for load in loads:
        load.wait()
    scores = None
    step = 2 * LANES
    stores = []
    for at in range(0, hidden, step):
        span = slice(at, at + step)
        back = lax.dot_general(
            grads_ref[...], down[span, :], (((1,), (1,)), ((), ())), preferred_element_type=f32
        )
        part = jnp.sum(score_factor[:, span] * back, axis=1, keepdims=True)
        scores = part if scores is None else scores + part
        for half, factor in enumerate((gate_factor, up_factor)):
            out = slice(half * hidden + at, half * hidden + at + step)
            joined[:, out] = (factor[:, span] * back).astype(bf16)
            sem = sems.at[len(down_refs) + 2 * (at // step) + half]
            stores.append(pltpu.make_async_copy(joined.at[:, out], joined_any.at[:, out], sem))
            stores[-1].start()
    scores_ref[...] = jnp.broadcast_to(scores, scores_ref.shape)
    for store in stores:
        store.wait()


def router_kernel(position_ref, select_ref, rows_ref, out_ref):
    experts = rows_ref.shape[0]
    own = [rows_ref[k, position_ref[0], :, :LANES] for k in range(experts)]
    parts = jnp.concatenate(own, axis=0).astype(f32)
    scores = (parts[:, 1:2] + parts[:, 2:3]) + parts[:, 3:4]
    out_ref[...] = jnp.sum(jnp.where(select_ref[...] > 0.5, scores, 0.0), axis=0, keepdims=True)


def head_kernel(master_ref, first_ref, second_ref, out_ref):
    for n, source in enumerate((master_ref, first_ref, second_ref)):
        out_ref[n] = source[...]


def ready_kernel(*refs):
    refs[-1][...] = jnp.zeros(refs[-1].shape, f32)


def slab_sum(total, turned_ref, slabs, joined_refs, span):
    for slab, ref in zip(slabs, joined_refs):
        piece = jnp.dot(turned_ref[slab], ref[:, span], preferred_element_type=f32)
        piece = piece.astype(bf16).astype(f32)
        total = piece if total is None else total + piece
    return total


def slabs_of(position, steps, chips):
    own = [lax.rem(position + 2 * (chips - k), 2 * chips) for k in steps]
    return [slab ^ other for slab in own for other in (0, 1)]


def early_kernel(position_ref, turned_ref, *refs, steps, chips):
    joined_refs, base, sum_ref = refs[: 2 * len(steps)], refs[2 * len(steps) : -1], refs[-1]
    step = 2 * LANES
    slabs = slabs_of(position_ref[0], steps, chips)
    for at in range(0, sum_ref.shape[1], step):
        span = slice(at, at + step)
        total = base[0][:, span] if base else None
        sum_ref[:, span] = slab_sum(total, turned_ref, slabs, joined_refs, span)


def adam(grad, old, first, second):
    first_new = beta_one * first + (1.0 - beta_one) * grad
    second_new = beta_two * second + (1.0 - beta_two) * grad * grad
    below = jnp.sqrt(second_new * (1.0 / (1.0 - beta_two**adam_step))) + adam_eps
    update = first_new * (learn_rate / (1.0 - beta_one**adam_step)) / below
    return old * (1.0 - learn_rate * decay_rate) - update, first_new, second_new


def final_kernel(
    position_ref,
    offsets_ref,
    turned_ref,
    early_ref,
    heads_ref,
    own_ref,
    other_ref,
    old,
    first,
    second,
    out_master,
    out_first,
    out_second,
    weight_ref,
    sums,
    moved,
    new_old,
    new_first,
    new_second,
    head_new,
    sems,
    *,
    even_size,
    head_rows,
    chips,
):
    kept, columns = early_ref.shape
    per = weight_ref.shape[0]
    lines = columns // LANES
    before = (kept - per) * lines
    bucket_rows = old.shape[0]
    flat_rows = even_size // LANES
    position = position_ref[0]
    start = offsets_ref[position]
    finish = offsets_ref[position + 1]
    shift = position * even_size - start
    next_shift = (position + 1) * even_size - finish
    length = finish - start
    whole, part = shift // LANES, shift % LANES
    odd = whole % 8
    next_whole, next_part = next_shift // LANES, next_shift % LANES

    step = 2 * LANES
    slabs = slabs_of(position, [chips - 1], chips)
    for begin in range(0, columns, step):
        span = slice(begin, begin + step)
        total = slab_sum(early_ref[:, span], turned_ref, slabs, (own_ref, other_ref), span)
        for c in range(step // LANES):
            block = pltpu.roll(total[:, c * LANES : (c + 1) * LANES], part, 1)
            line = begin // LANES + c
            sums[pl.ds(odd + line, kept, stride=lines), :] = block
            moved[pl.ds(odd + line + 1, kept, stride=lines), :] = block

    def slots_of(row, count):
        at = pl.multiple_of(row + before - (whole - odd), 8)
        lane = iota((count, LANES), 1)
        return jnp.where(lane >= part, sums[pl.ds(at, count), :], moved[pl.ds(at, count), :])

    def update(row, count):
        span = pl.ds(row, count)
        a, b, c = adam(slots_of(row, count), old[span, :], first[span, :], second[span, :])
        new_old[span, :], new_first[span, :], new_second[span, :] = a, b, c

    def masked(row, count):
        span = pl.ds(row, count)
        inside = (row + iota((count, LANES), 0)) * LANES + iota((count, LANES), 1) < length
        grad = jnp.where(inside, slots_of(row, count), 0.0)
        a, b, c = adam(grad, old[span, :], first[span, :], second[span, :])
        new_old[span, :] = jnp.where(inside, a, 0.0)
        new_first[span, :] = jnp.where(inside, b, 0.0)
        new_second[span, :] = jnp.where(inside, c, 0.0)

    def send(begin, count, slot):
        span = pl.ds(begin, count)
        stores = [
            pltpu.make_async_copy(source.at[span], target.at[span], sems.at[slot, n])
            for n, (source, target) in enumerate(
                ((new_old, out_master), (new_first, out_first), (new_second, out_second))
            )
        ]
        for store in stores:
            store.start()
        return stores

    def chunk(n, carry):
        update(pl.multiple_of(n * CHUNK, 8), CHUNK)
        return carry

    safe = (flat_rows - head_rows) // CHUNK
    third = -(-safe // 3)
    stores = []
    for slot, begin in enumerate(range(0, safe, third)):
        end = min(begin + third, safe)
        lax.fori_loop(begin, end, chunk, 0)
        stores += send(begin * CHUNK, (end - begin) * CHUNK, slot)
    for row in range(safe * CHUNK, bucket_rows, CHUNK):
        masked(row, min(CHUNK, bucket_rows - row))
    stores += send(safe * CHUNK, bucket_rows - safe * CHUNK, 3)

    def next_slots():
        lane = iota((head_rows, LANES), 1)
        base = flat_rows + before - next_whole + odd
        here = pltpu.roll(sums[pl.ds(base, head_rows), :], (LANES - part) % LANES, 1)
        above = pltpu.roll(sums[pl.ds(base - 1, head_rows), :], (LANES - part) % LANES, 1)
        return pltpu.roll(jnp.where(lane < LANES - next_part, here, above), next_part, 1)

    edge = round_up(-(-head_rows // lines), 16)
    head_new[pl.ds(edge * lines, head_rows), :] = adam(next_slots(), heads_ref[0], heads_ref[1], heads_ref[2])[0]

    flat_row = iota((edge, LANES), 0) + (per - edge)
    for c in range(lines):
        lane = iota((per, LANES), 1)
        here = new_old[pl.ds(c + whole, per, stride=lines), :]
        below = new_old[pl.ds(c + whole + 1, per, stride=lines), :]
        own = pltpu.roll(jnp.where(lane >= part, here, below), (LANES - part) % LANES, 1)
        base = c + next_whole
        lane = iota((edge, LANES), 1)
        here = head_new[pl.ds(base, edge, stride=lines), :]
        below = head_new[pl.ds(base + 1, edge, stride=lines), :]
        other = pltpu.roll(jnp.where(lane >= next_part, here, below), (LANES - next_part) % LANES, 1)
        flat = (flat_row * lines + c) * LANES + lane
        last = jnp.where(flat < even_size - next_shift, own[per - edge :], other)
        out = slice(c * LANES, (c + 1) * LANES)
        if per > edge:
            weight_ref[: per - edge, out] = own[: per - edge].astype(bf16)
        weight_ref[per - edge :, out] = last.astype(bf16)

    for store in stores:
        store.wait()


def vmem():
    return pl.BlockSpec(memory_space=pltpu.VMEM)


def anywhere():
    return pl.BlockSpec(memory_space=pl.ANY)


def hbm():
    return pl.BlockSpec(memory_space=pltpu.HBM)


def smem():
    return pl.BlockSpec(memory_space=pltpu.SMEM)


def call(kernel, outs, scalars, args, name, mib, flops=0, moved=0):
    many = isinstance(outs, (list, tuple))
    return pl.pallas_call(
        kernel,
        out_shape=outs,
        in_specs=[smem()] * len(scalars) + [vmem()] * len(args),
        out_specs=[vmem()] * len(outs) if many else vmem(),
        compiler_params=params(mib),
        cost_estimate=cost(flops, moved),
        name=name,
    )(*scalars, *args)


def struct(shape, kind):
    return jax.ShapeDtypeStruct(shape, kind)


def shards(
    tokens,
    out_grad,
    gate_up,
    route_weight,
    routes,
    down_weight,
    master,
    moment_one,
    moment_two,
    offsets,
):
    token_count, model_width = tokens.shape
    columns = gate_up.shape[2]
    hidden = columns // 2
    bucket_cap = master.shape[2]
    groups = lax.axis_size("expert")
    parts = lax.axis_size("dp")
    experts = groups * master.shape[0]
    cap = 2 * token_count // experts
    rows = experts * cap
    per = model_width // parts
    even_size = per * columns
    margin = bucket_cap - even_size
    extra = round_up(-(-margin // columns), 16)
    width = round_up(per + extra + 4, LANES)
    kept = per + extra
    lines = columns // LANES
    bucket_rows = bucket_cap // LANES
    head_rows = round_up(margin // LANES, 8)

    chips = parts // 2
    position = lax.axis_index("dp").astype(i32).reshape(1)
    state = struct((bucket_rows, LANES), f32)
    old, first, second = (array.reshape(bucket_rows, LANES) for array in (master, moment_one, moment_two))

    def onward(block):
        return lax.ppermute(block, "dp", [(i, (i + 2) % parts) for i in range(parts)])

    def swapped(block):
        return lax.ppermute(block, "dp", [(i, i ^ 1) for i in range(parts)])

    def exchanged(block, axis):
        return lax.all_to_all(block, axis, split_axis=0, concat_axis=0, tiled=True)

    def tied(*values):
        return lax.optimization_barrier(values)

    wide = model_width + columns + LANES
    select, target, packed = pl.pallas_call(
        pack_kernel,
        out_shape=[
            struct((rows, token_count), f32),
            struct((1, token_count), f32),
            struct((experts, cap, wide), bf16),
        ],
        in_specs=[vmem(), vmem(), hbm(), hbm()],
        out_specs=[vmem(), vmem(), hbm()],
        scratch_shapes=[
            pltpu.VMEM((token_count, model_width), bf16),
            pltpu.VMEM((token_count, columns), bf16),
            pltpu.VMEM((experts, cap, wide), bf16),
            pltpu.SemaphoreType.DMA((2 + experts,)),
        ],
        compiler_params=params(60),
        cost_estimate=cost(0, 6_000_000),
        name="pack",
    )(
        routes.reshape(1, token_count),
        route_weight.reshape(1, token_count),
        out_grad,
        gate_up.reshape(token_count, columns),
    )
    windows = call(
        functools.partial(window_kernel, per=per, lead=width - per),
        struct((parts, token_count, width), bf16),
        (),
        (target, tokens),
        "window",
        12,
        moved=2_000_000,
    )
    size = down_weight.shape[1] // 2
    if size % 16 == 0:
        places = [(0, 0, 0), (0, 1, 0)]
        other = [swapped(down_weight[0])]
        down = [down_weight[0], other[0]]
        blocks = [down_weight[0, :size], down_weight[0, size:]]
        for k in range(1, chips):
            blocks = [onward(block) for block in blocks]
            if k == 1:
                blocks[0], blocks[1], windows = tied(*blocks, windows)
            else:
                blocks[1], other = tied(blocks[1], other)
            if k == chips - 1:
                windows, blocks[0] = tied(windows, blocks[0])
            other = [swapped(block) for block in blocks]
            down += blocks + other
            places += [(k, o, h) for o in (0, 1) for h in (0, 1)]
    else:
        down = [lax.all_gather(down_weight, "dp", axis=1, tiled=True)[0]]
        windows, down[0] = tied(windows, down[0])
        places = None
    arrived = exchanged(packed, "expert").reshape(rows, wide)
    windows = exchanged(windows, "dp")
    factors = call(
        factor_kernel,
        [struct((rows, model_width), bf16)] + [struct((rows, hidden), f32)] * 3,
        (),
        (arrived,),
        "factors",
        20,
        moved=6_000_000,
    )
    ready = pl.pallas_call(
        ready_kernel,
        out_shape=struct((8, LANES), f32),
        in_specs=[anywhere()],
        out_specs=vmem(),
        compiler_params=params(4),
        cost_estimate=cost(0, 18_000_000),
        name="ready",
    )(down[-1])
    joined, scores = pl.pallas_call(
        functools.partial(row_kernel, chips=chips, places=places),
        out_shape=[struct((rows, columns), bf16), struct((rows, LANES), f32)],
        in_specs=[smem()] + [vmem()] * 4 + [anywhere()] * (len(down) + 1),
        out_specs=[hbm(), vmem()],
        scratch_shapes=[
            pltpu.VMEM((rows, columns), bf16),
            pltpu.VMEM((hidden, model_width), bf16),
            pltpu.SemaphoreType.DMA((len(down) + 2 * (hidden // (2 * LANES)),)),
        ],
        compiler_params=params(24),
        cost_estimate=cost(2 * rows * model_width * hidden, 8_000_000),
        name="rows",
    )(position, *factors, *down, ready)

    steps = [[joined, swapped(joined)]]
    step_one = onward(joined)
    heads = pl.pallas_call(
        head_kernel,
        grid=(1,),
        out_shape=struct((3, head_rows, LANES), f32),
        in_specs=[pl.BlockSpec((head_rows, LANES), lambda i: (0, 0))] * 3,
        out_specs=pl.BlockSpec((3, head_rows, LANES), lambda i: (0, 0, 0)),
        cost_estimate=cost(0, 400_000),
        name="heads",
    )(old, first, second)
    heads, _ = tied(heads, step_one)
    heads = lax.ppermute(heads, "dp", [(i + 1, i) for i in range(parts - 1)])
    compacted = call(
        compact_kernel,
        struct((experts, parts, cap, width), bf16),
        (position,),
        (windows, scores),
        "compact",
        12,
        moved=3_000_000,
    )
    compacted_rows = exchanged(compacted, "expert")
    turned = call(
        turn_kernel,
        struct((parts, kept, rows), bf16),
        (),
        (compacted_rows,),
        "turn",
        12,
        moved=3_000_000,
    )
    router_grad = call(
        router_kernel,
        struct((1, token_count), f32),
        (position,),
        (select, compacted_rows),
        "router",
        4,
        moved=300_000,
    )

    def early(name, at, pieces, sum_before):
        return call(
            functools.partial(early_kernel, steps=at, chips=chips),
            struct((kept, columns), f32),
            (position,),
            [turned] + pieces + sum_before,
            name,
            24,
            flops=4 * len(at) * rows * kept * columns,
            moved=8_000_000,
        )

    total = []
    arrival = joined
    for k in range(1, chips):
        arrival = onward(arrival) if k > 1 else step_one
        if k > 2:
            pieces = steps.pop()
            if k == 3:
                begun = early("early1", [0, 1], steps.pop(0) + steps.pop(0), [])
                total = [begun]
            total = [early("early%d" % (k - 1), [k - 1], pieces, total)]
        if k == chips - 1:
            arrival, total[0], router_grad, heads = tied(arrival, total[0], router_grad, heads)
        steps.append([arrival, swapped(arrival)])
    last = steps.pop()
    flat_rows = even_size // LANES
    sum_rows = round_up(kept * lines + head_rows + 32, 8)
    edge = round_up(-(-head_rows // lines), 16)
    new_master, new_one, new_two, new_weight = pl.pallas_call(
        functools.partial(final_kernel, even_size=even_size, head_rows=head_rows, chips=chips),
        out_shape=[state, state, state, struct((per, columns), bf16)],
        in_specs=[smem()] * 2 + [vmem()] * 8,
        out_specs=[anywhere(), anywhere(), anywhere(), vmem()],
        scratch_shapes=[
            pltpu.VMEM((sum_rows, LANES), f32),
            pltpu.VMEM((sum_rows, LANES), f32),
            pltpu.VMEM((round_up(flat_rows + head_rows + 32, 8), LANES), f32),
            pltpu.VMEM((bucket_rows, LANES), f32),
            pltpu.VMEM((bucket_rows, LANES), f32),
            pltpu.VMEM((edge * lines + 2 * head_rows + 32, LANES), f32),
            pltpu.SemaphoreType.DMA((4, 3)),
        ],
        compiler_params=params(32),
        cost_estimate=cost(4 * rows * kept * columns, 25_000_000),
        name="final",
    )(
        position,
        offsets,
        turned,
        total[0],
        heads,
        *last,
        old,
        first,
        second,
    )
    return (
        new_master.reshape(1, 1, bucket_cap),
        new_one.reshape(1, 1, bucket_cap),
        new_two.reshape(1, 1, bucket_cap),
        new_weight[None],
        router_grad.reshape(token_count, 1),
    )


def solution(mesh):
    placed = (
        P(("dp", "expert"), None),
        P(("dp", "expert"), None),
        P(("dp", "expert"), None, None),
        P(("dp", "expert"), None),
        P(("dp", "expert"), None),
        P("expert", "dp", None),
        P("expert", "dp", None),
        P("expert", "dp", None),
        P("expert", "dp", None),
        P(),
    )
    return jax.shard_map(
        shards,
        mesh=mesh,
        in_specs=placed,
        out_specs=(
            P("expert", "dp", None),
            P("expert", "dp", None),
            P("expert", "dp", None),
            P("expert", "dp", None),
            P(("dp", "expert"), None),
        ),
        check_vma=False,
    )
```

```python
import functools

import jax
import jax.numpy as jnp
from jax import lax
from jax.experimental import pallas as pl
from jax.experimental.pallas import tpu as pltpu
from jax.sharding import PartitionSpec as P

beta_one = 0.9
beta_two = 0.95
learn_rate = 0.001
decay_rate = 0.1
adam_eps = 1e-08
adam_step = 20.0

LANES = 128
CHUNK = 120

f32 = jnp.float32
bf16 = jnp.bfloat16
i32 = jnp.int32


def round_up(value, unit):
    return -(-value // unit) * unit


def iota(shape, axis):
    return lax.broadcasted_iota(i32, shape, axis)


def params(mib):
    return pltpu.CompilerParams(vmem_limit_bytes=mib * 1024 * 1024)


def cost(flops, moved):
    return pl.CostEstimate(flops=int(flops), bytes_accessed=int(moved), transcendentals=0)


def pack_kernel(me_ref, routes_ref, weight_ref, grads_any, saved_any, select_ref, target_ref, *refs):
    packed_anys, (grads, saved, packed, sems) = refs[:-4], refs[-4:]
    loads = [
        pltpu.make_async_copy(grads_any, grads, sems.at[0]),
        pltpu.make_async_copy(saved_any, saved, sems.at[1]),
    ]
    for load in loads:
        load.start()
    ids = routes_ref[...]
    experts, cap, _ = packed.shape
    count = ids.shape[1]
    width = grads.shape[1]
    hits = iota((round_up(experts, 8), count), 0) == ids
    before = (iota((count, count), 0) < iota((count, count), 1)).astype(bf16)
    earlier = jnp.dot(hits.astype(f32).astype(bf16), before, preferred_element_type=f32)
    slot = jnp.sum(jnp.where(hits, earlier, 0.0), axis=0, keepdims=True)
    target = ids * cap + slot.astype(i32)
    chosen = iota((experts * cap, count), 0) == target
    select = chosen.astype(f32).astype(bf16)
    select_ref[...] = chosen.astype(f32)
    target_ref[...] = target.astype(f32)
    weight = jnp.sum(jnp.where(chosen, weight_ref[...].astype(f32), 0.0), axis=1, keepdims=True)
    weight = jnp.broadcast_to(weight, (experts * cap, LANES)).astype(bf16)
    for load in loads:
        load.wait()
    picked_grads = jnp.dot(select, grads[...], preferred_element_type=f32).astype(bf16)
    picked_saved = jnp.dot(select, saved[...], preferred_element_type=f32).astype(bf16)
    stores = []
    for k in range(experts):
        span = slice(k * cap, (k + 1) * cap)
        packed[k, :, :width] = picked_grads[span]
        packed[k, :, width:-LANES] = picked_saved[span]
        packed[k, :, -LANES:] = weight[span]
    for k, packed_any in enumerate(packed_anys):
        stores.append(pltpu.make_async_copy(packed.at[me_ref[0] ^ k], packed_any, sems.at[2 + k]))
        stores[-1].start()
    for store in stores:
        store.wait()


def window_kernel(target_ref, tokens_ref, out_ref, *, per, lead):
    parts, count, width = out_ref.shape
    diagonal = iota((count, count), 0) == iota((count, count), 1)
    column = jnp.sum(jnp.where(diagonal, target_ref[...], 0.0), axis=1, keepdims=True)
    note = jnp.broadcast_to(column, (count, width)).astype(bf16)
    lane = iota((count, width), 1)
    for j in range(parts):
        start = per * j - lead
        if start < 0:
            blank = jnp.zeros((count, -start), bf16)
            piece = jnp.concatenate([blank, tokens_ref[:, : start + width]], axis=1)
        else:
            piece = tokens_ref[:, start : start + width]
        out_ref[j] = jnp.where(lane == 0, note, piece)


def compact_kernel(position_ref, windows_ref, scores_ref, out_ref):
    parts, count, width = windows_ref.shape
    experts, _, cap, _ = out_ref.shape
    diagonal = iota((count, count), 0) == iota((count, count), 1)
    slots = iota((experts * cap, count), 0)
    for i in range(parts):
        block = windows_ref[i]
        column = block[:, 0:1].astype(f32)
        target = jnp.sum(jnp.where(diagonal, column, 0.0), axis=0, keepdims=True).astype(i32)
        select = (slots == target).astype(f32).astype(bf16)
        rows = jnp.dot(select, block, preferred_element_type=f32).astype(bf16)
        for k in range(experts):
            out_ref[k, i] = rows[k * cap : (k + 1) * cap]
    lane = iota((cap, LANES), 1)
    for k in range(experts):
        rest = scores_ref[k * cap : (k + 1) * cap, :]
        first = out_ref[k, position_ref[0], :, :LANES]
        for c in range(3):
            part = rest.astype(bf16)
            rest = rest - part.astype(f32)
            first = jnp.where(lane == 1 + c, part, first)
        out_ref[k, position_ref[0], :, :LANES] = first


def turn_kernel(rows_ref, out_ref):
    experts, parts, _, width = rows_ref.shape
    kept = out_ref.shape[1]
    for i in range(parts):
        slab = jnp.concatenate([rows_ref[k, i] for k in range(experts)], axis=0)
        out_ref[i] = slab.T[width - kept :, :]


def factor_kernel(me_ref, *refs):
    arrived_refs, (grads_ref, gate_ref, up_ref, score_ref) = refs[:-4], refs[-4:]
    width, hidden = grads_ref.shape[1], gate_ref.shape[1]
    cap = arrived_refs[0].shape[0]
    for k, arrived_ref in enumerate(arrived_refs):
        span = pl.ds(pl.multiple_of((me_ref[0] ^ k) * cap, 16), cap)
        grads_ref[span, :] = arrived_ref[:, :width]
        gate = arrived_ref[:, width : width + hidden].astype(f32)
        up = arrived_ref[:, width + hidden : width + 2 * hidden].astype(f32)
        weight = arrived_ref[:, width + 2 * hidden :].astype(f32)[:, 0:1]
        sig = jax.nn.sigmoid(gate)
        act = gate * sig
        score_ref[span, :] = act * up
        up_ref[span, :] = weight * act
        gate_ref[span, :] = weight * (up * sig * (1.0 + gate * (1.0 - sig)))


def row_kernel(position_ref, grads_ref, gate_factor, up_factor, score_factor, *refs, chips):
    down_refs, refs = refs[:-5], refs[-5:]
    joined_any, scores_ref, joined, down, sems = refs
    hidden = down.shape[0]
    loads = []
    for n, down_ref in enumerate(down_refs):
        size = down_ref.shape[0]
        if size == hidden:
            at = 0
        else:
            slab = lax.rem(position_ref[0] + 2 * (chips - n // 2), 2 * chips) ^ (n % 2)
            at = pl.multiple_of(slab * size, 16)
        loads.append(pltpu.make_async_copy(down_ref, down.at[pl.ds(at, size)], sems.at[n]))
    for load in loads:
        load.start()
    for load in loads:
        load.wait()
    scores = None
    step = 2 * LANES
    stores = []
    for at in range(0, hidden, step):
        span = slice(at, at + step)
        back = lax.dot_general(
            grads_ref[...], down[span, :], (((1,), (1,)), ((), ())), preferred_element_type=f32
        )
        part = jnp.sum(score_factor[:, span] * back, axis=1, keepdims=True)
        scores = part if scores is None else scores + part
        for half, factor in enumerate((gate_factor, up_factor)):
            out = slice(half * hidden + at, half * hidden + at + step)
            joined[:, out] = (factor[:, span] * back).astype(bf16)
            sem = sems.at[len(down_refs) + 2 * (at // step) + half]
            stores.append(pltpu.make_async_copy(joined.at[:, out], joined_any.at[:, out], sem))
            stores[-1].start()
    scores_ref[...] = jnp.broadcast_to(scores, scores_ref.shape)
    for store in stores:
        store.wait()


def router_kernel(position_ref, select_ref, rows_ref, out_ref):
    experts = rows_ref.shape[0]
    own = [rows_ref[k, position_ref[0], :, :LANES] for k in range(experts)]
    parts = jnp.concatenate(own, axis=0).astype(f32)
    scores = (parts[:, 1:2] + parts[:, 2:3]) + parts[:, 3:4]
    out_ref[...] = jnp.sum(jnp.where(select_ref[...] > 0.5, scores, 0.0), axis=0, keepdims=True)


def head_kernel(master_ref, first_ref, second_ref, out_ref):
    for n, source in enumerate((master_ref, first_ref, second_ref)):
        out_ref[n] = source[...]


def slab_sum(total, turned_ref, slabs, joined_refs, span):
    for slab, ref in zip(slabs, joined_refs):
        piece = jnp.dot(turned_ref[slab], ref[:, span], preferred_element_type=f32)
        piece = piece.astype(bf16).astype(f32)
        total = piece if total is None else total + piece
    return total


def slabs_of(position, steps, chips):
    own = [lax.rem(position + 2 * (chips - k), 2 * chips) for k in steps]
    return [slab ^ other for slab in own for other in (0, 1)]


def early_kernel(position_ref, turned_ref, *refs, steps, chips):
    joined_refs, base, sum_ref = refs[: 2 * len(steps)], refs[2 * len(steps) : -1], refs[-1]
    step = 2 * LANES
    slabs = slabs_of(position_ref[0], steps, chips)
    for at in range(0, sum_ref.shape[1], step):
        span = slice(at, at + step)
        total = base[0][:, span] if base else None
        sum_ref[:, span] = slab_sum(total, turned_ref, slabs, joined_refs, span)


def adam(grad, old, first, second):
    first_new = beta_one * first + (1.0 - beta_one) * grad
    second_new = beta_two * second + (1.0 - beta_two) * grad * grad
    below = jnp.sqrt(second_new * (1.0 / (1.0 - beta_two**adam_step))) + adam_eps
    update = first_new * (learn_rate / (1.0 - beta_one**adam_step)) / below
    return old * (1.0 - learn_rate * decay_rate) - update, first_new, second_new


def final_kernel(
    position_ref,
    offsets_ref,
    turned_ref,
    early_ref,
    heads_ref,
    own_ref,
    other_ref,
    old,
    first,
    second,
    out_master,
    out_first,
    out_second,
    weight_ref,
    sums,
    moved,
    new_old,
    new_first,
    new_second,
    head_new,
    sems,
    *,
    even_size,
    head_rows,
    chips,
):
    kept, columns = early_ref.shape
    per = weight_ref.shape[0]
    lines = columns // LANES
    before = (kept - per) * lines
    bucket_rows = old.shape[0]
    flat_rows = even_size // LANES
    position = position_ref[0]
    start = offsets_ref[position]
    finish = offsets_ref[position + 1]
    shift = position * even_size - start
    next_shift = (position + 1) * even_size - finish
    length = finish - start
    whole, part = shift // LANES, shift % LANES
    odd = whole % 8
    next_whole, next_part = next_shift // LANES, next_shift % LANES

    step = 2 * LANES
    slabs = slabs_of(position, [chips - 1], chips)
    for begin in range(0, columns, step):
        span = slice(begin, begin + step)
        total = slab_sum(early_ref[:, span], turned_ref, slabs, (own_ref, other_ref), span)
        for c in range(step // LANES):
            block = pltpu.roll(total[:, c * LANES : (c + 1) * LANES], part, 1)
            line = begin // LANES + c
            sums[pl.ds(odd + line, kept, stride=lines), :] = block
            moved[pl.ds(odd + line + 1, kept, stride=lines), :] = block

    def slots_of(row, count):
        at = pl.multiple_of(row + before - (whole - odd), 8)
        lane = iota((count, LANES), 1)
        return jnp.where(lane >= part, sums[pl.ds(at, count), :], moved[pl.ds(at, count), :])

    def update(row, count):
        span = pl.ds(row, count)
        a, b, c = adam(slots_of(row, count), old[span, :], first[span, :], second[span, :])
        new_old[span, :], new_first[span, :], new_second[span, :] = a, b, c

    def masked(row, count):
        span = pl.ds(row, count)
        inside = (row + iota((count, LANES), 0)) * LANES + iota((count, LANES), 1) < length
        grad = jnp.where(inside, slots_of(row, count), 0.0)
        a, b, c = adam(grad, old[span, :], first[span, :], second[span, :])
        new_old[span, :] = jnp.where(inside, a, 0.0)
        new_first[span, :] = jnp.where(inside, b, 0.0)
        new_second[span, :] = jnp.where(inside, c, 0.0)

    def send(begin, count, slot):
        span = pl.ds(begin, count)
        stores = [
            pltpu.make_async_copy(source.at[span], target.at[span], sems.at[slot, n])
            for n, (source, target) in enumerate(
                ((new_old, out_master), (new_first, out_first), (new_second, out_second))
            )
        ]
        for store in stores:
            store.start()
        return stores

    def chunk(n, carry):
        update(pl.multiple_of(n * CHUNK, 8), CHUNK)
        return carry

    safe = (flat_rows - head_rows) // CHUNK
    third = -(-safe // 3)
    stores = []
    for slot, begin in enumerate(range(0, safe, third)):
        end = min(begin + third, safe)
        lax.fori_loop(begin, end, chunk, 0)
        stores += send(begin * CHUNK, (end - begin) * CHUNK, slot)
    for row in range(safe * CHUNK, bucket_rows, CHUNK):
        masked(row, min(CHUNK, bucket_rows - row))
    stores += send(safe * CHUNK, bucket_rows - safe * CHUNK, 3)

    def next_slots():
        lane = iota((head_rows, LANES), 1)
        base = flat_rows + before - next_whole + odd
        here = pltpu.roll(sums[pl.ds(base, head_rows), :], (LANES - part) % LANES, 1)
        above = pltpu.roll(sums[pl.ds(base - 1, head_rows), :], (LANES - part) % LANES, 1)
        return pltpu.roll(jnp.where(lane < LANES - next_part, here, above), next_part, 1)

    edge = round_up(-(-head_rows // lines), 16)
    head_new[pl.ds(edge * lines, head_rows), :] = adam(next_slots(), heads_ref[0], heads_ref[1], heads_ref[2])[0]

    flat_row = iota((edge, LANES), 0) + (per - edge)
    for c in range(lines):
        lane = iota((per, LANES), 1)
        here = new_old[pl.ds(c + whole, per, stride=lines), :]
        below = new_old[pl.ds(c + whole + 1, per, stride=lines), :]
        own = pltpu.roll(jnp.where(lane >= part, here, below), (LANES - part) % LANES, 1)
        base = c + next_whole
        lane = iota((edge, LANES), 1)
        here = head_new[pl.ds(base, edge, stride=lines), :]
        below = head_new[pl.ds(base + 1, edge, stride=lines), :]
        other = pltpu.roll(jnp.where(lane >= next_part, here, below), (LANES - next_part) % LANES, 1)
        flat = (flat_row * lines + c) * LANES + lane
        last = jnp.where(flat < even_size - next_shift, own[per - edge :], other)
        out = slice(c * LANES, (c + 1) * LANES)
        if per > edge:
            weight_ref[: per - edge, out] = own[: per - edge].astype(bf16)
        weight_ref[per - edge :, out] = last.astype(bf16)

    for store in stores:
        store.wait()


def vmem():
    return pl.BlockSpec(memory_space=pltpu.VMEM)


def anywhere():
    return pl.BlockSpec(memory_space=pl.ANY)


def hbm():
    return pl.BlockSpec(memory_space=pltpu.HBM)


def smem():
    return pl.BlockSpec(memory_space=pltpu.SMEM)


def call(kernel, outs, scalars, args, name, mib, flops=0, moved=0):
    many = isinstance(outs, (list, tuple))
    return pl.pallas_call(
        kernel,
        out_shape=outs,
        in_specs=[smem()] * len(scalars) + [vmem()] * len(args),
        out_specs=[vmem()] * len(outs) if many else vmem(),
        compiler_params=params(mib),
        cost_estimate=cost(flops, moved),
        name=name,
    )(*scalars, *args)


def struct(shape, kind):
    return jax.ShapeDtypeStruct(shape, kind)


def shards(
    tokens,
    out_grad,
    gate_up,
    route_weight,
    routes,
    down_weight,
    master,
    moment_one,
    moment_two,
    offsets,
):
    token_count, model_width = tokens.shape
    columns = gate_up.shape[2]
    hidden = columns // 2
    bucket_cap = master.shape[2]
    groups = lax.axis_size("expert")
    parts = lax.axis_size("dp")
    experts = groups * master.shape[0]
    cap = 2 * token_count // experts
    rows = experts * cap
    per = model_width // parts
    even_size = per * columns
    margin = bucket_cap - even_size
    extra = round_up(-(-margin // columns), 16)
    width = round_up(per + extra + 4, LANES)
    kept = per + extra
    lines = columns // LANES
    bucket_rows = bucket_cap // LANES
    head_rows = round_up(margin // LANES, 8)

    chips = parts // 2
    position = lax.axis_index("dp").astype(i32).reshape(1)
    state = struct((bucket_rows, LANES), f32)
    old, first, second = (array.reshape(bucket_rows, LANES) for array in (master, moment_one, moment_two))

    def onward(block):
        return lax.ppermute(block, "dp", [(i, (i + 2) % parts) for i in range(parts)])

    def swapped(block):
        return lax.ppermute(block, "dp", [(i, i ^ 1) for i in range(parts)])

    def exchanged(block, axis):
        return lax.all_to_all(block, axis, split_axis=0, concat_axis=0, tiled=True)

    def tied(*values):
        return lax.optimization_barrier(values)

    wide = model_width + columns + LANES
    me = lax.axis_index("expert").astype(i32).reshape(1)
    select, target, *packed = pl.pallas_call(
        pack_kernel,
        out_shape=[
            struct((rows, token_count), f32),
            struct((1, token_count), f32),
        ]
        + [struct((cap, wide), bf16)] * experts,
        in_specs=[smem(), vmem(), vmem(), hbm(), hbm()],
        out_specs=[vmem(), vmem()] + [hbm()] * experts,
        scratch_shapes=[
            pltpu.VMEM((token_count, model_width), bf16),
            pltpu.VMEM((token_count, columns), bf16),
            pltpu.VMEM((experts, cap, wide), bf16),
            pltpu.SemaphoreType.DMA((2 + experts,)),
        ],
        compiler_params=params(60),
        cost_estimate=cost(0, 6_000_000),
        name="pack",
    )(
        me,
        routes.reshape(1, token_count),
        route_weight.reshape(1, token_count),
        out_grad,
        gate_up.reshape(token_count, columns),
    )
    windows = call(
        functools.partial(window_kernel, per=per, lead=width - per),
        struct((parts, token_count, width), bf16),
        (),
        (target, tokens),
        "window",
        12,
        moved=2_000_000,
    )
    arrived = packed[:1] + [
        lax.ppermute(packed[k], "expert", [(i, i ^ k) for i in range(experts)]) for k in range(1, experts)
    ]
    windows = exchanged(windows, "dp")
    if down_weight.shape[1] % 16 == 0:
        held, other = [down_weight[0]], [swapped(down_weight[0])]
        for k in range(1, chips):
            arrival = onward(held[-1])
            held.append(arrival)
            if k == chips - 2:
                held[-1], arrived[1], arrived[2] = tied(held[-1], arrived[1], arrived[2])
                arrived[-1], windows, block = tied(arrived[-1], windows, held[-1])
                other.append(swapped(block))
                continue
            other.append(swapped(held[-1]))
        down = [piece for pair in zip(held, other) for piece in pair]
    else:
        down = [lax.all_gather(down_weight, "dp", axis=1, tiled=True)[0]]
    factors = call(
        factor_kernel,
        [struct((rows, model_width), bf16)] + [struct((rows, hidden), f32)] * 3,
        (me,),
        arrived,
        "factors",
        20,
        moved=6_000_000,
    )
    joined, scores = pl.pallas_call(
        functools.partial(row_kernel, chips=chips),
        out_shape=[struct((rows, columns), bf16), struct((rows, LANES), f32)],
        in_specs=[smem()] + [vmem()] * 4 + [anywhere()] * len(down),
        out_specs=[hbm(), vmem()],
        scratch_shapes=[
            pltpu.VMEM((rows, columns), bf16),
            pltpu.VMEM((hidden, model_width), bf16),
            pltpu.SemaphoreType.DMA((len(down) + 2 * (hidden // (2 * LANES)),)),
        ],
        compiler_params=params(24),
        cost_estimate=cost(2 * rows * model_width * hidden, 8_000_000),
        name="rows",
    )(position, *factors, *down)

    steps = [[joined, swapped(joined)]]
    step_one = onward(joined)
    heads = pl.pallas_call(
        head_kernel,
        grid=(1,),
        out_shape=struct((3, head_rows, LANES), f32),
        in_specs=[pl.BlockSpec((head_rows, LANES), lambda i: (0, 0))] * 3,
        out_specs=pl.BlockSpec((3, head_rows, LANES), lambda i: (0, 0, 0)),
        cost_estimate=cost(0, 400_000),
        name="heads",
    )(old, first, second)
    heads, _ = tied(heads, step_one)
    heads = lax.ppermute(heads, "dp", [(i + 1, i) for i in range(parts - 1)])
    compacted = call(
        compact_kernel,
        struct((experts, parts, cap, width), bf16),
        (position,),
        (windows, scores),
        "compact",
        12,
        moved=3_000_000,
    )
    compacted_rows = exchanged(compacted, "expert")
    turned = call(
        turn_kernel,
        struct((parts, kept, rows), bf16),
        (),
        (compacted_rows,),
        "turn",
        12,
        moved=3_000_000,
    )
    router_grad = call(
        router_kernel,
        struct((1, token_count), f32),
        (position,),
        (select, compacted_rows),
        "router",
        4,
        moved=300_000,
    )

    def early(name, at, pieces, sum_before):
        return call(
            functools.partial(early_kernel, steps=at, chips=chips),
            struct((kept, columns), f32),
            (position,),
            [turned] + pieces + sum_before,
            name,
            24,
            flops=4 * len(at) * rows * kept * columns,
            moved=8_000_000,
        )

    total = []
    arrival = joined
    for k in range(1, chips):
        arrival = onward(arrival) if k > 1 else step_one
        if k > 2:
            pieces = steps.pop()
            if k == 3:
                begun = early("early1", [0, 1], steps.pop(0) + steps.pop(0), [])
                total = [begun]
            total = [early("early%d" % (k - 1), [k - 1], pieces, total)]
        if k == chips - 1:
            arrival, total[0], router_grad, heads = tied(arrival, total[0], router_grad, heads)
        steps.append([arrival, swapped(arrival)])
    last = steps.pop()
    flat_rows = even_size // LANES
    sum_rows = round_up(kept * lines + head_rows + 32, 8)
    edge = round_up(-(-head_rows // lines), 16)
    new_master, new_one, new_two, new_weight = pl.pallas_call(
        functools.partial(final_kernel, even_size=even_size, head_rows=head_rows, chips=chips),
        out_shape=[state, state, state, struct((per, columns), bf16)],
        in_specs=[smem()] * 2 + [vmem()] * 8,
        out_specs=[anywhere(), anywhere(), anywhere(), vmem()],
        scratch_shapes=[
            pltpu.VMEM((sum_rows, LANES), f32),
            pltpu.VMEM((sum_rows, LANES), f32),
            pltpu.VMEM((round_up(flat_rows + head_rows + 32, 8), LANES), f32),
            pltpu.VMEM((bucket_rows, LANES), f32),
            pltpu.VMEM((bucket_rows, LANES), f32),
            pltpu.VMEM((edge * lines + 2 * head_rows + 32, LANES), f32),
            pltpu.SemaphoreType.DMA((4, 3)),
        ],
        compiler_params=params(32),
        cost_estimate=cost(4 * rows * kept * columns, 25_000_000),
        name="final",
    )(
        position,
        offsets,
        turned,
        total[0],
        heads,
        *last,
        old,
        first,
        second,
    )
    return (
        new_master.reshape(1, 1, bucket_cap),
        new_one.reshape(1, 1, bucket_cap),
        new_two.reshape(1, 1, bucket_cap),
        new_weight[None],
        router_grad.reshape(token_count, 1),
    )


def solution(mesh):
    placed = (
        P(("dp", "expert"), None),
        P(("dp", "expert"), None),
        P(("dp", "expert"), None, None),
        P(("dp", "expert"), None),
        P(("dp", "expert"), None),
        P("expert", "dp", None),
        P("expert", "dp", None),
        P("expert", "dp", None),
        P("expert", "dp", None),
        P(),
    )
    return jax.shard_map(
        shards,
        mesh=mesh,
        in_specs=placed,
        out_specs=(
            P("expert", "dp", None),
            P("expert", "dp", None),
            P("expert", "dp", None),
            P("expert", "dp", None),
            P(("dp", "expert"), None),
        ),
        check_vma=False,
    )
```

```python
import functools

import jax
import jax.numpy as jnp
from jax import lax
from jax.experimental import pallas as pl
from jax.experimental.pallas import tpu as pltpu
from jax.sharding import PartitionSpec as P

beta_one = 0.9
beta_two = 0.95
learn_rate = 0.001
decay_rate = 0.1
adam_eps = 1e-08
adam_step = 20.0

LANES = 128
CHUNK = 120

f32 = jnp.float32
bf16 = jnp.bfloat16
i32 = jnp.int32


def round_up(value, unit):
    return -(-value // unit) * unit


def iota(shape, axis):
    return lax.broadcasted_iota(i32, shape, axis)


def params(mib):
    return pltpu.CompilerParams(vmem_limit_bytes=mib * 1024 * 1024)


def cost(flops, moved):
    return pl.CostEstimate(flops=int(flops), bytes_accessed=int(moved), transcendentals=0)


def pack_kernel(me_ref, routes_ref, weight_ref, grads_any, saved_any, select_ref, target_ref, *refs):
    packed_anys, (grads, saved, packed, sems) = refs[:-4], refs[-4:]
    loads = [
        pltpu.make_async_copy(grads_any, grads, sems.at[0]),
        pltpu.make_async_copy(saved_any, saved, sems.at[1]),
    ]
    for load in loads:
        load.start()
    ids = routes_ref[...]
    experts, cap, _ = packed.shape
    count = ids.shape[1]
    width = grads.shape[1]
    hits = iota((round_up(experts, 8), count), 0) == ids
    before = (iota((count, count), 0) < iota((count, count), 1)).astype(bf16)
    earlier = jnp.dot(hits.astype(f32).astype(bf16), before, preferred_element_type=f32)
    slot = jnp.sum(jnp.where(hits, earlier, 0.0), axis=0, keepdims=True)
    target = ids * cap + slot.astype(i32)
    chosen = iota((experts * cap, count), 0) == target
    select = chosen.astype(f32).astype(bf16)
    select_ref[...] = chosen.astype(f32)
    target_ref[...] = target.astype(f32)
    weight = jnp.sum(jnp.where(chosen, weight_ref[...].astype(f32), 0.0), axis=1, keepdims=True)
    weight = jnp.broadcast_to(weight, (experts * cap, LANES)).astype(bf16)
    for load in loads:
        load.wait()
    picked_grads = jnp.dot(select, grads[...], preferred_element_type=f32).astype(bf16)
    picked_saved = jnp.dot(select, saved[...], preferred_element_type=f32).astype(bf16)
    stores = []
    for k in range(experts):
        span = slice(k * cap, (k + 1) * cap)
        packed[k, :, :width] = picked_grads[span]
        packed[k, :, width:-LANES] = picked_saved[span]
        packed[k, :, -LANES:] = weight[span]
    for k, packed_any in enumerate(packed_anys):
        stores.append(pltpu.make_async_copy(packed.at[me_ref[0] ^ k], packed_any, sems.at[2 + k]))
        stores[-1].start()
    for store in stores:
        store.wait()


def window_kernel(target_ref, tokens_ref, out_ref, *, per, lead):
    parts, count, width = out_ref.shape
    diagonal = iota((count, count), 0) == iota((count, count), 1)
    column = jnp.sum(jnp.where(diagonal, target_ref[...], 0.0), axis=1, keepdims=True)
    note = jnp.broadcast_to(column, (count, width)).astype(bf16)
    lane = iota((count, width), 1)
    for j in range(parts):
        start = per * j - lead
        if start < 0:
            blank = jnp.zeros((count, -start), bf16)
            piece = jnp.concatenate([blank, tokens_ref[:, : start + width]], axis=1)
        else:
            piece = tokens_ref[:, start : start + width]
        out_ref[j] = jnp.where(lane == 0, note, piece)


def compact_kernel(position_ref, windows_ref, scores_ref, out_ref):
    parts, count, width = windows_ref.shape
    experts, _, cap, _ = out_ref.shape
    diagonal = iota((count, count), 0) == iota((count, count), 1)
    slots = iota((experts * cap, count), 0)
    for i in range(parts):
        block = windows_ref[i]
        column = block[:, 0:1].astype(f32)
        target = jnp.sum(jnp.where(diagonal, column, 0.0), axis=0, keepdims=True).astype(i32)
        select = (slots == target).astype(f32).astype(bf16)
        rows = jnp.dot(select, block, preferred_element_type=f32).astype(bf16)
        for k in range(experts):
            out_ref[k, i] = rows[k * cap : (k + 1) * cap]
    lane = iota((cap, LANES), 1)
    for k in range(experts):
        rest = scores_ref[k * cap : (k + 1) * cap, :]
        first = out_ref[k, position_ref[0], :, :LANES]
        for c in range(3):
            part = rest.astype(bf16)
            rest = rest - part.astype(f32)
            first = jnp.where(lane == 1 + c, part, first)
        out_ref[k, position_ref[0], :, :LANES] = first


def turn_kernel(rows_ref, out_ref):
    experts, parts, _, width = rows_ref.shape
    kept = out_ref.shape[1]
    for i in range(parts):
        slab = jnp.concatenate([rows_ref[k, i] for k in range(experts)], axis=0)
        out_ref[i] = slab.T[width - kept :, :]


def factor_kernel(me_ref, *refs):
    arrived_refs, (grads_ref, gate_ref, up_ref, score_ref) = refs[:-4], refs[-4:]
    width, hidden = grads_ref.shape[1], gate_ref.shape[1]
    cap = arrived_refs[0].shape[0]
    for k, arrived_ref in enumerate(arrived_refs):
        span = pl.ds(pl.multiple_of((me_ref[0] ^ k) * cap, 16), cap)
        grads_ref[span, :] = arrived_ref[:, :width]
        gate = arrived_ref[:, width : width + hidden].astype(f32)
        up = arrived_ref[:, width + hidden : width + 2 * hidden].astype(f32)
        weight = arrived_ref[:, width + 2 * hidden :].astype(f32)[:, 0:1]
        sig = jax.nn.sigmoid(gate)
        act = gate * sig
        score_ref[span, :] = act * up
        up_ref[span, :] = weight * act
        gate_ref[span, :] = weight * (up * sig * (1.0 + gate * (1.0 - sig)))


def row_kernel(position_ref, grads_ref, gate_factor, up_factor, score_factor, *refs, chips):
    down_refs, refs = refs[:-5], refs[-5:]
    joined_any, scores_ref, joined, down, sems = refs
    hidden = down.shape[0]
    loads = []
    for n, down_ref in enumerate(down_refs):
        size = down_ref.shape[0]
        if size == hidden:
            at = 0
        else:
            slab = lax.rem(position_ref[0] + 2 * (chips - n // 2), 2 * chips) ^ (n % 2)
            at = pl.multiple_of(slab * size, 16)
        loads.append(pltpu.make_async_copy(down_ref, down.at[pl.ds(at, size)], sems.at[n]))
    for load in loads:
        load.start()
    for load in loads:
        load.wait()
    scores = None
    step = 2 * LANES
    stores = []
    for at in range(0, hidden, step):
        span = slice(at, at + step)
        back = lax.dot_general(
            grads_ref[...], down[span, :], (((1,), (1,)), ((), ())), preferred_element_type=f32
        )
        part = jnp.sum(score_factor[:, span] * back, axis=1, keepdims=True)
        scores = part if scores is None else scores + part
        for half, factor in enumerate((gate_factor, up_factor)):
            out = slice(half * hidden + at, half * hidden + at + step)
            joined[:, out] = (factor[:, span] * back).astype(bf16)
            sem = sems.at[len(down_refs) + 2 * (at // step) + half]
            stores.append(pltpu.make_async_copy(joined.at[:, out], joined_any.at[:, out], sem))
            stores[-1].start()
    scores_ref[...] = jnp.broadcast_to(scores, scores_ref.shape)
    for store in stores:
        store.wait()


def router_kernel(position_ref, select_ref, rows_ref, out_ref):
    experts = rows_ref.shape[0]
    own = [rows_ref[k, position_ref[0], :, :LANES] for k in range(experts)]
    parts = jnp.concatenate(own, axis=0).astype(f32)
    scores = (parts[:, 1:2] + parts[:, 2:3]) + parts[:, 3:4]
    out_ref[...] = jnp.sum(jnp.where(select_ref[...] > 0.5, scores, 0.0), axis=0, keepdims=True)


def head_kernel(master_ref, first_ref, second_ref, out_ref):
    for n, source in enumerate((master_ref, first_ref, second_ref)):
        out_ref[n] = source[...]


def slab_sum(total, turned_ref, slabs, joined_refs, span):
    for slab, ref in zip(slabs, joined_refs):
        piece = jnp.dot(turned_ref[slab], ref[:, span], preferred_element_type=f32)
        piece = piece.astype(bf16).astype(f32)
        total = piece if total is None else total + piece
    return total


def slabs_of(position, steps, chips):
    own = [lax.rem(position + 2 * (chips - k), 2 * chips) for k in steps]
    return [slab ^ other for slab in own for other in (0, 1)]


def early_kernel(position_ref, turned_ref, *refs, steps, chips):
    joined_refs, base, sum_ref = refs[: 2 * len(steps)], refs[2 * len(steps) : -1], refs[-1]
    step = 2 * LANES
    slabs = slabs_of(position_ref[0], steps, chips)
    for at in range(0, sum_ref.shape[1], step):
        span = slice(at, at + step)
        total = base[0][:, span] if base else None
        sum_ref[:, span] = slab_sum(total, turned_ref, slabs, joined_refs, span)


def adam(grad, old, first, second):
    first_new = beta_one * first + (1.0 - beta_one) * grad
    second_new = beta_two * second + (1.0 - beta_two) * grad * grad
    below = jnp.sqrt(second_new * (1.0 / (1.0 - beta_two**adam_step))) + adam_eps
    update = first_new * (learn_rate / (1.0 - beta_one**adam_step)) / below
    return old * (1.0 - learn_rate * decay_rate) - update, first_new, second_new


def final_kernel(
    position_ref,
    offsets_ref,
    turned_ref,
    early_ref,
    heads_ref,
    own_ref,
    other_ref,
    old,
    first,
    second,
    out_master,
    out_first,
    out_second,
    weight_ref,
    sums,
    moved,
    new_old,
    new_first,
    new_second,
    head_new,
    sems,
    *,
    even_size,
    head_rows,
    chips,
):
    kept, columns = early_ref.shape
    per = weight_ref.shape[0]
    lines = columns // LANES
    before = (kept - per) * lines
    bucket_rows = old.shape[0]
    flat_rows = even_size // LANES
    position = position_ref[0]
    start = offsets_ref[position]
    finish = offsets_ref[position + 1]
    shift = position * even_size - start
    next_shift = (position + 1) * even_size - finish
    length = finish - start
    whole, part = shift // LANES, shift % LANES
    odd = whole % 8
    next_whole, next_part = next_shift // LANES, next_shift % LANES

    step = 2 * LANES
    slabs = slabs_of(position, [chips - 1], chips)
    for begin in range(0, columns, step):
        span = slice(begin, begin + step)
        total = slab_sum(early_ref[:, span], turned_ref, slabs, (own_ref, other_ref), span)
        for c in range(step // LANES):
            block = pltpu.roll(total[:, c * LANES : (c + 1) * LANES], part, 1)
            line = begin // LANES + c
            sums[pl.ds(odd + line, kept, stride=lines), :] = block
            moved[pl.ds(odd + line + 1, kept, stride=lines), :] = block

    def slots_of(row, count):
        at = pl.multiple_of(row + before - (whole - odd), 8)
        lane = iota((count, LANES), 1)
        return jnp.where(lane >= part, sums[pl.ds(at, count), :], moved[pl.ds(at, count), :])

    def update(row, count):
        span = pl.ds(row, count)
        a, b, c = adam(slots_of(row, count), old[span, :], first[span, :], second[span, :])
        new_old[span, :], new_first[span, :], new_second[span, :] = a, b, c

    def masked(row, count):
        span = pl.ds(row, count)
        inside = (row + iota((count, LANES), 0)) * LANES + iota((count, LANES), 1) < length
        grad = jnp.where(inside, slots_of(row, count), 0.0)
        a, b, c = adam(grad, old[span, :], first[span, :], second[span, :])
        new_old[span, :] = jnp.where(inside, a, 0.0)
        new_first[span, :] = jnp.where(inside, b, 0.0)
        new_second[span, :] = jnp.where(inside, c, 0.0)

    def send(begin, count, slot):
        span = pl.ds(begin, count)
        stores = [
            pltpu.make_async_copy(source.at[span], target.at[span], sems.at[slot, n])
            for n, (source, target) in enumerate(
                ((new_old, out_master), (new_first, out_first), (new_second, out_second))
            )
        ]
        for store in stores:
            store.start()
        return stores

    def chunk(n, carry):
        update(pl.multiple_of(n * CHUNK, 8), CHUNK)
        return carry

    safe = (flat_rows - head_rows) // CHUNK
    third = -(-safe // 3)
    stores = []
    for slot, begin in enumerate(range(0, safe, third)):
        end = min(begin + third, safe)
        lax.fori_loop(begin, end, chunk, 0)
        stores += send(begin * CHUNK, (end - begin) * CHUNK, slot)
    for row in range(safe * CHUNK, bucket_rows, CHUNK):
        masked(row, min(CHUNK, bucket_rows - row))
    stores += send(safe * CHUNK, bucket_rows - safe * CHUNK, 3)

    def next_slots():
        lane = iota((head_rows, LANES), 1)
        base = flat_rows + before - next_whole + odd
        here = pltpu.roll(sums[pl.ds(base, head_rows), :], (LANES - part) % LANES, 1)
        above = pltpu.roll(sums[pl.ds(base - 1, head_rows), :], (LANES - part) % LANES, 1)
        return pltpu.roll(jnp.where(lane < LANES - next_part, here, above), next_part, 1)

    edge = round_up(-(-head_rows // lines), 16)
    head_new[pl.ds(edge * lines, head_rows), :] = adam(next_slots(), heads_ref[0], heads_ref[1], heads_ref[2])[0]

    flat_row = iota((edge, LANES), 0) + (per - edge)
    for c in range(lines):
        lane = iota((per, LANES), 1)
        here = new_old[pl.ds(c + whole, per, stride=lines), :]
        below = new_old[pl.ds(c + whole + 1, per, stride=lines), :]
        own = pltpu.roll(jnp.where(lane >= part, here, below), (LANES - part) % LANES, 1)
        base = c + next_whole
        lane = iota((edge, LANES), 1)
        here = head_new[pl.ds(base, edge, stride=lines), :]
        below = head_new[pl.ds(base + 1, edge, stride=lines), :]
        other = pltpu.roll(jnp.where(lane >= next_part, here, below), (LANES - next_part) % LANES, 1)
        flat = (flat_row * lines + c) * LANES + lane
        last = jnp.where(flat < even_size - next_shift, own[per - edge :], other)
        out = slice(c * LANES, (c + 1) * LANES)
        if per > edge:
            weight_ref[: per - edge, out] = own[: per - edge].astype(bf16)
        weight_ref[per - edge :, out] = last.astype(bf16)

    for store in stores:
        store.wait()


def vmem():
    return pl.BlockSpec(memory_space=pltpu.VMEM)


def anywhere():
    return pl.BlockSpec(memory_space=pl.ANY)


def hbm():
    return pl.BlockSpec(memory_space=pltpu.HBM)


def smem():
    return pl.BlockSpec(memory_space=pltpu.SMEM)


def call(kernel, outs, scalars, args, name, mib, flops=0, moved=0):
    many = isinstance(outs, (list, tuple))
    return pl.pallas_call(
        kernel,
        out_shape=outs,
        in_specs=[smem()] * len(scalars) + [vmem()] * len(args),
        out_specs=[vmem()] * len(outs) if many else vmem(),
        compiler_params=params(mib),
        cost_estimate=cost(flops, moved),
        name=name,
    )(*scalars, *args)


def struct(shape, kind):
    return jax.ShapeDtypeStruct(shape, kind)


def shards(
    tokens,
    out_grad,
    gate_up,
    route_weight,
    routes,
    down_weight,
    master,
    moment_one,
    moment_two,
    offsets,
):
    token_count, model_width = tokens.shape
    columns = gate_up.shape[2]
    hidden = columns // 2
    bucket_cap = master.shape[2]
    groups = lax.axis_size("expert")
    parts = lax.axis_size("dp")
    experts = groups * master.shape[0]
    cap = 2 * token_count // experts
    rows = experts * cap
    per = model_width // parts
    even_size = per * columns
    margin = bucket_cap - even_size
    extra = round_up(-(-margin // columns), 16)
    width = round_up(per + extra + 4, LANES)
    kept = per + extra
    lines = columns // LANES
    bucket_rows = bucket_cap // LANES
    head_rows = round_up(margin // LANES, 8)

    chips = parts // 2
    position = lax.axis_index("dp").astype(i32).reshape(1)
    state = struct((bucket_rows, LANES), f32)
    old, first, second = (array.reshape(bucket_rows, LANES) for array in (master, moment_one, moment_two))

    def onward(block):
        return lax.ppermute(block, "dp", [(i, (i + 2) % parts) for i in range(parts)])

    def swapped(block):
        return lax.ppermute(block, "dp", [(i, i ^ 1) for i in range(parts)])

    def exchanged(block, axis):
        return lax.all_to_all(block, axis, split_axis=0, concat_axis=0, tiled=True)

    def tied(*values):
        return lax.optimization_barrier(values)

    wide = model_width + columns + LANES
    me = lax.axis_index("expert").astype(i32).reshape(1)
    select, target, *packed = pl.pallas_call(
        pack_kernel,
        out_shape=[
            struct((rows, token_count), f32),
            struct((1, token_count), f32),
        ]
        + [struct((cap, wide), bf16)] * experts,
        in_specs=[smem(), vmem(), vmem(), hbm(), hbm()],
        out_specs=[vmem(), vmem()] + [hbm()] * experts,
        scratch_shapes=[
            pltpu.VMEM((token_count, model_width), bf16),
            pltpu.VMEM((token_count, columns), bf16),
            pltpu.VMEM((experts, cap, wide), bf16),
            pltpu.SemaphoreType.DMA((2 + experts,)),
        ],
        compiler_params=params(60),
        cost_estimate=cost(0, 6_000_000),
        name="pack",
    )(
        me,
        routes.reshape(1, token_count),
        route_weight.reshape(1, token_count),
        out_grad,
        gate_up.reshape(token_count, columns),
    )
    windows = call(
        functools.partial(window_kernel, per=per, lead=width - per),
        struct((parts, token_count, width), bf16),
        (),
        (target, tokens),
        "window",
        12,
        moved=2_000_000,
    )
    arrived = packed[:1] + [
        lax.ppermute(packed[k], "expert", [(i, i ^ k) for i in range(experts)]) for k in range(1, experts)
    ]
    windows = exchanged(windows, "dp")
    if down_weight.shape[1] % 16 == 0:
        held, other = [down_weight[0]], [swapped(down_weight[0])]
        for k in range(1, chips):
            arrival = onward(held[-1])
            held.append(arrival)
            if k == chips - 2:
                held[-1], arrived[1] = tied(held[-1], arrived[1])
                arrived[-1], windows, block = tied(arrived[-1], windows, held[-1])
                other.append(swapped(block))
                continue
            other.append(swapped(held[-1]))
        down = [piece for pair in zip(held, other) for piece in pair]
    else:
        down = [lax.all_gather(down_weight, "dp", axis=1, tiled=True)[0]]
    factors = call(
        factor_kernel,
        [struct((rows, model_width), bf16)] + [struct((rows, hidden), f32)] * 3,
        (me,),
        arrived,
        "factors",
        20,
        moved=6_000_000,
    )
    joined, scores = pl.pallas_call(
        functools.partial(row_kernel, chips=chips),
        out_shape=[struct((rows, columns), bf16), struct((rows, LANES), f32)],
        in_specs=[smem()] + [vmem()] * 4 + [anywhere()] * len(down),
        out_specs=[hbm(), vmem()],
        scratch_shapes=[
            pltpu.VMEM((rows, columns), bf16),
            pltpu.VMEM((hidden, model_width), bf16),
            pltpu.SemaphoreType.DMA((len(down) + 2 * (hidden // (2 * LANES)),)),
        ],
        compiler_params=params(24),
        cost_estimate=cost(2 * rows * model_width * hidden, 8_000_000),
        name="rows",
    )(position, *factors, *down)

    steps = [[joined, swapped(joined)]]
    step_one = onward(joined)
    heads = pl.pallas_call(
        head_kernel,
        grid=(1,),
        out_shape=struct((3, head_rows, LANES), f32),
        in_specs=[pl.BlockSpec((head_rows, LANES), lambda i: (0, 0))] * 3,
        out_specs=pl.BlockSpec((3, head_rows, LANES), lambda i: (0, 0, 0)),
        cost_estimate=cost(0, 400_000),
        name="heads",
    )(old, first, second)
    heads, _ = tied(heads, step_one)
    heads = lax.ppermute(heads, "dp", [(i + 1, i) for i in range(parts - 1)])
    compacted = call(
        compact_kernel,
        struct((experts, parts, cap, width), bf16),
        (position,),
        (windows, scores),
        "compact",
        12,
        moved=3_000_000,
    )
    compacted_rows = exchanged(compacted, "expert")
    turned = call(
        turn_kernel,
        struct((parts, kept, rows), bf16),
        (),
        (compacted_rows,),
        "turn",
        12,
        moved=3_000_000,
    )
    router_grad = call(
        router_kernel,
        struct((1, token_count), f32),
        (position,),
        (select, compacted_rows),
        "router",
        4,
        moved=300_000,
    )

    def early(name, at, pieces, sum_before):
        return call(
            functools.partial(early_kernel, steps=at, chips=chips),
            struct((kept, columns), f32),
            (position,),
            [turned] + pieces + sum_before,
            name,
            24,
            flops=4 * len(at) * rows * kept * columns,
            moved=8_000_000,
        )

    total = []
    arrival = joined
    for k in range(1, chips):
        arrival = onward(arrival) if k > 1 else step_one
        if k > 2:
            pieces = steps.pop()
            if k == 3:
                begun = early("early1", [0, 1], steps.pop(0) + steps.pop(0), [])
                total = [begun]
            total = [early("early%d" % (k - 1), [k - 1], pieces, total)]
        if k == chips - 1:
            arrival, total[0], router_grad, heads = tied(arrival, total[0], router_grad, heads)
        steps.append([arrival, swapped(arrival)])
    last = steps.pop()
    flat_rows = even_size // LANES
    sum_rows = round_up(kept * lines + head_rows + 32, 8)
    edge = round_up(-(-head_rows // lines), 16)
    new_master, new_one, new_two, new_weight = pl.pallas_call(
        functools.partial(final_kernel, even_size=even_size, head_rows=head_rows, chips=chips),
        out_shape=[state, state, state, struct((per, columns), bf16)],
        in_specs=[smem()] * 2 + [vmem()] * 8,
        out_specs=[anywhere(), anywhere(), anywhere(), vmem()],
        scratch_shapes=[
            pltpu.VMEM((sum_rows, LANES), f32),
            pltpu.VMEM((sum_rows, LANES), f32),
            pltpu.VMEM((round_up(flat_rows + head_rows + 32, 8), LANES), f32),
            pltpu.VMEM((bucket_rows, LANES), f32),
            pltpu.VMEM((bucket_rows, LANES), f32),
            pltpu.VMEM((edge * lines + 2 * head_rows + 32, LANES), f32),
            pltpu.SemaphoreType.DMA((4, 3)),
        ],
        compiler_params=params(32),
        cost_estimate=cost(4 * rows * kept * columns, 25_000_000),
        name="final",
    )(
        position,
        offsets,
        turned,
        total[0],
        heads,
        *last,
        old,
        first,
        second,
    )
    return (
        new_master.reshape(1, 1, bucket_cap),
        new_one.reshape(1, 1, bucket_cap),
        new_two.reshape(1, 1, bucket_cap),
        new_weight[None],
        router_grad.reshape(token_count, 1),
    )


def solution(mesh):
    placed = (
        P(("dp", "expert"), None),
        P(("dp", "expert"), None),
        P(("dp", "expert"), None, None),
        P(("dp", "expert"), None),
        P(("dp", "expert"), None),
        P("expert", "dp", None),
        P("expert", "dp", None),
        P("expert", "dp", None),
        P("expert", "dp", None),
        P(),
    )
    return jax.shard_map(
        shards,
        mesh=mesh,
        in_specs=placed,
        out_specs=(
            P("expert", "dp", None),
            P("expert", "dp", None),
            P("expert", "dp", None),
            P("expert", "dp", None),
            P(("dp", "expert"), None),
        ),
        check_vma=False,
    )
```

```python
import functools

import jax
import jax.numpy as jnp
from jax import lax
from jax.experimental import pallas as pl
from jax.experimental.pallas import tpu as pltpu
from jax.sharding import PartitionSpec as P

beta_one = 0.9
beta_two = 0.95
learn_rate = 0.001
decay_rate = 0.1
adam_eps = 1e-08
adam_step = 20.0

LANES = 128
CHUNK = 120

f32 = jnp.float32
bf16 = jnp.bfloat16
i32 = jnp.int32


def round_up(value, unit):
    return -(-value // unit) * unit


def iota(shape, axis):
    return lax.broadcasted_iota(i32, shape, axis)


def params(mib):
    return pltpu.CompilerParams(vmem_limit_bytes=mib * 1024 * 1024)


def cost(flops, moved):
    return pl.CostEstimate(flops=int(flops), bytes_accessed=int(moved), transcendentals=0)


def pack_kernel(me_ref, routes_ref, weight_ref, grads_any, saved_any, select_ref, target_ref, *refs):
    packed_anys, (grads, saved, packed, sems) = refs[:-4], refs[-4:]
    loads = [
        pltpu.make_async_copy(grads_any, grads, sems.at[0]),
        pltpu.make_async_copy(saved_any, saved, sems.at[1]),
    ]
    for load in loads:
        load.start()
    ids = routes_ref[...]
    experts, cap, _ = packed.shape
    count = ids.shape[1]
    width = grads.shape[1]
    hits = iota((round_up(experts, 8), count), 0) == ids
    before = (iota((count, count), 0) < iota((count, count), 1)).astype(bf16)
    earlier = jnp.dot(hits.astype(f32).astype(bf16), before, preferred_element_type=f32)
    slot = jnp.sum(jnp.where(hits, earlier, 0.0), axis=0, keepdims=True)
    target = ids * cap + slot.astype(i32)
    chosen = iota((experts * cap, count), 0) == target
    select = chosen.astype(f32).astype(bf16)
    select_ref[...] = chosen.astype(f32)
    target_ref[...] = target.astype(f32)
    weight = jnp.sum(jnp.where(chosen, weight_ref[...].astype(f32), 0.0), axis=1, keepdims=True)
    weight = jnp.broadcast_to(weight, (experts * cap, LANES)).astype(bf16)
    for load in loads:
        load.wait()
    picked_grads = jnp.dot(select, grads[...], preferred_element_type=f32).astype(bf16)
    picked_saved = jnp.dot(select, saved[...], preferred_element_type=f32).astype(bf16)
    stores = []
    for k in range(experts):
        span = slice(k * cap, (k + 1) * cap)
        packed[k, :, :width] = picked_grads[span]
        packed[k, :, width:-LANES] = picked_saved[span]
        packed[k, :, -LANES:] = weight[span]
    for k, packed_any in enumerate(packed_anys):
        stores.append(pltpu.make_async_copy(packed.at[me_ref[0] ^ k], packed_any, sems.at[2 + k]))
        stores[-1].start()
    for store in stores:
        store.wait()


def window_kernel(target_ref, tokens_ref, out_ref, *, per, lead):
    parts, count, width = out_ref.shape
    diagonal = iota((count, count), 0) == iota((count, count), 1)
    column = jnp.sum(jnp.where(diagonal, target_ref[...], 0.0), axis=1, keepdims=True)
    note = jnp.broadcast_to(column, (count, width)).astype(bf16)
    lane = iota((count, width), 1)
    for j in range(parts):
        start = per * j - lead
        if start < 0:
            blank = jnp.zeros((count, -start), bf16)
            piece = jnp.concatenate([blank, tokens_ref[:, : start + width]], axis=1)
        else:
            piece = tokens_ref[:, start : start + width]
        out_ref[j] = jnp.where(lane == 0, note, piece)


def compact_kernel(position_ref, windows_ref, scores_ref, out_ref):
    parts, count, width = windows_ref.shape
    experts, _, cap, _ = out_ref.shape
    diagonal = iota((count, count), 0) == iota((count, count), 1)
    slots = iota((experts * cap, count), 0)
    for i in range(parts):
        block = windows_ref[i]
        column = block[:, 0:1].astype(f32)
        target = jnp.sum(jnp.where(diagonal, column, 0.0), axis=0, keepdims=True).astype(i32)
        select = (slots == target).astype(f32).astype(bf16)
        rows = jnp.dot(select, block, preferred_element_type=f32).astype(bf16)
        for k in range(experts):
            out_ref[k, i] = rows[k * cap : (k + 1) * cap]
    lane = iota((cap, LANES), 1)
    for k in range(experts):
        rest = scores_ref[k * cap : (k + 1) * cap, :]
        first = out_ref[k, position_ref[0], :, :LANES]
        for c in range(3):
            part = rest.astype(bf16)
            rest = rest - part.astype(f32)
            first = jnp.where(lane == 1 + c, part, first)
        out_ref[k, position_ref[0], :, :LANES] = first


def turn_kernel(rows_ref, out_ref):
    experts, parts, _, width = rows_ref.shape
    kept = out_ref.shape[1]
    for i in range(parts):
        slab = jnp.concatenate([rows_ref[k, i] for k in range(experts)], axis=0)
        out_ref[i] = slab.T[width - kept :, :]


def factor_kernel(me_ref, *refs):
    arrived_refs, (grads_ref, gate_ref, up_ref, score_ref) = refs[:-4], refs[-4:]
    width, hidden = grads_ref.shape[1], gate_ref.shape[1]
    cap = arrived_refs[0].shape[0]
    for k, arrived_ref in enumerate(arrived_refs):
        span = pl.ds(pl.multiple_of((me_ref[0] ^ k) * cap, 16), cap)
        grads_ref[span, :] = arrived_ref[:, :width]
        gate = arrived_ref[:, width : width + hidden].astype(f32)
        up = arrived_ref[:, width + hidden : width + 2 * hidden].astype(f32)
        weight = arrived_ref[:, width + 2 * hidden :].astype(f32)[:, 0:1]
        sig = jax.nn.sigmoid(gate)
        act = gate * sig
        score_ref[span, :] = act * up
        up_ref[span, :] = weight * act
        gate_ref[span, :] = weight * (up * sig * (1.0 + gate * (1.0 - sig)))


def row_kernel(position_ref, grads_ref, gate_factor, up_factor, score_factor, *refs, chips):
    down_refs, refs = refs[:-5], refs[-5:]
    joined_any, scores_ref, joined, down, sems = refs
    hidden = down.shape[0]
    loads = []
    for n, down_ref in enumerate(down_refs):
        size = down_ref.shape[0]
        if size == hidden:
            at = 0
        else:
            slab = lax.rem(position_ref[0] + 2 * (chips - n // 2), 2 * chips) ^ (n % 2)
            at = pl.multiple_of(slab * size, 16)
        loads.append(pltpu.make_async_copy(down_ref, down.at[pl.ds(at, size)], sems.at[n]))
    for load in loads:
        load.start()
    for load in loads:
        load.wait()
    scores = None
    step = 2 * LANES
    stores = []
    for at in range(0, hidden, step):
        span = slice(at, at + step)
        back = lax.dot_general(
            grads_ref[...], down[span, :], (((1,), (1,)), ((), ())), preferred_element_type=f32
        )
        part = jnp.sum(score_factor[:, span] * back, axis=1, keepdims=True)
        scores = part if scores is None else scores + part
        for half, factor in enumerate((gate_factor, up_factor)):
            out = slice(half * hidden + at, half * hidden + at + step)
            joined[:, out] = (factor[:, span] * back).astype(bf16)
            sem = sems.at[len(down_refs) + 2 * (at // step) + half]
            stores.append(pltpu.make_async_copy(joined.at[:, out], joined_any.at[:, out], sem))
            stores[-1].start()
    scores_ref[...] = jnp.broadcast_to(scores, scores_ref.shape)
    for store in stores:
        store.wait()


def router_kernel(position_ref, select_ref, rows_ref, out_ref):
    experts = rows_ref.shape[0]
    own = [rows_ref[k, position_ref[0], :, :LANES] for k in range(experts)]
    parts = jnp.concatenate(own, axis=0).astype(f32)
    scores = (parts[:, 1:2] + parts[:, 2:3]) + parts[:, 3:4]
    out_ref[...] = jnp.sum(jnp.where(select_ref[...] > 0.5, scores, 0.0), axis=0, keepdims=True)


def head_kernel(master_ref, first_ref, second_ref, out_ref):
    for n, source in enumerate((master_ref, first_ref, second_ref)):
        out_ref[n] = source[...]


def slab_sum(total, turned_ref, slabs, joined_refs, span):
    for slab, ref in zip(slabs, joined_refs):
        piece = jnp.dot(turned_ref[slab], ref[:, span], preferred_element_type=f32)
        piece = piece.astype(bf16).astype(f32)
        total = piece if total is None else total + piece
    return total


def slabs_of(position, steps, chips):
    own = [lax.rem(position + 2 * (chips - k), 2 * chips) for k in steps]
    return [slab ^ other for slab in own for other in (0, 1)]


def early_kernel(position_ref, turned_ref, *refs, steps, chips):
    joined_refs, base, sum_ref = refs[: 2 * len(steps)], refs[2 * len(steps) : -1], refs[-1]
    step = 2 * LANES
    slabs = slabs_of(position_ref[0], steps, chips)
    for at in range(0, sum_ref.shape[1], step):
        span = slice(at, at + step)
        total = base[0][:, span] if base else None
        sum_ref[:, span] = slab_sum(total, turned_ref, slabs, joined_refs, span)


def adam(grad, old, first, second):
    first_new = beta_one * first + (1.0 - beta_one) * grad
    second_new = beta_two * second + (1.0 - beta_two) * grad * grad
    below = jnp.sqrt(second_new * (1.0 / (1.0 - beta_two**adam_step))) + adam_eps
    update = first_new * (learn_rate / (1.0 - beta_one**adam_step)) / below
    return old * (1.0 - learn_rate * decay_rate) - update, first_new, second_new


def final_kernel(
    position_ref,
    offsets_ref,
    turned_ref,
    early_ref,
    heads_ref,
    own_ref,
    other_ref,
    old,
    first,
    second,
    out_master,
    out_first,
    out_second,
    weight_ref,
    sums,
    moved,
    new_old,
    new_first,
    new_second,
    head_new,
    sems,
    *,
    even_size,
    head_rows,
    chips,
):
    kept, columns = early_ref.shape
    per = weight_ref.shape[0]
    lines = columns // LANES
    before = (kept - per) * lines
    bucket_rows = old.shape[0]
    flat_rows = even_size // LANES
    position = position_ref[0]
    start = offsets_ref[position]
    finish = offsets_ref[position + 1]
    shift = position * even_size - start
    next_shift = (position + 1) * even_size - finish
    length = finish - start
    whole, part = shift // LANES, shift % LANES
    odd = whole % 8
    next_whole, next_part = next_shift // LANES, next_shift % LANES

    step = 2 * LANES
    slabs = slabs_of(position, [chips - 1], chips)
    for begin in range(0, columns, step):
        span = slice(begin, begin + step)
        total = slab_sum(early_ref[:, span], turned_ref, slabs, (own_ref, other_ref), span)
        for c in range(step // LANES):
            block = pltpu.roll(total[:, c * LANES : (c + 1) * LANES], part, 1)
            line = begin // LANES + c
            sums[pl.ds(odd + line, kept, stride=lines), :] = block
            moved[pl.ds(odd + line + 1, kept, stride=lines), :] = block

    def slots_of(row, count):
        at = pl.multiple_of(row + before - (whole - odd), 8)
        lane = iota((count, LANES), 1)
        return jnp.where(lane >= part, sums[pl.ds(at, count), :], moved[pl.ds(at, count), :])

    def update(row, count):
        span = pl.ds(row, count)
        a, b, c = adam(slots_of(row, count), old[span, :], first[span, :], second[span, :])
        new_old[span, :], new_first[span, :], new_second[span, :] = a, b, c

    def masked(row, count):
        span = pl.ds(row, count)
        inside = (row + iota((count, LANES), 0)) * LANES + iota((count, LANES), 1) < length
        grad = jnp.where(inside, slots_of(row, count), 0.0)
        a, b, c = adam(grad, old[span, :], first[span, :], second[span, :])
        new_old[span, :] = jnp.where(inside, a, 0.0)
        new_first[span, :] = jnp.where(inside, b, 0.0)
        new_second[span, :] = jnp.where(inside, c, 0.0)

    def send(begin, count, slot):
        span = pl.ds(begin, count)
        stores = [
            pltpu.make_async_copy(source.at[span], target.at[span], sems.at[slot, n])
            for n, (source, target) in enumerate(
                ((new_old, out_master), (new_first, out_first), (new_second, out_second))
            )
        ]
        for store in stores:
            store.start()
        return stores

    def chunk(n, carry):
        update(pl.multiple_of(n * CHUNK, 8), CHUNK)
        return carry

    safe = (flat_rows - head_rows) // CHUNK
    third = -(-safe // 3)
    stores = []
    for slot, begin in enumerate(range(0, safe, third)):
        end = min(begin + third, safe)
        lax.fori_loop(begin, end, chunk, 0)
        stores += send(begin * CHUNK, (end - begin) * CHUNK, slot)
    for row in range(safe * CHUNK, bucket_rows, CHUNK):
        masked(row, min(CHUNK, bucket_rows - row))
    stores += send(safe * CHUNK, bucket_rows - safe * CHUNK, 3)

    def next_slots():
        lane = iota((head_rows, LANES), 1)
        base = flat_rows + before - next_whole + odd
        here = pltpu.roll(sums[pl.ds(base, head_rows), :], (LANES - part) % LANES, 1)
        above = pltpu.roll(sums[pl.ds(base - 1, head_rows), :], (LANES - part) % LANES, 1)
        return pltpu.roll(jnp.where(lane < LANES - next_part, here, above), next_part, 1)

    edge = round_up(-(-head_rows // lines), 16)
    head_new[pl.ds(edge * lines, head_rows), :] = adam(next_slots(), heads_ref[0], heads_ref[1], heads_ref[2])[0]

    flat_row = iota((edge, LANES), 0) + (per - edge)
    for c in range(lines):
        lane = iota((per, LANES), 1)
        here = new_old[pl.ds(c + whole, per, stride=lines), :]
        below = new_old[pl.ds(c + whole + 1, per, stride=lines), :]
        own = pltpu.roll(jnp.where(lane >= part, here, below), (LANES - part) % LANES, 1)
        base = c + next_whole
        lane = iota((edge, LANES), 1)
        here = head_new[pl.ds(base, edge, stride=lines), :]
        below = head_new[pl.ds(base + 1, edge, stride=lines), :]
        other = pltpu.roll(jnp.where(lane >= next_part, here, below), (LANES - next_part) % LANES, 1)
        flat = (flat_row * lines + c) * LANES + lane
        last = jnp.where(flat < even_size - next_shift, own[per - edge :], other)
        out = slice(c * LANES, (c + 1) * LANES)
        if per > edge:
            weight_ref[: per - edge, out] = own[: per - edge].astype(bf16)
        weight_ref[per - edge :, out] = last.astype(bf16)

    for store in stores:
        store.wait()


def vmem():
    return pl.BlockSpec(memory_space=pltpu.VMEM)


def anywhere():
    return pl.BlockSpec(memory_space=pl.ANY)


def hbm():
    return pl.BlockSpec(memory_space=pltpu.HBM)


def smem():
    return pl.BlockSpec(memory_space=pltpu.SMEM)


def call(kernel, outs, scalars, args, name, mib, flops=0, moved=0):
    many = isinstance(outs, (list, tuple))
    return pl.pallas_call(
        kernel,
        out_shape=outs,
        in_specs=[smem()] * len(scalars) + [vmem()] * len(args),
        out_specs=[vmem()] * len(outs) if many else vmem(),
        compiler_params=params(mib),
        cost_estimate=cost(flops, moved),
        name=name,
    )(*scalars, *args)


def struct(shape, kind):
    return jax.ShapeDtypeStruct(shape, kind)


def shards(
    tokens,
    out_grad,
    gate_up,
    route_weight,
    routes,
    down_weight,
    master,
    moment_one,
    moment_two,
    offsets,
):
    token_count, model_width = tokens.shape
    columns = gate_up.shape[2]
    hidden = columns // 2
    bucket_cap = master.shape[2]
    groups = lax.axis_size("expert")
    parts = lax.axis_size("dp")
    experts = groups * master.shape[0]
    cap = 2 * token_count // experts
    rows = experts * cap
    per = model_width // parts
    even_size = per * columns
    margin = bucket_cap - even_size
    extra = round_up(-(-margin // columns), 16)
    width = round_up(per + extra + 4, LANES)
    kept = per + extra
    lines = columns // LANES
    bucket_rows = bucket_cap // LANES
    head_rows = round_up(margin // LANES, 8)

    chips = parts // 2
    position = lax.axis_index("dp").astype(i32).reshape(1)
    state = struct((bucket_rows, LANES), f32)
    old, first, second = (array.reshape(bucket_rows, LANES) for array in (master, moment_one, moment_two))

    def onward(block):
        return lax.ppermute(block, "dp", [(i, (i + 2) % parts) for i in range(parts)])

    def swapped(block):
        return lax.ppermute(block, "dp", [(i, i ^ 1) for i in range(parts)])

    def exchanged(block, axis):
        return lax.all_to_all(block, axis, split_axis=0, concat_axis=0, tiled=True)

    def tied(*values):
        return lax.optimization_barrier(values)

    wide = model_width + columns + LANES
    me = lax.axis_index("expert").astype(i32).reshape(1)
    select, target, *packed = pl.pallas_call(
        pack_kernel,
        out_shape=[
            struct((rows, token_count), f32),
            struct((1, token_count), f32),
        ]
        + [struct((cap, wide), bf16)] * experts,
        in_specs=[smem(), vmem(), vmem(), hbm(), hbm()],
        out_specs=[vmem(), vmem()] + [hbm()] * experts,
        scratch_shapes=[
            pltpu.VMEM((token_count, model_width), bf16),
            pltpu.VMEM((token_count, columns), bf16),
            pltpu.VMEM((experts, cap, wide), bf16),
            pltpu.SemaphoreType.DMA((2 + experts,)),
        ],
        compiler_params=params(60),
        cost_estimate=cost(0, 6_000_000),
        name="pack",
    )(
        me,
        routes.reshape(1, token_count),
        route_weight.reshape(1, token_count),
        out_grad,
        gate_up.reshape(token_count, columns),
    )
    windows = call(
        functools.partial(window_kernel, per=per, lead=width - per),
        struct((parts, token_count, width), bf16),
        (),
        (target, tokens),
        "window",
        12,
        moved=2_000_000,
    )
    arrived = packed[:1] + [
        lax.ppermute(packed[k], "expert", [(i, i ^ k) for i in range(experts)]) for k in range(1, experts)
    ]
    windows = exchanged(windows, "dp")
    if down_weight.shape[1] % 16 == 0:
        held, other = [down_weight[0]], [swapped(down_weight[0])]
        for k in range(1, chips):
            arrival = onward(held[-1])
            held.append(arrival)
            if k == chips - 2:
                held[-1], arrived[1], arrived[2] = tied(held[-1], arrived[1], arrived[2])
                arrived[-1], windows, block = tied(arrived[-1], windows, held[-1])
                other.append(swapped(block))
                continue
            other.append(swapped(held[-1]))
        down = [piece for pair in zip(held, other) for piece in pair]
    else:
        down = [lax.all_gather(down_weight, "dp", axis=1, tiled=True)[0]]
    factors = call(
        factor_kernel,
        [struct((rows, model_width), bf16)] + [struct((rows, hidden), f32)] * 3,
        (me,),
        arrived,
        "factors",
        20,
        moved=6_000_000,
    )
    joined, scores = pl.pallas_call(
        functools.partial(row_kernel, chips=chips),
        out_shape=[struct((rows, columns), bf16), struct((rows, LANES), f32)],
        in_specs=[smem()] + [vmem()] * 4 + [anywhere()] * len(down),
        out_specs=[hbm(), vmem()],
        scratch_shapes=[
            pltpu.VMEM((rows, columns), bf16),
            pltpu.VMEM((hidden, model_width), bf16),
            pltpu.SemaphoreType.DMA((len(down) + 2 * (hidden // (2 * LANES)),)),
        ],
        compiler_params=params(24),
        cost_estimate=cost(2 * rows * model_width * hidden, 8_000_000),
        name="rows",
    )(position, *factors, *down)

    steps = [[joined, swapped(joined)]]
    step_one = onward(joined)
    heads = pl.pallas_call(
        head_kernel,
        grid=(1,),
        out_shape=struct((3, head_rows, LANES), f32),
        in_specs=[pl.BlockSpec((head_rows, LANES), lambda i: (0, 0))] * 3,
        out_specs=pl.BlockSpec((3, head_rows, LANES), lambda i: (0, 0, 0)),
        cost_estimate=cost(0, 400_000),
        name="heads",
    )(old, first, second)
    heads, _ = tied(heads, step_one)
    heads = lax.ppermute(heads, "dp", [(i + 1, i) for i in range(parts - 1)])
    compacted = call(
        compact_kernel,
        struct((experts, parts, cap, width), bf16),
        (position,),
        (windows, scores),
        "compact",
        12,
        moved=3_000_000,
    )
    compacted_rows = exchanged(compacted, "expert")
    turned = call(
        turn_kernel,
        struct((parts, kept, rows), bf16),
        (),
        (compacted_rows,),
        "turn",
        12,
        moved=3_000_000,
    )
    router_grad = call(
        router_kernel,
        struct((1, token_count), f32),
        (position,),
        (select, compacted_rows),
        "router",
        4,
        moved=300_000,
    )

    def early(name, at, pieces, sum_before):
        return call(
            functools.partial(early_kernel, steps=at, chips=chips),
            struct((kept, columns), f32),
            (position,),
            [turned] + pieces + sum_before,
            name,
            24,
            flops=4 * len(at) * rows * kept * columns,
            moved=8_000_000,
        )

    total = []
    arrival = joined
    for k in range(1, chips):
        arrival = onward(arrival) if k > 1 else step_one
        if k == 2:
            arrival, heads = tied(arrival, heads)
        if k > 2:
            pieces = steps.pop()
            if k == 3:
                begun = early("early1", [0, 1], steps.pop(0) + steps.pop(0), [])
                total = [begun]
            total = [early("early%d" % (k - 1), [k - 1], pieces, total)]
        if k == chips - 1:
            arrival, total[0], router_grad = tied(arrival, total[0], router_grad)
        steps.append([arrival, swapped(arrival)])
    last = steps.pop()
    flat_rows = even_size // LANES
    sum_rows = round_up(kept * lines + head_rows + 32, 8)
    edge = round_up(-(-head_rows // lines), 16)
    new_master, new_one, new_two, new_weight = pl.pallas_call(
        functools.partial(final_kernel, even_size=even_size, head_rows=head_rows, chips=chips),
        out_shape=[state, state, state, struct((per, columns), bf16)],
        in_specs=[smem()] * 2 + [vmem()] * 8,
        out_specs=[anywhere(), anywhere(), anywhere(), vmem()],
        scratch_shapes=[
            pltpu.VMEM((sum_rows, LANES), f32),
            pltpu.VMEM((sum_rows, LANES), f32),
            pltpu.VMEM((round_up(flat_rows + head_rows + 32, 8), LANES), f32),
            pltpu.VMEM((bucket_rows, LANES), f32),
            pltpu.VMEM((bucket_rows, LANES), f32),
            pltpu.VMEM((edge * lines + 2 * head_rows + 32, LANES), f32),
            pltpu.SemaphoreType.DMA((4, 3)),
        ],
        compiler_params=params(32),
        cost_estimate=cost(4 * rows * kept * columns, 25_000_000),
        name="final",
    )(
        position,
        offsets,
        turned,
        total[0],
        heads,
        *last,
        old,
        first,
        second,
    )
    return (
        new_master.reshape(1, 1, bucket_cap),
        new_one.reshape(1, 1, bucket_cap),
        new_two.reshape(1, 1, bucket_cap),
        new_weight[None],
        router_grad.reshape(token_count, 1),
    )


def solution(mesh):
    placed = (
        P(("dp", "expert"), None),
        P(("dp", "expert"), None),
        P(("dp", "expert"), None, None),
        P(("dp", "expert"), None),
        P(("dp", "expert"), None),
        P("expert", "dp", None),
        P("expert", "dp", None),
        P("expert", "dp", None),
        P("expert", "dp", None),
        P(),
    )
    return jax.shard_map(
        shards,
        mesh=mesh,
        in_specs=placed,
        out_specs=(
            P("expert", "dp", None),
            P("expert", "dp", None),
            P("expert", "dp", None),
            P("expert", "dp", None),
            P(("dp", "expert"), None),
        ),
        check_vma=False,
    )
```
